32 devices in a mesh: shard: 4 (over z), replica: 8 (over y, x, core).
Axes of the slice: x: 2, y: 2, z: 4, core: 2. Of those that a mesh axis runs over, the one named last changes fastest.
Arguments:
- tokens: bfloat16 [8192, 1024], P(('shard', 'replica')), may hold values from -6 to 6
- segment_ids: int32 [32, 256], P(('shard', 'replica')), may hold values from 0 to 5, never falling along the last dimension, each value on 1 to 128 neighbouring positions
- attn_gain: float32 [1024], replicated, may hold values from 0.25 to 1.75
- w_query: bfloat16 [1024, 2048], P('shard'), may hold values from -0.1875 to 0.1875
- w_key: bfloat16 [1024, 1024], P('shard'), may hold values from -0.1875 to 0.1875
- w_value: bfloat16 [1024, 1024], P('shard'), may hold values from -0.1875 to 0.1875
- query_gain: float32 [128], replicated, may hold values from 0.1 to 1.9
- key_gain: float32 [128], replicated, may hold values from 0.1 to 1.9
- w_out: bfloat16 [2048, 1024], P('shard'), may hold values from -0.5 to 0.5
- mlp_gain: float32 [1024], replicated, may hold values from 0.25 to 1.75
- w_gate: bfloat16 [1024, 3072], P('shard'), may hold values from -0.1875 to 0.1875
- w_up: bfloat16 [1024, 3072], P('shard'), may hold values from -0.1875 to 0.1875
- w_down: bfloat16 [3072, 1024], P('shard'), may hold values from -0.21875 to 0.21875
- cotangent: bfloat16 [8192, 1024], P(('shard', 'replica')), may hold values from -6 to 6
Outputs:
- activations: bfloat16 [8192, 1024], P(('shard', 'replica'))
- input_grad: bfloat16 [8192, 1024], P(('shard', 'replica'))
- attn_gain_grad: float32 [1024], replicated
- w_query_grad: float32 [1024, 2048], P('shard')
- w_key_grad: float32 [1024, 1024], P('shard')
- w_value_grad: float32 [1024, 1024], P('shard')
- query_gain_grad: float32 [128], replicated
- key_gain_grad: float32 [128], replicated
- w_out_grad: float32 [2048, 1024], P('shard')
- mlp_gain_grad: float32 [1024], replicated
- w_gate_grad: float32 [1024, 3072], P('shard')
- w_up_grad: float32 [1024, 3072], P('shard')
- w_down_grad: float32 [3072, 1024], P('shard')
The draws below stay inside these ranges and needn't reach their ends.
Inputs may be any that keep to these rules, and one draw needn't show every extreme that they name: `segment_ids`: document numbers never fall along a sequence; every number from 0 to 5 is used; each document has 1 to 128 tokens, and one has exactly that many.
All inputs are finite; a program needn't handle non-finite values.
Results may differ from the reference program's by a relative error of at most 0.02.
Values may be sent and summed in bfloat16 or wider, within the bound.
No kernel may reach another device: no remote copies, remote signals or barrier semaphores. Data moves between devices by JAX's collectives and lax.ppermute only.
A program may use at most 256 MiB of HBM per device.

```python
import math
import jax
import jax.numpy as jnp
import numpy as np
from jax import lax

D = 1024
HEADS = 16
KV_HEADS = 8
HEAD = 128
FF = 3072
LENGTH = 256
SEQS = 32
TOKENS = 8192


def block_levels(rng, shape, pieces, least, largest):
    def one(dim, parts):
        steps = jax.random.uniform(jax.random.fold_in(jax.random.fold_in(rng, 6), dim), (parts,), jnp.float32, least / len(pieces), largest / len(pieces))
        return jnp.repeat(jnp.exp(steps), shape[dim] // parts).reshape((-1,) + (1,) * (len(shape) - dim - 1))

    factor_of = one(*pieces[0])
    for cut in pieces[1:]:
        factor_of = factor_of * one(*cut)
    return factor_of


def profile(count, total, limit, slope):
    portions = [(1 << 20) // math.isqrt(grade ** slope) + 1 for grade in range(2, count + 1)]
    surplus, counts = total - limit - (count - 1), [1] * (count - 1)
    while surplus > 0:
        candidates = [i for i in range(count - 1) if counts[i] < limit]
        mass, left = sum([portions[i] for i in candidates]), surplus
        for i in candidates:
            addition = min(limit - counts[i], max(1, left * portions[i] // mass), surplus)
            counts[i] = counts[i] + addition
            surplus = surplus - addition
    return np.array([limit] + counts)


def ragged_sizes(rng, number_of, total, limit, slope):
    if number_of == 2:
        one = jax.random.randint(rng, (), max(1, total - limit), min(limit, total - 1) + 1)
        return jnp.stack([one, total - one])
    lengths = jnp.asarray(profile(number_of, total, limit, slope), jnp.int32)
    couples = (number_of - 1) // 2
    donor, receiver = lengths[1:1 + 2 * couples:2], lengths[2:2 + 2 * couples:2]
    room = jnp.minimum(donor - 1, limit - receiver)
    passed = jax.random.randint(jax.random.fold_in(rng, 1), (couples,), 0, 1 << 20) % (room + 1)
    lengths = lengths.at[1:1 + 2 * couples:2].set(donor - passed).at[2:2 + 2 * couples:2].set(receiver + passed)
    return lengths[jax.random.permutation(jax.random.fold_in(rng, 2), number_of)]


def normal_values(rng, shape, scale, most, pieces=(), kind=jnp.bfloat16):
    result = scale * jax.random.normal(rng, shape, jnp.float32)
    if pieces:
        result = result * block_levels(rng, shape, pieces, -0.22, 0.18)
    return jnp.clip(result, -most, most).astype(kind)


def setup_inputs(seed: int = 0) -> dict:
    seeds = jax.random.split(jax.random.key(seed), 15)
    tokens = normal_values(seeds[0], (TOKENS, D), 1.0, 6.0, ((0, 32),))
    segment_ids = jax.vmap(lambda own: jnp.searchsorted(jnp.cumsum(ragged_sizes(own, 6, LENGTH, LENGTH // 2, 1)), jnp.arange(LENGTH), side="right"))(jax.random.split(seeds[1], SEQS)).reshape((SEQS, LENGTH)).astype(jnp.int32)
    attn_gain = jnp.clip(1.0 + 0.15 * jax.random.normal(seeds[2], (D,), jnp.float32), 0.25, 1.75)
    w_query = normal_values(seeds[3], (D, HEADS * HEAD), D ** -0.5, 0.1875, ((0, 4),))
    w_key = normal_values(seeds[4], (D, KV_HEADS * HEAD), D ** -0.5, 0.1875, ((0, 4),))
    w_value = normal_values(seeds[5], (D, KV_HEADS * HEAD), D ** -0.5, 0.1875, ((0, 4),))
    query_gain = jnp.clip(1.0 + 0.18 * jax.random.normal(seeds[6], (HEAD,), jnp.float32), 0.1, 1.9)
    key_gain = jnp.clip(1.0 + 0.18 * jax.random.normal(seeds[7], (HEAD,), jnp.float32), 0.1, 1.9)
    w_out = normal_values(seeds[8], (HEADS * HEAD, D), (HEADS * HEAD // 16) ** -0.5, 0.5, ((0, 4),))
    mlp_gain = jnp.clip(1.0 + 0.15 * jax.random.normal(seeds[9], (D,), jnp.float32), 0.25, 1.75)
    w_gate = normal_values(seeds[10], (D, FF), D ** -0.5, 0.1875, ((0, 4),))
    w_up = normal_values(seeds[11], (D, FF), D ** -0.5, 0.1875, ((0, 4),))
    w_down = normal_values(seeds[12], (FF, D), (FF // 4) ** -0.5, 0.21875, ((0, 4),))
    cotangent = normal_values(seeds[13], (TOKENS, D), 1.0, 6.0, ((0, 32),))
    return dict(tokens=tokens, segment_ids=segment_ids, attn_gain=attn_gain, w_query=w_query, w_key=w_key, w_value=w_value, query_gain=query_gain, key_gain=key_gain, w_out=w_out, mlp_gain=mlp_gain, w_gate=w_gate, w_up=w_up, w_down=w_down, cotangent=cotangent)


epsilon = 1e-06
rope_base = 1000000.0
masked_score = -1e+30
highest = lax.Precision.HIGHEST

@jax.custom_vjp
def low(v):
    return lax.optimization_barrier(v.astype(jnp.bfloat16)).astype(jnp.float32)

@jax.custom_vjp
def low_back(v):
    return v

def low_keep(v):
    return (low(v), None)

def low_pass(kept, grad):
    return (grad,)

def back_keep(v):
    return (v, None)

def back_low(kept, grad):
    return (low(grad),)
low.defvjp(low_keep, low_pass)
low_back.defvjp(back_keep, back_low)

def matmul(left, right):
    return jnp.dot(left, right, precision=highest, preferred_element_type=jnp.float32)

def norm_rows(values, gain):
    return values * lax.rsqrt(lax.optimization_barrier(jnp.mean(values * values, axis=-1, keepdims=True)) + epsilon) * gain

def positions(segment_row):
    index_row = jnp.arange(segment_row.shape[0], dtype=jnp.int32)
    change = jnp.concatenate([jnp.ones((1,), dtype=jnp.bool_), segment_row[1:] != segment_row[:-1]])
    starting = lax.cummax(jnp.where(change, index_row, jnp.zeros_like(index_row)), axis=0)
    return index_row - starting

def rotary_tables(segment_row):
    half_dim = HEAD // 2
    freqs = rope_base ** (-2.0 * jnp.arange(half_dim, dtype=jnp.float32) / HEAD)
    angles = positions(segment_row).astype(jnp.float32)[:, None] * freqs[None, :]
    return (jnp.cos(angles), jnp.sin(angles))

def apply_rotary(values, cosine, sine):
    half_dim = values.shape[-1] // 2
    first_half = values[..., :half_dim]
    second_half = values[..., half_dim:]
    return jnp.concatenate([first_half * cosine - second_half * sine, second_half * cosine + first_half * sine], axis=-1)

def causal_mask(segment_row):
    index_row = jnp.arange(segment_row.shape[0], dtype=jnp.int32)
    return (index_row[None, :] <= index_row[:, None]) & (segment_row[:, None] == segment_row[None, :])

def attend_sequence(q_lin, k_lin, v_lin, query_gain, key_gain, segment_row):
    length = segment_row.shape[0]
    cosine, sine = rotary_tables(segment_row)
    cosine = cosine[:, None, :]
    sine = sine[:, None, :]
    queries = low(apply_rotary(norm_rows(q_lin.reshape(length, HEADS, HEAD), query_gain), cosine, sine))
    key_rows = low(apply_rotary(norm_rows(k_lin.reshape(length, KV_HEADS, HEAD), key_gain), cosine, sine))
    value_rows = v_lin.reshape(length, KV_HEADS, HEAD)
    grouped = queries.reshape(length, KV_HEADS, HEADS // KV_HEADS, HEAD)
    raw_scores = jnp.einsum('qkgd,tkd->kgqt', grouped, key_rows, precision=highest)
    scores = low_back(jnp.where(causal_mask(segment_row), raw_scores * HEAD ** (-0.5), masked_score))
    row_max = lax.optimization_barrier(jnp.max(scores, axis=-1, keepdims=True))
    exponent = jnp.exp(scores - row_max)
    attention = low(exponent / lax.optimization_barrier(jnp.sum(exponent, axis=-1, keepdims=True)))
    mixed_rows = jnp.einsum('kgqt,tkd->qkgd', attention, value_rows, precision=highest)
    return mixed_rows.reshape(length, HEADS * HEAD)

def layer(inputs, attn_gain, w_query, w_key, w_value, query_gain, key_gain, w_out, mlp_gain, w_gate, w_up, w_down, segments):
    count, length = segments.shape
    flat = inputs.reshape(count * length, D)
    normed_in = low(norm_rows(flat, attn_gain))
    q_lin = low_back(matmul(normed_in, w_query))
    k_lin = low_back(matmul(normed_in, w_key))
    v_lin = low(low_back(matmul(normed_in, w_value)))

    def per_sequence(q_part, k_part, v_part, segment_row):
        return attend_sequence(q_part, k_part, v_part, query_gain, key_gain, segment_row)
    mixed = jax.vmap(per_sequence)(q_lin.reshape(count, length, HEADS * HEAD), k_lin.reshape(count, length, KV_HEADS * HEAD), v_lin.reshape(count, length, KV_HEADS * HEAD), segments)
    mixed = low(low_back(mixed.reshape(count * length, HEADS * HEAD)))
    hidden = flat + low_back(matmul(mixed, w_out))
    normed_mid = low(norm_rows(hidden, mlp_gain))
    gate = low_back(matmul(normed_mid, w_gate))
    up_rows = low_back(matmul(normed_mid, w_up))
    product = low(jax.nn.silu(gate) * up_rows)
    output = hidden + low_back(matmul(product, w_down))
    return output.reshape(count, length, D)

def reference(tokens, segment_ids, attn_gain, w_query, w_key, w_value, query_gain, key_gain, w_out, mlp_gain, w_gate, w_up, w_down, cotangent):
    params = tuple((w.astype(jnp.float32) for w in (attn_gain, w_query, w_key, w_value, query_gain, key_gain, w_out, mlp_gain, w_gate, w_up, w_down)))
    per_group = math.gcd(SEQS, max(1, 4096 // LENGTH))
    groups = SEQS // per_group
    inputs = tokens.astype(jnp.float32).reshape(groups, per_group, LENGTH, D)
    cots = cotangent.astype(jnp.float32).reshape(groups, per_group, LENGTH, D)
    segs = segment_ids.reshape(groups, per_group, LENGTH)

    def step(totals, item):
        block_in, block_seg, block_cot = item

        def forward(block_x, *weights):
            return layer(block_x, *weights, block_seg)
        output, pull = jax.vjp(forward, block_in, *params)
        grads = pull(block_cot)
        totals = tuple((t + g for t, g in zip(totals, grads[1:])))
        return (totals, (output.astype(jnp.bfloat16), grads[0].astype(jnp.bfloat16)))
    initial = tuple((jnp.zeros_like(w) for w in params))
    totals, (outputs, in_grads) = lax.scan(step, initial, (inputs, segs, cots))
    return (outputs.reshape(TOKENS, D), in_grads.reshape(TOKENS, D), totals[0], totals[1], totals[2], totals[3], totals[4], totals[5], totals[6], totals[7], totals[8], totals[9], totals[10])
```

```python
import jax
import jax.numpy as jnp
from jax import lax
from jax.sharding import Mesh
from jax.sharding import PartitionSpec as P

HEADS = 16
KV_HEADS = 8
HEAD = 128
GROUP = HEADS // KV_HEADS

EPS = 1e-06
ROPE_BASE = 1000000.0
MASKED = -1e30
SCALE = HEAD ** (-0.5)
BF = jnp.bfloat16
F32 = jnp.float32
SWAP = [(0, 1), (1, 0)]


def dot(a, b):
    return jnp.dot(a, b, preferred_element_type=F32)


def dot_nt(a, b):
    return lax.dot_general(a, b, (((1,), (1,)), ((), ())), preferred_element_type=F32)


def dot_tn(a, b):
    return lax.dot_general(a, b, (((0,), (0,)), ((), ())), preferred_element_type=F32)


def swap(a, axis):
    return lax.ppermute(a, axis, SWAP)


class Plane:
    def __init__(self, ny, nx):
        self.ny, self.nx, self.n = ny, nx, ny * nx
        self.square = ny == 2 and nx == 2
        self.axes = ("y", "x")

    def index(self):
        return lax.axis_index("y") * self.nx + lax.axis_index("x")

    def gather(self, a):
        if not self.square:
            g = lax.all_gather(a, self.axes, axis=0, tiled=False)
            return [g[i] for i in range(self.n)]
        half = a.shape[0] // 32 * 16
        ax, ay = swap(a, "x"), swap(a, "y")
        d0, d1 = swap(ay[:half], "x"), swap(ax[half:], "y")
        return [a, ax, ay, jnp.concatenate([d0, d1], 0)]

    def scatter(self, blocks):
        if not self.square:
            s = jnp.concatenate(blocks, 0).astype(BF)
            return lax.psum_scatter(s, self.axes, scatter_dimension=0, tiled=True).astype(F32)
        own, bx, by, bd = blocks
        half = own.shape[0] // 2
        low = bd.astype(BF)
        fx, fy = swap(low[:half], "x"), swap(low[half:], "y")
        bx = jnp.concatenate([bx[:half].astype(BF), (bx[half:] + fy.astype(F32)).astype(BF)], 0)
        by = jnp.concatenate([(by[:half] + fx.astype(F32)).astype(BF), by[half:].astype(BF)], 0)
        rx, ry = swap(bx, "x"), swap(by, "y")
        return own + rx.astype(F32) + ry.astype(F32)

    def absolute(self, blocks):
        if not self.square:
            return blocks
        xb, yb = lax.axis_index("x") == 1, lax.axis_index("y") == 1
        a0, a1 = jnp.where(xb, blocks[1], blocks[0]), jnp.where(xb, blocks[0], blocks[1])
        a2, a3 = jnp.where(xb, blocks[3], blocks[2]), jnp.where(xb, blocks[2], blocks[3])
        return [jnp.where(yb, a2, a0), jnp.where(yb, a3, a1), jnp.where(yb, a0, a2), jnp.where(yb, a1, a3)]

    def exchange(self, a):
        if not self.square:
            return lax.all_to_all(a, self.axes, split_axis=0, concat_axis=0, tiled=True)
        t = self.index()
        pick = lambda k: lax.dynamic_index_in_dim(a, jnp.bitwise_xor(t, k), 0, keepdims=False)
        got = [
            pick(0),
            swap(pick(1), "x"),
            swap(pick(2), "y"),
            lax.ppermute(pick(3), self.axes, [(i, 3 - i) for i in range(4)]),
        ]
        return jnp.stack(self.absolute(got), 0)


def norm_parts(v):
    return lax.rsqrt(jnp.mean(v * v, axis=-1, keepdims=True) + EPS)


def norm_back(v, r, gain, d):
    dg = d * gain
    return r * (dg - v * (r * r) * jnp.mean(dg * v, axis=-1, keepdims=True))


def make_body(size, plane, halves):
    n = plane.n

    def body(tokens, segment_ids, attn_gain, w_query, w_key, w_value, query_gain, key_gain,
             w_out, mlp_gain, w_gate, w_up, w_down, cotangent):
        t = plane.index()
        c = lax.axis_index("c") if halves else 0
        parts = 2 if halves else 1
        rows, width = tokens.shape
        length = segment_ids.shape[1]
        assert rows == length
        kv_local = KV_HEADS // n // parts

        def cols(w):
            per = w.shape[1] // n
            h = per // parts
            return lax.dynamic_slice_in_dim(w, t * per + c * h, h, axis=1)

        def row_piece(w):
            q = w.shape[0] // parts // n
            return lax.dynamic_slice_in_dim(w, c * (n * q) + t * q, q, axis=0)

        def both(a):
            return [a, swap(a, "c")] if halves else [a]

        qkv_piece = jnp.concatenate([cols(w_query), cols(w_key), cols(w_value)], 1)
        wqkv = both(lax.all_gather(qkv_piece, "shard", axis=0, tiled=True))
        out_rows, down_rows = w_out.shape[0] // parts // n, w_down.shape[0] // parts // n
        od_piece = jnp.concatenate([row_piece(w_out), row_piece(w_down)], 0)
        od = lax.all_gather(od_piece, "shard", axis=0, tiled=False)
        gu_piece = jnp.concatenate([cols(w_gate), cols(w_up)], 1)
        wgu = both(lax.all_gather(gu_piece, "shard", axis=0, tiled=True))
        od = plane.exchange(od)
        od = both(od)
        wo = [w[:, :out_rows].reshape(n * out_rows, width) for w in od]
        wd = [w[:, out_rows:].reshape(n * down_rows, width) for w in od]

        seg_rows = jnp.pad(segment_ids.astype(BF), ((0, 15), (0, width - length)))
        ext = plane.gather(jnp.concatenate([tokens, seg_rows], 0))
        x_all = jnp.concatenate([b[:rows] for b in ext], 0)
        segs = jnp.stack([b[rows, :length] for b in ext], 0).astype(jnp.int32)
        cot_all = jnp.concatenate(plane.gather(cotangent), 0)
        x32 = x_all.astype(F32)
        r_in = norm_parts(x32)
        normed_in = (x32 * r_in * attn_gain).astype(BF)

        idx = jnp.arange(length, dtype=jnp.int32)
        start = jnp.sum((segs[:, None, :] < segs[:, :, None]).astype(jnp.int32), axis=-1)
        pos = idx[None, :] - start
        freqs = ROPE_BASE ** (-2.0 * jnp.arange(HEAD // 2, dtype=F32) / HEAD)
        ang = pos.astype(F32)[:, :, None] * freqs
        cos, sin = jnp.cos(ang)[:, :, None], jnp.sin(ang)[:, :, None]
        mask = (idx[None, :] <= idx[:, None])[None] & (segs[:, :, None] == segs[:, None, :])

        def rot(u):
            u1, u2 = u[..., : HEAD // 2], u[..., HEAD // 2 :]
            return jnp.concatenate([u1 * cos - u2 * sin, u2 * cos + u1 * sin], -1)

        def rot_back(u):
            u1, u2 = u[..., : HEAD // 2], u[..., HEAD // 2 :]
            return jnp.concatenate([u1 * cos + u2 * sin, u2 * cos - u1 * sin], -1)

        nq = kv_local * GROUP
        kept, mixed, partial = [], [], 0.0
        for h in range(parts):
            lin = dot(normed_in, wqkv[h])
            q = lin[:, : nq * HEAD].reshape(n, length, nq, HEAD)
            k = lin[:, nq * HEAD : (nq + kv_local) * HEAD].reshape(n, length, kv_local, HEAD)
            v = lin[:, (nq + kv_local) * HEAD :].astype(BF).reshape(n, length, kv_local, HEAD)
            rq, rk = norm_parts(q), norm_parts(k)
            qr = rot(q * rq * query_gain).astype(BF).reshape(n, length, kv_local, GROUP, HEAD)
            kr = rot(k * rk * key_gain).astype(BF)
            s = jnp.einsum("sqkgd,stkd->skgqt", qr, kr, preferred_element_type=F32)
            s = jnp.where(mask[:, None, None], s * SCALE, MASKED)
            e = jnp.exp(s - jnp.max(s, axis=-1, keepdims=True))
            p = e / jnp.sum(e, axis=-1, keepdims=True)
            m = jnp.einsum("skgqt,stkd->sqkgd", p.astype(BF), v, preferred_element_type=F32)
            m = m.astype(BF).reshape(n * length, nq * HEAD)
            kept.append((q, k, v, rq, rk, qr, kr, p))
            mixed.append(m)
            partial = partial + dot(m, wo[h])

        split = lambda a: [a[i * rows : (i + 1) * rows] for i in range(n)]
        hidden = tokens.astype(F32) + plane.scatter(split(partial))
        r_mid = norm_parts(hidden)
        normed_mid = jnp.concatenate(plane.gather((hidden * r_mid * mlp_gain).astype(BF)), 0)

        ff = wd[0].shape[0]
        partial, d_mid, gu_terms, down_terms = 0.0, 0.0, [], []
        for h in range(parts):
            gu = dot(normed_mid, wgu[h])
            gate, up = gu[:, :ff], gu[:, ff:]
            sg = jax.nn.sigmoid(gate)
            act = gate * sg
            product = (act * up).astype(BF)
            partial = partial + dot(product, wd[h])
            dp = dot_nt(cot_all, wd[h])
            d_up = (dp * act).astype(BF)
            d_gate = (dp * up * (sg + act * (1.0 - sg))).astype(BF)
            dgu = jnp.concatenate([d_gate, d_up], 1)
            d_mid = d_mid + dot_nt(dgu, wgu[h])
            gu_terms.append(dot_tn(normed_mid, dgu))
            down_terms.append(dot_tn(product, cot_all))
        d_mid = plane.scatter(split(d_mid))
        activations = (hidden + plane.scatter(split(partial))).astype(BF)

        def owned(terms):
            if halves:
                return (terms[0] + swap(terms[1].astype(BF), "c").astype(F32)).astype(BF)
            return lax.psum(terms[0].astype(BF), "c")

        def reduce_cols(terms):
            return lax.psum_scatter(owned(terms), "shard", scatter_dimension=0, tiled=True)

        def reduce_rows(terms):
            a = owned(terms)
            a = plane.exchange(a.reshape(n, a.shape[0] // n, width))
            return lax.psum_scatter(a.reshape(-1, width), "shard", scatter_dimension=0, tiled=True)

        def spread(piece):
            got = [jnp.stack(plane.absolute(plane.gather(piece)), 0)]
            if halves:
                got.append(swap(got[0], "c"))
                first = c == 0
                got = [jnp.where(first, got[0], got[1]), jnp.where(first, got[1], got[0])]
            return jnp.stack(got, 0).astype(F32)

        down_piece = reduce_rows(down_terms)
        gu_piece = reduce_cols(gu_terms)

        dh_norm = norm_back(hidden, r_mid, mlp_gain, d_mid)
        mlp_gain_grad = jnp.sum(d_mid * hidden * r_mid, axis=0)
        d_hidden = cotangent.astype(F32) + dh_norm
        dh_low = jnp.concatenate(plane.gather(d_hidden.astype(BF)), 0)

        d_in, qkv_terms, out_terms, qg_grad, kg_grad = 0.0, [], [], 0.0, 0.0
        for h in range(parts):
            q, k, v, rq, rk, qr, kr, p = kept[h]
            out_terms.append(dot_tn(mixed[h], dh_low))
            dm = dot_nt(dh_low, wo[h]).astype(BF).reshape(n, length, kv_local, GROUP, HEAD)
            da = jnp.einsum("sqkgd,stkd->skgqt", dm, v, preferred_element_type=F32)
            dv = jnp.einsum("skgqt,sqkgd->stkd", p.astype(BF), dm, preferred_element_type=F32)
            ds = (p * (da - jnp.sum(p * da, axis=-1, keepdims=True))).astype(BF)
            dq = SCALE * jnp.einsum("skgqt,stkd->sqkgd", ds, kr, preferred_element_type=F32)
            dk = SCALE * jnp.einsum("skgqt,sqkgd->stkd", ds, qr, preferred_element_type=F32)
            dq = rot_back(dq.reshape(n, length, nq, HEAD))
            dk = rot_back(dk)
            qg_grad = qg_grad + jnp.sum(dq * q * rq, axis=(0, 1, 2))
            kg_grad = kg_grad + jnp.sum(dk * k * rk, axis=(0, 1, 2))
            dq = norm_back(q, rq, query_gain, dq).astype(BF)
            dk = norm_back(k, rk, key_gain, dk).astype(BF)
            flat = lambda a: a.reshape(n * length, -1)
            dqkv = jnp.concatenate([flat(dq), flat(dk), flat(dv.astype(BF))], 1)
            qkv_terms.append(dot_tn(normed_in, dqkv))
            d_in = d_in + dot_nt(dqkv, wqkv[h])
        out_piece = reduce_rows(out_terms)
        qkv_piece = reduce_cols(qkv_terms)
        attn_gain_grad = jnp.sum(d_in * (x32 * r_in), axis=0)
        d_in = plane.scatter(split(d_in))
        x_own = tokens.astype(F32)
        input_grad = (d_hidden + norm_back(x_own, norm_parts(x_own), attn_gain, d_in)).astype(BF)

        gains = lax.psum(
            jnp.concatenate([attn_gain_grad, mlp_gain_grad, qg_grad, kg_grad]),
            ("shard", "y", "x", "c"),
        )
        cuts = [width, 2 * width, 2 * width + HEAD]
        attn_gain_grad, mlp_gain_grad, qg_grad, kg_grad = jnp.split(gains, cuts)

        def place_cols(a):
            return a.transpose(2, 1, 0, 3).reshape(a.shape[2], -1)

        qkv = spread(qkv_piece)
        gu = spread(gu_piece)
        a, b = nq * HEAD, (nq + kv_local) * HEAD
        return (
            activations,
            input_grad,
            attn_gain_grad,
            place_cols(qkv[..., :a]),
            place_cols(qkv[..., a:b]),
            place_cols(qkv[..., b:]),
            qg_grad,
            kg_grad,
            spread(out_piece).reshape(-1, width),
            mlp_gain_grad,
            place_cols(gu[..., :ff]),
            place_cols(gu[..., ff:]),
            spread(down_piece).reshape(-1, width),
        )

    return body


def solution(mesh):
    size, replicas = mesh.shape["shard"], mesh.shape["replica"]
    ny, nx = replicas // 4, 2
    assert size == ny * nx
    plane = Plane(ny, nx)
    fine = Mesh(mesh.devices.reshape(size, ny, nx, 2), ("shard", "y", "x", "c"))
    halves = KV_HEADS % (2 * plane.n) == 0
    every = P(("shard", "y", "x", "c"), None)
    shard, copy = P("shard", None), P()
    return jax.shard_map(
        make_body(size, plane, halves),
        mesh=fine,
        in_specs=(every, every, copy, shard, shard, shard, copy, copy, shard, copy, shard, shard, shard, every),
        out_specs=(every, every, copy, shard, shard, shard, copy, copy, shard, copy, shard, shard, shard),
        check_vma=False,
    )
```

```python
import functools
import math

import jax
import jax.numpy as jnp
from jax import lax
from jax.experimental import pallas as pl
from jax.experimental.pallas import tpu as pltpu
from jax.sharding import Mesh
from jax.sharding import PartitionSpec as P

HEADS = 16
KV_HEADS = 8
HEAD = 128
GROUP = HEADS // KV_HEADS

EPS = 1e-06
ROPE_BASE = 1000000.0
MASKED = -1e30
SCALE = HEAD ** (-0.5)
BF = jnp.bfloat16
F32 = jnp.float32
SWAP = [(0, 1), (1, 0)]
B = 256


def dot(a, b):
    return jnp.dot(a, b, preferred_element_type=F32)


def dot_nt(a, b):
    return lax.dot_general(a, b, (((1,), (1,)), ((), ())), preferred_element_type=F32)


def dot_tn(a, b):
    return lax.dot_general(a, b, (((0,), (0,)), ((), ())), preferred_element_type=F32)


def swap(a, axis):
    return lax.ppermute(a, axis, SWAP)


tie = lax.optimization_barrier


def sds(shape, dtype):
    return jax.ShapeDtypeStruct(shape, dtype)


def hbm(shape, dtype):
    return pltpu.HBM(shape, dtype)


VM = pl.BlockSpec(memory_space=pltpu.VMEM)
SM = pl.BlockSpec(memory_space=pltpu.SMEM)


def kernel_call(body, outs, args, flops=0, scalars=0, **kw):
    moved = sum(a.size * a.dtype.itemsize for a in args) + sum(math.prod(o.shape) * o.dtype.itemsize for o in outs)
    if "grid" not in kw:
        kw = dict(in_specs=[SM] * scalars + [VM] * (len(args) - scalars), out_specs=[VM] * len(outs))
    return pl.pallas_call(
        body,
        out_shape=outs,
        compiler_params=pltpu.CompilerParams(vmem_limit_bytes=44 * 1024 * 1024),
        cost_estimate=pl.CostEstimate(flops=flops, bytes_accessed=moved, transcendentals=0),
        **kw,
    )(*args)


class Plane:
    def __init__(self, ny, nx):
        self.ny, self.nx, self.n = ny, nx, ny * nx
        self.square = ny == 2 and nx == 2
        self.axes = ("y", "x")

    def index(self):
        return lax.axis_index("y") * self.nx + lax.axis_index("x")

    def place(self, t, r):
        return jnp.bitwise_xor(t, r) if self.square else r

    def gather(self, top, low):
        if not self.square:
            g, h = (lax.all_gather(a, self.axes, axis=0, tiled=False) for a in (top, low))
            return [[g[i], h[i]] for i in range(self.n)]
        ty, lx = swap(top, "y"), swap(low, "x")
        tx, ly = swap(top, "x"), swap(low, "y")
        return [[top, low], [tx, lx], [ty, ly], [swap(ty, "x"), swap(lx, "y")]]

    def gather_whole(self, a):
        if not self.square:
            g = lax.all_gather(a, self.axes, axis=0, tiled=False)
            return [g[i] for i in range(self.n)]
        return [a, swap(a, "x"), swap(a, "y"), lax.ppermute(a, self.axes, [(i, 3 - i) for i in range(4)])]

    def scatter(self, blocks):
        if not self.square:
            a = jnp.concatenate([h for b in blocks for h in b], 0)
            a = lax.psum_scatter(a, self.axes, scatter_dimension=0, tiled=True)
            return [[a[: a.shape[0] // 2]], [a[a.shape[0] // 2 :]]]
        own, bx, by, bd = blocks
        fx, fy = swap(bd[0], "x"), swap(bd[1], "y")
        xt, yl = swap(bx[0], "x"), swap(by[1], "y")
        add = lambda u, v: (u.astype(F32) + v.astype(F32)).astype(BF)
        yt, xl = swap(add(by[0], fx), "y"), swap(add(bx[1], fy), "x")
        return [[own[0], xt, yt], [own[1], xl, yl]]

    def exchange(self, slice_for):
        if not self.square:
            a = jnp.stack([slice_for(i) for i in range(self.n)], 0)
            a = lax.all_to_all(a, self.axes, split_axis=0, concat_axis=0, tiled=True)
            return [a[i] for i in range(self.n)]
        t = self.index()
        return [
            slice_for(t),
            swap(slice_for(jnp.bitwise_xor(t, 1)), "x"),
            swap(slice_for(jnp.bitwise_xor(t, 2)), "y"),
            lax.ppermute(slice_for(jnp.bitwise_xor(t, 3)), self.axes, [(i, 3 - i) for i in range(4)]),
        ]


def columns(ref, lo, count, rows):
    s = ref.shape[0]
    got = [ref[:, (lo + j) * rows : (lo + j + 1) * rows, :].reshape(s * rows, B) for j in range(count)]
    return got[0] if count == 1 else jnp.concatenate(got, 1)


def split(ref):
    return jnp.concatenate([ref[0][...], ref[1][...]], 0)


def put(halves, value):
    k = halves[0].shape[0]
    halves[0][...] = value[:k].astype(halves[0].dtype)
    halves[1][...] = value[k:].astype(halves[1].dtype)


def rsq(v):
    return lax.rsqrt(jnp.mean(v * v, axis=-1, keepdims=True) + EPS)


def norm_back(v, r, gain, d):
    dg = d * gain
    return r * (dg - v * (r * r) * jnp.mean(dg * v, axis=-1, keepdims=True))


def half_roll(u):
    return pltpu.roll(u, HEAD // 2, 1)


def prep_block(length, gain, freq, tok, cotseg, nin, cos, sin, mask):
    x = tok[...].astype(F32)
    nin[...] = (x * rsq(x) * gain[...]).astype(BF)
    row = cotseg[length : length + 16, :length].astype(F32)[:1]
    row = jnp.broadcast_to(row, (length, length))
    col = row.T
    start = jnp.sum(jnp.where(row < col, 1.0, 0.0), axis=-1, keepdims=True)
    i = lax.broadcasted_iota(jnp.int32, (length, length), 0)
    j = lax.broadcasted_iota(jnp.int32, (length, length), 1)
    mask[...] = jnp.where((j <= i) & (row == col), 1.0, 0.0)
    pos = lax.broadcasted_iota(jnp.int32, (length, HEAD), 0).astype(F32) - start
    ang = pos * freq[...]
    lane = lax.broadcasted_iota(jnp.int32, (length, HEAD), 1)
    s = jnp.sin(ang)
    cos[...] = jnp.cos(ang)
    sin[...] = jnp.where(lane < HEAD // 2, -s, s)


def soft(qr, kr, mask):
    s = jnp.where(mask, dot_nt(qr, kr) * SCALE, MASKED)
    e = jnp.exp(s - jnp.max(s, axis=-1, keepdims=True))
    return e * (1.0 / jnp.sum(e, axis=-1, keepdims=True))


def attend_block(parts, wrows, qg, kg, wa, wo, nin, cos, sin, mask, lin, vals, mixed, out0, out1):
    keep = mask[...] > 0.0
    c, s = cos[...], sin[...]
    rot = lambda u: u * c + half_roll(u) * s
    n = nin[...]
    out = None
    for h in range(parts):
        q = dot(n, columns(wa[h], 0, 1, wrows))
        kv = dot(n, columns(wa[h], 1, 1, wrows))
        k, v = kv[:, :HEAD], kv[:, HEAD:].astype(BF)
        lin[:, h * 3 * HEAD : h * 3 * HEAD + 2 * HEAD] = q
        lin[:, h * 3 * HEAD + 2 * HEAD : (h + 1) * 3 * HEAD] = k
        vals[:, h * HEAD : (h + 1) * HEAD] = v
        kr = rot(k * rsq(k) * kg[...]).astype(BF)
        for g in range(GROUP):
            qh = q[:, g * HEAD : (g + 1) * HEAD]
            p = soft(rot(qh * rsq(qh) * qg[...]).astype(BF), kr, keep)
            at = h * GROUP * HEAD + g * HEAD
            mixed[:, at : at + HEAD] = dot(p.astype(BF), v).astype(BF)
        term = dot(mixed[:, h * GROUP * HEAD : (h + 1) * GROUP * HEAD], wo[h][...])
        out = term if out is None else out + term
    put((out0, out1), out)


def mlp_block(parts, wrows, ff, wgu, wd, nm0, nm1, cotseg, product, dgu, out0, out1, dm0, dm1):
    n, ct = split((nm0, nm1)), cotseg[: 2 * nm0.shape[0], :]
    out, dm = None, None
    for h in range(parts):
        w = columns(wgu[h], 0, 2 * ff // B, wrows)
        d = wd[h][...]
        gu = dot(n, w)
        gate, up = gu[:, :ff], gu[:, ff:]
        sg = jax.nn.sigmoid(gate)
        act = gate * sg
        pr = (act * up).astype(BF)
        product[:, h * ff : (h + 1) * ff] = pr
        dp = dot_nt(ct, d)
        d_gate = (dp * up * (sg + act * (1.0 - sg))).astype(BF)
        d_up = (dp * act).astype(BF)
        at = h * 2 * ff
        dgu[:, at : at + ff] = d_gate
        dgu[:, at + ff : at + 2 * ff] = d_up
        a, b = dot(pr, d), dot_nt(dgu[:, at : at + 2 * ff], w)
        out = a if out is None else out + a
        dm = b if dm is None else dm + b
    put((out0, out1), out)
    put((dm0, dm1), dm)


def attend_back_block(parts, wrows, qg, kg, wa, wo, dh0, dh1, tok, lin, vals, cos, sin, mask, dqkv, din0, din1, gains):
    keep = mask[...] > 0.0
    c, s = cos[...], sin[...]
    rot = lambda u: u * c + half_roll(u) * s
    rot_back = lambda u: u * c - half_roll(u) * s
    d = split((dh0, dh1))
    din, qgain, kgain = None, 0.0, 0.0
    for h in range(parts):
        dm = dot_nt(d, wo[h][...]).astype(BF)
        base = h * 3 * HEAD
        k = lin[:, base + 2 * HEAD : base + 3 * HEAD]
        v = vals[:, h * HEAD : (h + 1) * HEAD]
        rk = rsq(k)
        kr = rot(k * rk * kg[...]).astype(BF)
        dk, dv = 0.0, 0.0
        at = h * 4 * HEAD
        for g in range(GROUP):
            q = lin[:, base + g * HEAD : base + (g + 1) * HEAD]
            rq = rsq(q)
            qr = rot(q * rq * qg[...]).astype(BF)
            p = soft(qr, kr, keep)
            dmh = dm[:, g * HEAD : (g + 1) * HEAD]
            da = dot_nt(dmh, v)
            dv = dv + dot_tn(p.astype(BF), dmh)
            ds = (p * (da - jnp.sum(p * da, axis=-1, keepdims=True))).astype(BF)
            dq = rot_back(dot(ds, kr) * SCALE)
            dk = dk + dot_tn(ds, qr)
            qgain = qgain + jnp.sum(dq * q * rq, axis=0, keepdims=True)
            dqkv[:, at + g * HEAD : at + (g + 1) * HEAD] = norm_back(q, rq, qg[...], dq).astype(BF)
        dk = rot_back(dk * SCALE)
        kgain = kgain + jnp.sum(dk * k * rk, axis=0, keepdims=True)
        dqkv[:, at + 2 * HEAD : at + 3 * HEAD] = norm_back(k, rk, kg[...], dk).astype(BF)
        dqkv[:, at + 3 * HEAD : at + 4 * HEAD] = dv.astype(BF)
        term = dot_nt(dqkv[:, at : at + 4 * HEAD], columns(wa[h], 0, 2, wrows))
        din = term if din is None else din + term
    put((din0, din1), din)
    x = tok[...].astype(F32)
    width = x.shape[1]
    gains[:, :width] += jnp.sum(din * (x * rsq(x)), axis=0, keepdims=True)
    gains[:, width : width + HEAD] += qgain
    gains[:, width + HEAD :] += kgain


def added(refs):
    total = refs[0][...].astype(F32)
    for r in refs[1:]:
        total = total + r[...].astype(F32)
    return total


def mid_kernel(nterms, tokens, gain, *refs):
    terms, (hidden, nm0, nm1) = refs[: 2 * nterms], refs[2 * nterms :]
    half = tokens.shape[0] // 2
    for i, nm in enumerate((nm0, nm1)):
        at = slice(i * half, (i + 1) * half)
        h = tokens[at, :].astype(F32) + added(terms[i * nterms : (i + 1) * nterms])
        hidden[at, :] = h
        nm[...] = (h * rsq(h) * gain[...]).astype(BF)


def mid_back_kernel(nterms, hidden, cot, gain, *refs):
    terms, (d_hidden, low0, low1, ggrad) = refs[: 2 * nterms], refs[2 * nterms :]
    half = hidden.shape[0] // 2
    total = 0.0
    for i, low in enumerate((low0, low1)):
        at = slice(i * half, (i + 1) * half)
        d = added(terms[i * nterms : (i + 1) * nterms])
        h = hidden[at, :]
        r = rsq(h)
        out = cot[at, :].astype(F32) + norm_back(h, r, gain[...], d)
        d_hidden[at, :] = out
        low[...] = out.astype(BF)
        total = total + jnp.sum(d * h * r, axis=0, keepdims=True)
    ggrad[...] = total


def last_kernel(nterms, tokens, d_hidden, gain, *refs):
    terms, (out,) = refs[: 2 * nterms], refs[2 * nterms :]
    half = tokens.shape[0] // 2
    for i in range(2):
        at = slice(i * half, (i + 1) * half)
        x = tokens[at, :].astype(F32)
        d = added(terms[i * nterms : (i + 1) * nterms])
        out[at, :] = (d_hidden[at, :] + norm_back(x, rsq(x), gain[...], d)).astype(BF)


def out_kernel(nterms, hidden, *refs):
    terms, (out,) = refs[: 2 * nterms], refs[2 * nterms :]
    half = hidden.shape[0] // 2
    for i in range(2):
        at = slice(i * half, (i + 1) * half)
        out[at, :] = (hidden[at, :] + added(terms[i * nterms : (i + 1) * nterms])).astype(BF)


def arrange(plane, t, blocks, cb):
    q = blocks[0].shape[0] // cb

    def body(where, *refs):
        for r, ref in enumerate(refs[:-1]):
            start = pl.multiple_of(plane.place(where[0], r) * q, 16)
            for j in range(cb):
                refs[-1][pl.ds(start, q), j * B : (j + 1) * B] = ref[j * q : (j + 1) * q, :]

    return kernel_call(body, [sds((len(blocks) * q, cb * B), BF)], [t.astype(jnp.int32)[None], *blocks], scalars=1)[0]


def grad_columns(plane, t, lhs, rhs, half, width, size, other, below=None):
    nblk = width // B
    flat_l, flat_r = sum(lhs, []), sum(rhs, [])
    nl, nr = len(flat_l), len(flat_r)
    rows = flat_l[0].shape[1] // size
    more = 0 if below is None else below[0].shape[0]

    def body(where, *refs):
        left = jnp.concatenate([r[...] for r in refs[:nl]], 0)
        right = jnp.concatenate([r[...] for r in refs[nl : nl + nr]], 0)
        rest, out = refs[nl + nr : -1], refs[-1]
        got = dot_tn(left, right)
        for j in range(nblk):
            part = got[:, j * B : (j + 1) * B]
            if other is not None:
                part = part + rest[0][0, j * rows : (j + 1) * rows, :].astype(F32)
            out[0, j * rows : (j + 1) * rows, :] = part.astype(BF)
        if more:
            z = pl.program_id(0)
            for r in range(plane.n):
                @pl.when(plane.place(where[0], r) == z)
                def _():
                    out[0, nblk * rows :, :] = rest[-plane.n + r][...]

    tall = lambda k: pl.BlockSpec((1, k, B), lambda z, w: (z, 0, 0))
    in_specs = [pl.BlockSpec((a.shape[0], rows), lambda z, w: (0, z)) for a in flat_l]
    in_specs += [pl.BlockSpec((a.shape[0], width), lambda z, w: (0, half)) for a in flat_r]
    args = flat_l + flat_r
    if other is not None:
        in_specs.append(tall(nblk * rows))
        args = args + [other]
    if more:
        in_specs += [pl.BlockSpec((more, B), lambda z, w: (0, 0))] * plane.n
        args = args + below
    tokens = sum(a.shape[0] for a in flat_l)
    out = sds((size, nblk * rows + more, B), BF)
    return pl.pallas_call(
        body,
        out_shape=out,
        grid_spec=pltpu.PrefetchScalarGridSpec(
            num_scalar_prefetch=1, grid=(size,), in_specs=in_specs, out_specs=tall(nblk * rows + more)
        ),
        compiler_params=pltpu.CompilerParams(vmem_limit_bytes=44 * 1024 * 1024),
        cost_estimate=pl.CostEstimate(
            flops=2 * tokens * rows * size * width,
            bytes_accessed=sum(a.size * 2 for a in args) + math.prod(out.shape) * 2,
            transcendentals=0,
        ),
    )(t.astype(jnp.int32)[None], *args)


def grad_rows(lhs, rhs, tokens_each, half, width, n, other):
    flat_l, flat_r = lhs, sum(rhs, [])
    nl = len(flat_l)
    cb = flat_r[0].shape[1] // B
    q = width // n

    def body(*refs):
        left = jnp.concatenate([r[...] for r in refs[:nl]], 0)
        right = jnp.concatenate([r[...] for r in refs[nl : nl + len(flat_r)]], 0)
        got = dot_tn(left, right).reshape(n, q, B)
        if other is not None:
            got = got + refs[-2][...].astype(F32)
        refs[-1][...] = got.astype(BF)

    spec = pl.BlockSpec((n, q, B), lambda j: (0, j, 0))
    in_specs = [pl.BlockSpec((a.shape[0], width), lambda j: (0, half)) for a in flat_l]
    in_specs += [pl.BlockSpec((tokens_each, B), lambda j: (0, j)) for a in flat_r]
    args = flat_l + flat_r
    if other is not None:
        in_specs.append(spec)
        args = args + [other]
    tokens = sum(a.shape[0] for a in flat_l)
    return kernel_call(
        body, [sds((n, cb * q, B), BF)], args, flops=2 * tokens * width * cb * B,
        grid=(cb,), in_specs=in_specs, out_specs=[spec],
    )[0]


def over_blocks(block, shared, per_block, outs, flops, total=False):
    flat = []
    shape = []
    for a in shared:
        shape.append(len(a) if isinstance(a, list) else None)
        flat += a if isinstance(a, list) else [a]
    nb, k, o = len(per_block), len(per_block[0]), len(outs[0])
    args = flat + sum(per_block, [])
    out_shapes = sum(outs, []) + ([total] if total else [])

    def body(*refs):
        at, head = 0, []
        for m in shape:
            head.append(refs[at] if m is None else refs[at : at + m])
            at += 1 if m is None else m
        ins, results = refs[at : at + nb * k], refs[at + nb * k :]
        tail = ()
        if total:
            results[-1][...] = jnp.zeros_like(results[-1])
            tail = (results[-1],)
        for b in range(nb):
            block(*head, *ins[b * k : (b + 1) * k], *results[b * o : (b + 1) * o], *tail)

    got = kernel_call(body, out_shapes, args, flops=flops * nb)
    return [got[b * o : (b + 1) * o] for b in range(nb)], (got[-1] if total else None)


def make_body(size, plane, halves):
    n = plane.n
    parts = 2 if halves else 1
    first, rest = [n - 1], list(range(n - 1))[::-1]

    def body(tokens, segment_ids, attn_gain, w_query, w_key, w_value, query_gain, key_gain,
             w_out, mlp_gain, w_gate, w_up, w_down, cotangent):
        t = plane.index()
        c = lax.axis_index("c") if halves else 0
        rows, width = tokens.shape
        length = segment_ids.shape[1]
        assert rows == length
        half = rows // 2
        cb = width // B
        wrows = w_query.shape[0]
        cut_a, cut_b = 2 * wrows, 2 * w_gate.shape[1] // n // parts // B * wrows
        out_rows, down_rows = w_out.shape[0] // parts // n, w_down.shape[0] // parts // n
        ff = n * down_rows
        gain_in, gain_mid = attn_gain[None, :], mlp_gain[None, :]
        qg, kg = query_gain[None, :], key_gain[None, :]
        freq = ROPE_BASE ** (-2.0 * (jnp.arange(HEAD) % (HEAD // 2)).astype(F32) / HEAD)[None, :]

        def pick(col_weights, row_weight):
            each = [w.shape[1] // n // parts for w in col_weights]
            total = sum(each)
            q = row_weight.shape[0] // parts // n
            high = total // B * wrows
            where = jnp.stack([t * parts + c, c * n + t]).astype(jnp.int32)

            def fill(_, *refs):
                a = jnp.concatenate([r[...] for r in refs[:-2]], 1)
                for j in range(total // B):
                    refs[-1][j * wrows : (j + 1) * wrows, :] = a[:, j * B : (j + 1) * B]
                for j in range(cb):
                    refs[-1][high + j * q : high + (j + 1) * q, :] = refs[-2][:, j * B : (j + 1) * B]

            return pl.pallas_call(
                fill,
                out_shape=sds((high + cb * q, B), BF),
                grid_spec=pltpu.PrefetchScalarGridSpec(
                    num_scalar_prefetch=1,
                    grid=(1,),
                    in_specs=[pl.BlockSpec((wrows, k), lambda i, at: (0, at[0])) for k in each]
                    + [pl.BlockSpec((q, width), lambda i, at: (at[1], 0))],
                    out_specs=pl.BlockSpec((high + cb * q, B), lambda i, at: (0, 0)),
                ),
            )(where, *col_weights, row_weight)

        def both(a):
            return [a, swap(a, "c")] if halves else [a]

        def rows_to_chip(got, cut):
            blocks = plane.exchange(lambda i: lax.dynamic_slice_in_dim(got, i, 1, 0)[0, cut:])
            return arrange(plane, t, blocks, cb)

        got_a = lax.all_gather(pick([w_query, w_key, w_value], w_out), "shard", axis=0, tiled=False)

        seg_rows = jnp.pad(segment_ids.astype(BF), ((0, 15), (0, width - length)))
        ext = plane.gather(tokens, jnp.concatenate([cotangent, seg_rows], 0))
        tok, cot = [b[0] for b in ext], [b[1] for b in ext]
        w_gate, w_up, w_down, tok[n - 1] = tie((w_gate, w_up, w_down, tok[n - 1]))
        piece_b = pick([w_gate, w_up], w_down)
        prep, _ = over_blocks(
            functools.partial(prep_block, length), [gain_in, freq],
            [[tok[r], cot[r]] for r in range(n)],
            [[hbm((length, width), BF), hbm((length, HEAD), F32), hbm((length, HEAD), F32), hbm((length, length), F32)]] * n,
            0,
        )
        got_a, prep, piece_b = tie((got_a, prep, piece_b))
        nin, tables = [a[0] for a in prep], [a[1:] for a in prep]
        got_b = lax.all_gather(piece_b, "shard", axis=0, tiled=False)
        wa, wo = both(got_a), both(rows_to_chip(got_a, cut_a))

        def term_types(r):
            return [sds((half, width), F32 if r == 0 and plane.square else BF)] * 2

        def run(block, shared, ins, outs, flops, order, total=None, before=lambda got: None):
            got, totals = {}, []
            for group in order:
                res, tot = over_blocks(block, shared, [ins[r] for r in group], [outs(r) for r in group], flops, total)
                got.update(zip(group, res))
                totals.append(tot)
            return [[got[r][i] for r in range(n)] for i in range(len(outs(0)))], totals

        (lin, vals, mixed, o0, o1), _ = run(
            functools.partial(attend_block, parts, wrows), [qg, kg, wa, wo],
            [[nin[r], *tables[r]] for r in range(n)],
            lambda r: [hbm((length, parts * 3 * HEAD), F32), hbm((length, parts * HEAD), BF),
                       hbm((length, parts * GROUP * HEAD), BF), *term_types(r)],
            2 * length * width * parts * 6 * HEAD, [first, rest],
        )
        terms = plane.scatter(list(zip(o0, o1)))
        nterms = len(terms[0])
        hidden, nm0, nm1 = kernel_call(
            functools.partial(mid_kernel, nterms),
            [hbm((rows, width), F32), sds((half, width), BF), sds((half, width), BF)],
            [tokens, gain_mid, *terms[0], *terms[1]],
        )
        nm = plane.gather(nm0, nm1)
        got_b, nm = tie((got_b, nm))
        wgu, wd = both(got_b), both(rows_to_chip(got_b, cut_b))

        (product, dgu, o0, o1, m0, m1), _ = run(
            functools.partial(mlp_block, parts, wrows, ff), [wgu, wd],
            [[*nm[r], cot[r]] for r in range(n)],
            lambda r: [hbm((rows, parts * ff), BF), hbm((rows, parts * 2 * ff), BF),
                       *[hbm(o.shape, o.dtype) for o in term_types(r)], *term_types(r)],
            2 * length * width * parts * 7 * ff, [first, rest],
        )
        terms_mid = plane.scatter(list(zip(m0, m1)))

        def owned(make):
            if halves:
                return make(0, swap(make(1, None), "c"))
            return lax.psum(make(0, None), "c")

        down = owned(lambda h, o: grad_rows(product, [[a] for a in cot], rows, h, ff, n, o))
        gu_other = grad_columns(plane, t, nm, [[a] for a in dgu], 1, 2 * ff, size, None) if halves else None
        terms_mid, gu_other, down = tie((terms_mid, gu_other, down))
        d_hidden, dh0, dh1, mlp_grad = kernel_call(
            functools.partial(mid_back_kernel, nterms),
            [hbm((rows, width), F32), sds((half, width), BF), sds((half, width), BF), sds((1, width), F32)],
            [hidden, cotangent, gain_mid, *terms_mid[0], *terms_mid[1]],
        )
        dh = plane.gather(dh0, dh1)

        def merged(lhs, rhs, width_, other, low):
            low = plane.exchange(lambda i: lax.dynamic_index_in_dim(low, i, 0, keepdims=False))
            if halves:
                return grad_columns(plane, t, lhs, rhs, 0, width_, size, swap(other, "c"), low)
            a = grad_columns(plane, t, lhs, rhs, 0, width_, size, None)
            return jnp.concatenate([lax.psum(a, "c"), jnp.stack(low, 0)], 1)

        grads_b = merged(nm, [[a] for a in dgu], 2 * ff, gu_other, down)
        dh[n - 1], o0, o1, grads_b = tie((dh[n - 1], o0, o1, grads_b))
        grads_b = lax.psum_scatter(grads_b.reshape(-1, B), "shard", scatter_dimension=0, tiled=True)
        terms_out = plane.scatter(list(zip(o0, o1)))

        out = owned(lambda h, o: grad_rows(mixed, dh, half, h, GROUP * HEAD, n, o))
        (dqkv, i0, i1), gains = run(
            functools.partial(attend_back_block, parts, wrows), [qg, kg, wa, wo],
            [[*dh[r], tok[r], lin[r], vals[r], *tables[r]] for r in range(n)],
            lambda r: [hbm((rows, parts * 4 * HEAD), BF), *term_types(r)],
            2 * length * width * parts * 6 * HEAD, [[0], list(range(1, n))], sds((1, width + 2 * HEAD), F32),
        )
        dqkv = [[a] for a in dqkv]
        lhs = [[a] for a in nin]
        qkv_other = grad_columns(plane, t, lhs, dqkv, 1, 4 * HEAD, size, None) if halves else None
        grads_a = merged(lhs, dqkv, 4 * HEAD, qkv_other, out)
        grads_a, grads_b, terms_out = tie((grads_a, grads_b, terms_out))
        grads_a = lax.psum_scatter(grads_a.reshape(-1, B), "shard", scatter_dimension=0, tiled=True)

        activations = kernel_call(
            functools.partial(out_kernel, nterms), [sds((rows, width), BF)],
            [hidden, *terms_out[0], *terms_out[1]],
        )[0]
        terms_in = plane.scatter(list(zip(i0, i1)))
        input_grad = kernel_call(
            functools.partial(last_kernel, nterms),
            [sds((rows, width), BF)],
            [tokens, d_hidden, gain_in, *terms_in[0], *terms_in[1]],
        )[0]

        gains = jnp.concatenate([functools.reduce(jnp.add, gains), mlp_grad], 1)
        if plane.square and size == 4:
            for axis in ("c", "x", "y"):
                gains = gains + swap(gains, axis)
            for k in (1, 2):
                gains = gains + lax.ppermute(gains, "shard", [(i, i ^ k) for i in range(4)])
        else:
            gains = lax.psum(gains, ("shard", "y", "x", "c"))
        gains = gains[0]

        def assemble(piece, outs, write):
            mine = plane.gather_whole(piece)
            got = [(r, 0, a) for r, a in enumerate(mine)]
            if halves:
                got += [(r, 1, swap(a, "c")) for r, a in enumerate(mine)]

            def body(where, *refs):
                for (r, other, _), ref in zip(got, refs):
                    core = jnp.bitwise_xor(where[1], other) if halves else 0
                    write(ref, plane.place(where[0], r), core, refs[len(got) :])

            where = jnp.stack([t, c]).astype(jnp.int32)
            return kernel_call(body, outs, [where] + [a for _, _, a in got], scalars=1)

        def write_cols(ref, j, todo, src, core):
            a = ref[j * wrows : (j + 1) * wrows, :].astype(F32)
            for lo, hi, out, per, at in todo:
                start = pl.multiple_of((src * parts + core) * per + at, HEAD)
                out[:, pl.ds(start, hi - lo)] = a[:, lo:hi]

        def write_rows(ref, base, q, src, core, out):
            start = pl.multiple_of((core * n + src) * q, 16)
            for j in range(cb):
                a = ref[base + j * q : base + (j + 1) * q, :].astype(F32)
                out[pl.ds(start, q), j * B : (j + 1) * B] = a

        def write_b(ref, src, core, outs):
            gate, up, down = outs
            for j in range(2 * ff // B):
                todo = []
                for out, lo in ((gate, 0), (up, ff)):
                    a, b = max(j * B, lo), min((j + 1) * B, lo + ff)
                    if a < b:
                        todo.append((a - j * B, b - j * B, out, ff, a - lo))
                write_cols(ref, j, todo, src, core)
            write_rows(ref, cut_b, down_rows, src, core, down)

        def write_a(ref, src, core, outs):
            q, k, v, out = outs
            write_cols(ref, 0, [(0, B, q, B, 0)], src, core)
            write_cols(ref, 1, [(0, HEAD, k, HEAD, 0), (HEAD, B, v, HEAD, 0)], src, core)
            write_rows(ref, cut_a, out_rows, src, core, out)

        like = lambda w: sds(w.shape, F32)
        gate_g, up_g, down_g = assemble(grads_b, [like(w_gate), like(w_up), like(w_down)], write_b)
        grads_a, gate_g, up_g, down_g = tie((grads_a, gate_g, up_g, down_g))
        query_g, key_g, value_g, out_g = assemble(
            grads_a, [like(w_query), like(w_key), like(w_value), like(w_out)], write_a)

        return (
            activations,
            input_grad,
            gains[:width],
            query_g,
            key_g,
            value_g,
            gains[width : width + HEAD],
            gains[width + HEAD : width + 2 * HEAD],
            out_g,
            gains[width + 2 * HEAD :],
            gate_g,
            up_g,
            down_g,
        )

    return body


def solution(mesh):
    size, replicas = mesh.shape["shard"], mesh.shape["replica"]
    ny, nx = replicas // 4, 2
    assert size == ny * nx
    plane = Plane(ny, nx)
    fine = Mesh(mesh.devices.reshape(size, ny, nx, 2), ("shard", "y", "x", "c"))
    halves = KV_HEADS % (2 * plane.n) == 0
    every = P(("shard", "y", "x", "c"), None)
    shard, copy = P("shard", None), P()
    return jax.shard_map(
        make_body(size, plane, halves),
        mesh=fine,
        in_specs=(every, every, copy, shard, shard, shard, copy, copy, shard, copy, shard, shard, shard, every),
        out_specs=(every, every, copy, shard, shard, shard, copy, copy, shard, copy, shard, shard, shard),
        check_vma=False,
    )
```

```python
import functools
import math

import jax
import jax.numpy as jnp
from jax import lax
from jax.experimental import pallas as pl
from jax.experimental.pallas import tpu as pltpu
from jax.sharding import Mesh
from jax.sharding import PartitionSpec as P

HEADS = 16
KV_HEADS = 8
HEAD = 128
GROUP = HEADS // KV_HEADS

EPS = 1e-06
ROPE_BASE = 1000000.0
MASKED = -1e30
SCALE = HEAD ** (-0.5)
BF = jnp.bfloat16
F32 = jnp.float32
SWAP = [(0, 1), (1, 0)]
VMEM_LIMIT = 24 * 1024 * 1024
B = 256


def dot(a, b):
    return jnp.dot(a, b, preferred_element_type=F32)


def dot_nt(a, b):
    return lax.dot_general(a, b, (((1,), (1,)), ((), ())), preferred_element_type=F32)


def dot_tn(a, b):
    return lax.dot_general(a, b, (((0,), (0,)), ((), ())), preferred_element_type=F32)


def swap(a, axis):
    return lax.ppermute(a, axis, SWAP)


tie = lax.optimization_barrier


def stay(a):
    return pltpu.with_memory_space_constraint(a, pltpu.HBM)


def sds(shape, dtype):
    return jax.ShapeDtypeStruct(shape, dtype)


def hbm(shape, dtype):
    return pltpu.HBM(shape, dtype)


VM = pl.BlockSpec(memory_space=pltpu.VMEM)
SM = pl.BlockSpec(memory_space=pltpu.SMEM)


def kernel_call(body, outs, args, flops=0, scalars=0, **kw):
    moved = sum(a.size * a.dtype.itemsize for a in args) + sum(math.prod(o.shape) * o.dtype.itemsize for o in outs)
    if "grid" not in kw:
        kw = dict(in_specs=[SM] * scalars + [VM] * (len(args) - scalars), out_specs=[VM] * len(outs))
    return pl.pallas_call(
        body,
        out_shape=outs,
        compiler_params=pltpu.CompilerParams(vmem_limit_bytes=VMEM_LIMIT),
        cost_estimate=pl.CostEstimate(flops=flops, bytes_accessed=moved, transcendentals=0),
        **kw,
    )(*args)


class Plane:
    def __init__(self, ny, nx):
        self.ny, self.nx, self.n = ny, nx, ny * nx
        self.square = ny == 2 and nx == 2
        self.axes = ("y", "x")

    def index(self):
        return lax.axis_index("y") * self.nx + lax.axis_index("x")

    def place(self, t, r):
        return jnp.bitwise_xor(t, r) if self.square else r

    def gather(self, top, low):
        return self.gather_far(self.gather_near(top, low))

    def gather_near(self, top, low):
        if not self.square:
            g, h = (lax.all_gather(a, self.axes, axis=0, tiled=False) for a in (top, low))
            return [[g[i], h[i]] for i in range(self.n)]
        ty, lx = swap(top, "y"), swap(low, "x")
        tx, ly = swap(top, "x"), swap(low, "y")
        return [[top, low], [tx, lx], [ty, ly]]

    def gather_far(self, near, *after):
        if not self.square:
            return near
        (ty, lx), _ = tie(([near[2][0], near[1][1]], after))
        return near + [[swap(ty, "x"), swap(lx, "y")]]

    def near(self, a):
        if not self.square:
            g = lax.all_gather(a, self.axes, axis=0, tiled=False)
            return [g[i] for i in range(self.n)]
        return [a, swap(a, "x"), swap(a, "y")]

    def far(self, a, near):
        if not self.square:
            return near
        return near + [lax.ppermute(a, self.axes, [(i, 3 - i) for i in range(4)])]

    def gather_whole(self, a):
        return self.far(a, self.near(a))

    def scatter(self, blocks):
        if not self.square:
            a = lax.psum_scatter(jnp.concatenate(blocks, 0), self.axes, scatter_dimension=0, tiled=True)
            return [a]
        far = lax.ppermute(blocks[3], self.axes, [(i, 3 - i) for i in range(4)])
        return [blocks[0], swap(blocks[1], "x"), swap(blocks[2], "y"), far]

    def exchange(self, slice_for):
        if not self.square:
            a = jnp.stack([slice_for(i) for i in range(self.n)], 0)
            a = lax.all_to_all(a, self.axes, split_axis=0, concat_axis=0, tiled=True)
            return [a[i] for i in range(self.n)]
        t = self.index()
        return [
            slice_for(t),
            swap(slice_for(jnp.bitwise_xor(t, 1)), "x"),
            swap(slice_for(jnp.bitwise_xor(t, 2)), "y"),
            lax.ppermute(slice_for(jnp.bitwise_xor(t, 3)), self.axes, [(i, 3 - i) for i in range(4)]),
        ]


def columns(ref, lo, count, rows):
    s = ref.shape[0]
    got = [ref[:, (lo + j) * rows : (lo + j + 1) * rows, :].reshape(s * rows, B) for j in range(count)]
    return got[0] if count == 1 else jnp.concatenate(got, 1)


def split(ref):
    return jnp.concatenate([ref[0][...], ref[1][...]], 0)


def rsq(v):
    return lax.rsqrt(jnp.mean(v * v, axis=-1, keepdims=True) + EPS)


def norm_back(v, r, gain, d):
    dg = d * gain
    return r * (dg - v * (r * r) * jnp.mean(dg * v, axis=-1, keepdims=True))


def half_roll(u):
    return pltpu.roll(u, HEAD // 2, 1)


def token_rows(top, low):
    return jnp.concatenate([top[...], low[: top.shape[0], :]], 0).astype(F32)


def prep_block(length, gain, freq, tok0, tok1, nin, cos, sin, mask):
    half = length // 2
    x = token_rows(tok0, tok1)
    nin[...] = (x * rsq(x) * gain[...]).astype(BF)
    row = tok1[half : half + 16, :length].astype(F32)[:1]
    row = jnp.broadcast_to(row, (length, length))
    col = row.T
    start = jnp.sum(jnp.where(row < col, 1.0, 0.0), axis=-1, keepdims=True)
    i = lax.broadcasted_iota(jnp.int32, (length, length), 0)
    j = lax.broadcasted_iota(jnp.int32, (length, length), 1)
    mask[...] = jnp.where((j <= i) & (row == col), 1.0, 0.0)
    pos = lax.broadcasted_iota(jnp.int32, (length, HEAD), 0).astype(F32) - start
    ang = pos * freq[...]
    lane = lax.broadcasted_iota(jnp.int32, (length, HEAD), 1)
    s = jnp.sin(ang)
    cos[...] = jnp.cos(ang)
    sin[...] = jnp.where(lane < HEAD // 2, -s, s)


def ones(rows, value=1.0):
    return jnp.full((rows, HEAD), value, BF)


def twice(a):
    return jnp.concatenate([a, a], 1)


def head_mean(v):
    return dot(v.astype(BF), ones(HEAD, 1.0 / HEAD))


def head_rsq(v):
    return lax.rsqrt(head_mean(v * v) + EPS)


def head_back(v, r, gain, d):
    dg = d * gain
    return r * (dg - v * (r * r) * head_mean(dg * v))


def weights_of(qr, kr, keep):
    return jnp.where(keep, jnp.exp(dot_nt(qr, kr) * SCALE), 0.0)


def attend_block(parts, wrows, qg, kg, wa, wo, nin, cos, sin, mask, lin, vals, mixed, partial):
    keep = mask[...] > 0.0
    c, s = cos[...], sin[...]
    rot = lambda u: u * c + half_roll(u) * s
    n = nin[...]
    one = ones(n.shape[0])
    out = None
    for h in range(parts):
        q = dot(n, columns(wa[h], 0, 1, wrows))
        kv = dot(n, columns(wa[h], 1, 1, wrows))
        k, v = kv[:, :HEAD], kv[:, HEAD:].astype(BF)
        lin[:, h * 3 * HEAD : h * 3 * HEAD + 2 * HEAD] = q
        lin[:, h * 3 * HEAD + 2 * HEAD : (h + 1) * 3 * HEAD] = k
        vals[:, h * HEAD : (h + 1) * HEAD] = v
        kr = rot(k * head_rsq(k) * kg[...]).astype(BF)
        v1 = jnp.concatenate([v, one], 1)
        for g in range(GROUP):
            qh = q[:, g * HEAD : (g + 1) * HEAD]
            e = weights_of(rot(qh * head_rsq(qh) * qg[...]).astype(BF), kr, keep)
            m = dot(e.astype(BF), v1)
            at = h * GROUP * HEAD + g * HEAD
            mixed[:, at : at + HEAD] = (m[:, :HEAD] / m[:, HEAD:]).astype(BF)
        term = dot(mixed[:, h * GROUP * HEAD : (h + 1) * GROUP * HEAD], wo[h][...])
        out = term if out is None else out + term
    partial[...] = out.astype(partial.dtype)


def down_rows_of(ref, base, s0):
    def piece(s, lo, hi):
        return jnp.concatenate([ref[s, base + j * 192 + lo : base + j * 192 + hi, :] for j in range(2)], 1)

    return jnp.concatenate([piece(s0, 0, 128), piece(s0 + 1, 0, 128), piece(s0, 128, 192), piece(s0 + 1, 128, 192)], 0)


def mlp_block(spread, parts, wrows, ff, core, wgu, wd, nm0, nm1, cot0, cot1, product, dgu, partial, d_mid):
    n = split((nm0, nm1))
    blocks = 2 * ff // B
    width = n.shape[1]
    side = width // 2
    out, dm = {}, None
    for h in range(parts):
        w = columns(wgu[h], 0, blocks, wrows)
        if spread:
            s0 = 2 * jnp.bitwise_xor(core[0], h)
            where = [pl.multiple_of(jnp.bitwise_xor(core[0], j) * side, side) for j in range(2)]
            d = [(pl.ds(where[j], side), down_rows_of(wgu[j], blocks * wrows, s0)) for j in range(2)]
        else:
            d = [(slice(None), wd[h][...])]
        gu = dot(n, w)
        gate, up = gu[:, :ff], gu[:, ff:]
        sg = jax.nn.sigmoid(gate)
        act = gate * sg
        pr = (act * up).astype(BF)
        product[:, h * ff : (h + 1) * ff] = pr
        dp = None
        for at, rows in d:
            term = dot_nt(jnp.concatenate([cot0[:, at], cot1[:, at]], 0), rows)
            dp = term if dp is None else dp + term
        d_gate = (dp * up * (sg + act * (1.0 - sg))).astype(BF)
        d_up = (dp * act).astype(BF)
        at = h * 2 * ff
        dgu[:, at : at + ff] = d_gate
        dgu[:, at + ff : at + 2 * ff] = d_up
        for j, (_, rows) in enumerate(d):
            term = dot(pr, rows)
            out[j] = out[j] + term if j in out else term
        term = dot_nt(dgu[:, at : at + 2 * ff], w)
        dm = term if dm is None else dm + term
    for j, (at, _) in enumerate(d):
        partial[:, at] = out[j].astype(partial.dtype)
    d_mid[...] = dm.astype(d_mid.dtype)


def attend_back_block(parts, wrows, qg, kg, wa, wo, dh0, dh1, tok0, tok1, lin, vals, cos, sin, mask, dqkv, d_in, gains):
    keep = mask[...] > 0.0
    c, s = cos[...], sin[...]
    rot = lambda u: u * c + half_roll(u) * s
    rot_back = lambda u: u * c - half_roll(u) * s
    d = split((dh0, dh1))
    one = ones(d.shape[0])
    din, qgain, kgain = None, 0.0, 0.0
    for h in range(parts):
        dm = dot_nt(d, wo[h][...]).astype(BF)
        base = h * 3 * HEAD
        k = lin[:, base + 2 * HEAD : base + 3 * HEAD]
        v = vals[:, h * HEAD : (h + 1) * HEAD]
        rk = head_rsq(k)
        kr = rot(k * rk * kg[...]).astype(BF)
        ps, dss, qrs, dms = [], [], [], []
        at = h * 4 * HEAD
        for g in range(GROUP):
            q = lin[:, base + g * HEAD : base + (g + 1) * HEAD]
            rq = head_rsq(q)
            qr = rot(q * rq * qg[...]).astype(BF)
            e = weights_of(qr, kr, keep)
            p = e * twice(1.0 / dot(e.astype(BF), one))
            dmh = dm[:, g * HEAD : (g + 1) * HEAD]
            pd = p * dot_nt(dmh, v)
            ds = (pd - p * twice(dot(pd.astype(BF), one))).astype(BF)
            ps.append(p.astype(BF))
            dss.append(ds)
            qrs.append(qr)
            dms.append(dmh)
            dq = rot_back(dot(ds, kr) * SCALE)
            qgain = qgain + jnp.sum(dq * q * rq, axis=0, keepdims=True)
            dqkv[:, at + g * HEAD : at + (g + 1) * HEAD] = head_back(q, rq, qg[...], dq).astype(BF)
        dv = dot_tn(jnp.concatenate(ps, 0), jnp.concatenate(dms, 0))
        dk = rot_back(dot_tn(jnp.concatenate(dss, 0), jnp.concatenate(qrs, 0)) * SCALE)
        kgain = kgain + jnp.sum(dk * k * rk, axis=0, keepdims=True)
        dqkv[:, at + 2 * HEAD : at + 3 * HEAD] = head_back(k, rk, kg[...], dk).astype(BF)
        dqkv[:, at + 3 * HEAD : at + 4 * HEAD] = dv.astype(BF)
        term = dot_nt(dqkv[:, at : at + 4 * HEAD], columns(wa[h], 0, 2, wrows))
        din = term if din is None else din + term
    d_in[...] = din.astype(d_in.dtype)
    x = token_rows(tok0, tok1)
    width = x.shape[1]
    gains[:, :width] += jnp.sum(din * (x * rsq(x)), axis=0, keepdims=True)
    gains[:, width : width + HEAD] += qgain
    gains[:, width + HEAD :] += kgain


def added(refs):
    total = refs[0][...].astype(F32)
    for r in refs[1:]:
        total = total + r[...].astype(F32)
    return total


def mid_kernel(tokens, gain, *refs):
    terms, (hidden, nm0, nm1) = refs[:-3], refs[-3:]
    h = tokens[...].astype(F32) + added(terms)
    hidden[...] = h
    nm = (h * rsq(h) * gain[...]).astype(BF)
    nm0[...] = nm[: nm0.shape[0]]
    nm1[...] = nm[nm0.shape[0] :]


def mid_back_kernel(hidden, cot, gain, *refs):
    terms, (d_hidden, low0, low1, ggrad) = refs[:-4], refs[-4:]
    d = added(terms)
    h = hidden[...]
    r = rsq(h)
    out = cot[...].astype(F32) + norm_back(h, r, gain[...], d)
    d_hidden[...] = out
    low0[...] = out[: low0.shape[0]].astype(BF)
    low1[...] = out[low0.shape[0] :].astype(BF)
    ggrad[...] = jnp.sum(d * h * r, axis=0, keepdims=True)


def last_kernel(tokens, d_hidden, gain, *refs):
    terms, (out,) = refs[:-1], refs[-1:]
    x = tokens[...].astype(F32)
    out[...] = (d_hidden[...] + norm_back(x, rsq(x), gain[...], added(terms))).astype(BF)


def out_kernel(hidden, *refs):
    refs[-1][...] = (hidden[...] + added(refs[:-1])).astype(BF)


def arrange(plane, t, blocks, cb):
    q = blocks[0].shape[0] // cb

    def body(where, *refs):
        for r, ref in enumerate(refs[:-1]):
            start = pl.multiple_of(plane.place(where[0], r) * q, 16)
            for j in range(cb):
                refs[-1][pl.ds(start, q), j * B : (j + 1) * B] = ref[j * q : (j + 1) * q, :]

    return kernel_call(body, [sds((len(blocks) * q, cb * B), BF)], [t.astype(jnp.int32)[None], *blocks], scalars=1)[0]


def grad_columns(plane, t, lhs, rhs, half, width, size, other, below=None):
    nblk = width // B
    flat_l, flat_r = sum(lhs, []), sum(rhs, [])
    nl, nr = len(flat_l), len(flat_r)
    rows = flat_l[0].shape[1] // size
    ready = below is not None and not isinstance(below, list)
    more = 0 if below is None else below.shape[1] if ready else below[0].shape[0]

    def body(where, *refs):
        left = jnp.concatenate([r[...] for r in refs[:nl]], 0)
        right = jnp.concatenate([r[...] for r in refs[nl : nl + nr]], 0)
        rest, out = refs[nl + nr : -1], refs[-1]
        got = dot_tn(left, right)
        for j in range(nblk):
            part = got[:, j * B : (j + 1) * B]
            if other is not None:
                part = part + rest[0][0, j * rows : (j + 1) * rows, :].astype(F32)
            out[0, j * rows : (j + 1) * rows, :] = part.astype(BF)
        if ready:
            out[0, nblk * rows :, :] = rest[-1][0]
        elif more:
            z = pl.program_id(0)
            for r in range(plane.n):
                @pl.when(plane.place(where[0], r) == z)
                def _():
                    out[0, nblk * rows :, :] = rest[-plane.n + r][...]

    tall = lambda k: pl.BlockSpec((1, k, B), lambda z, w: (z, 0, 0))
    in_specs = [pl.BlockSpec((a.shape[0], rows), lambda z, w: (0, z)) for a in flat_l]
    in_specs += [pl.BlockSpec((a.shape[0], width), lambda z, w: (0, half)) for a in flat_r]
    args = flat_l + flat_r
    if other is not None:
        in_specs.append(tall(nblk * rows))
        args = args + [other]
    if ready:
        in_specs.append(tall(more))
        args = args + [below]
    elif more:
        in_specs += [pl.BlockSpec((more, B), lambda z, w: (0, 0))] * plane.n
        args = args + below
    tokens = sum(a.shape[0] for a in flat_l)
    out = sds((size, nblk * rows + more, B), BF)
    return pl.pallas_call(
        body,
        out_shape=out,
        grid_spec=pltpu.PrefetchScalarGridSpec(
            num_scalar_prefetch=1, grid=(size,), in_specs=in_specs, out_specs=tall(nblk * rows + more)
        ),
        compiler_params=pltpu.CompilerParams(vmem_limit_bytes=VMEM_LIMIT),
        cost_estimate=pl.CostEstimate(
            flops=2 * tokens * rows * size * width,
            bytes_accessed=sum(a.size * 2 for a in args) + math.prod(out.shape) * 2,
            transcendentals=0,
        ),
    )(t.astype(jnp.int32)[None], *args)


def grad_rows(lhs, rhs, tokens_each, half, width, n, other):
    flat_l, flat_r = lhs, sum(rhs, [])
    nl = len(flat_l)
    cb = flat_r[0].shape[1] // B
    q = width // n

    def body(*refs):
        left = jnp.concatenate([r[...] for r in refs[:nl]], 0)
        right = jnp.concatenate([r[...] for r in refs[nl : nl + len(flat_r)]], 0)
        got = dot_tn(left, right).reshape(n, q, B)
        if other is not None:
            got = got + refs[-2][...].astype(F32)
        refs[-1][...] = got.astype(BF)

    spec = pl.BlockSpec((n, q, B), lambda j: (0, j, 0))
    in_specs = [pl.BlockSpec((a.shape[0], width), lambda j: (0, half)) for a in flat_l]
    in_specs += [pl.BlockSpec((tokens_each, B), lambda j: (0, j)) for a in flat_r]
    args = flat_l + flat_r
    if other is not None:
        in_specs.append(spec)
        args = args + [other]
    tokens = sum(a.shape[0] for a in flat_l)
    return kernel_call(
        body, [sds((n, cb * q, B), BF)], args, flops=2 * tokens * width * cb * B,
        grid=(cb,), in_specs=in_specs, out_specs=[spec],
    )[0]


def grad_down(core, product, cot, other, size, ff):
    flat_r = sum(cot, [])
    nl, nr = len(product), len(flat_r)
    mine = other is not None

    def body(where, *refs):
        left = jnp.concatenate([r[...] for r in refs[:nl]], 0)
        right = jnp.concatenate([r[...] for r in refs[nl : nl + nr]], 0)
        out = refs[-1]
        got = dot_tn(left, right)
        for h in range(2):
            for i in range(2):
                s = 2 * jnp.bitwise_xor(where[0], h) + i
                at = h * ff
                part = jnp.concatenate(
                    [got[at + i * 128 : at + (i + 1) * 128], got[at + 256 + i * 64 : at + 256 + (i + 1) * 64]], 0)
                if mine:
                    part = part + refs[-2][s].astype(F32)
                out[s] = part.astype(BF)

    def column(j, w):
        return (0, jnp.bitwise_xor(w[0], 0 if mine else 1) * 2 + j)

    spec = pl.BlockSpec((size, 192, B), lambda j, w: (0, j, 0))
    in_specs = [pl.BlockSpec(a.shape, lambda j, w: (0, 0)) for a in product]
    in_specs += [pl.BlockSpec((a.shape[0], B), column) for a in flat_r]
    args = product + flat_r + ([other] if mine else [])
    return pl.pallas_call(
        body,
        out_shape=sds((size, 2 * 192, B), BF),
        grid_spec=pltpu.PrefetchScalarGridSpec(
            num_scalar_prefetch=1, grid=(2,), in_specs=in_specs + [spec] * mine, out_specs=spec
        ),
        compiler_params=pltpu.CompilerParams(vmem_limit_bytes=VMEM_LIMIT),
        cost_estimate=pl.CostEstimate(
            flops=2 * sum(a.size for a in product) * 512, bytes_accessed=sum(a.size * 2 for a in args), transcendentals=0
        ),
    )(core, *args)


def over_blocks(block, shared, per_block, outs, flops, total=False):
    flat = []
    shape = []
    for a in shared:
        shape.append(len(a) if isinstance(a, list) else None)
        flat += a if isinstance(a, list) else [a]
    nb, k, o = len(per_block), len(per_block[0]), len(outs[0])
    scalars = sum(1 for a in flat if a.dtype == jnp.int32)
    args = flat + sum(per_block, [])
    out_shapes = sum(outs, []) + ([total] if total else [])

    def body(*refs):
        at, head = 0, []
        for m in shape:
            head.append(refs[at] if m is None else refs[at : at + m])
            at += 1 if m is None else m
        ins, results = refs[at : at + nb * k], refs[at + nb * k :]
        tail = ()
        if total:
            results[-1][...] = jnp.zeros_like(results[-1])
            tail = (results[-1],)
        for b in range(nb):
            block(*head, *ins[b * k : (b + 1) * k], *results[b * o : (b + 1) * o], *tail)

    got = kernel_call(body, out_shapes, args, flops=flops * nb, scalars=scalars)
    return [got[b * o : (b + 1) * o] for b in range(nb)], (got[-1] if total else None)


def make_body(size, plane, halves):
    n = plane.n
    parts = 2 if halves else 1
    one_by_one = [[r] for r in (n - 1, *range(1, n - 1), 0)]
    three = [[n - 1], list(range(1, n - 1)), [0]]

    def body(tokens, segment_ids, attn_gain, w_query, w_key, w_value, query_gain, key_gain,
             w_out, mlp_gain, w_gate, w_up, w_down, cotangent):
        t = plane.index()
        c = lax.axis_index("c") if halves else 0
        rows, width = tokens.shape
        length = segment_ids.shape[1]
        assert rows == length
        half = rows // 2
        cb = width // B
        wrows = w_query.shape[0]
        cut_a, cut_b = 2 * wrows, 2 * w_gate.shape[1] // n // parts // B * wrows
        out_rows, down_rows = w_out.shape[0] // parts // n, w_down.shape[0] // parts // n
        ff = n * down_rows
        spread = plane.square and halves and size == 4 and ff == 384 and width == 1024
        core = jnp.stack([c]).astype(jnp.int32)
        gain_in, gain_mid = attn_gain[None, :], mlp_gain[None, :]
        qg, kg = query_gain[None, :], key_gain[None, :]
        freq = ROPE_BASE ** (-2.0 * (jnp.arange(HEAD) % (HEAD // 2)).astype(F32) / HEAD)[None, :]

        def pick(col_weights, row_weight):
            each = [w.shape[1] // n // parts for w in col_weights]
            total = sum(each)
            high = total // B * wrows
            q = row_weight.shape[0] // parts // n if row_weight is not None else 0
            where = jnp.stack([t * parts + c, c * n + t]).astype(jnp.int32)

            def fill(_, *refs):
                a = [r[...] for r in refs[: len(each)]]
                if a:
                    a = jnp.concatenate(a, 1)
                for j in range(total // B):
                    refs[-1][j * wrows : (j + 1) * wrows, :] = a[:, j * B : (j + 1) * B]
                for j in range(cb if q else 0):
                    refs[-1][high + j * q : high + (j + 1) * q, :] = refs[-2][:, j * B : (j + 1) * B]

            rows_of = [row_weight] if q else []
            return pl.pallas_call(
                fill,
                out_shape=sds((high + cb * q, B), BF),
                grid_spec=pltpu.PrefetchScalarGridSpec(
                    num_scalar_prefetch=1,
                    grid=(1,),
                    in_specs=[pl.BlockSpec((wrows, k), lambda i, at: (0, at[0])) for k in each]
                    + [pl.BlockSpec((q, width), lambda i, at: (at[1], 0)) for _ in rows_of],
                    out_specs=pl.BlockSpec((high + cb * q, B), lambda i, at: (0, 0)),
                ),
                compiler_params=pltpu.CompilerParams(vmem_limit_bytes=VMEM_LIMIT),
            )(where, *[pltpu.with_memory_space_constraint(w, pltpu.HBM) for w in (*col_weights, *rows_of)])

        def pick_spread():
            where = jnp.stack([t, c]).astype(jnp.int32)
            aligned = lambda i, k: lambda _, w: (0, 6 * (2 * w[1] + i) + (3 * w[0]) // 2 + k)

            def fill(w, *refs):
                odd = jnp.full((wrows, HEAD), w[0] % 2) == 1
                low = lax.broadcasted_iota(jnp.int32, (wrows, HEAD), 1) < HEAD // 2
                cols = []
                for m in range(2):
                    full, rest = [], []
                    for i in range(2):
                        w0, w1 = (refs[4 * m + 2 * i + k][...].astype(F32) for k in range(2))
                        r0, r1 = half_roll(w0), half_roll(w1)
                        full.append(jnp.where(odd, jnp.where(low, r0, r1), w0))
                        rest.append(jnp.where(odd, r1, w1) if i == 0 else jnp.where(odd, w1, r1))
                    cols += [*full, jnp.where(low, *rest)]
                out, down = refs[-1], refs[-2]
                for j, a in enumerate(cols):
                    out[j // 2 * wrows : (j // 2 + 1) * wrows, j % 2 * HEAD : (j % 2 + 1) * HEAD] = a.astype(BF)
                for j in range(2):
                    out[cut_b + j * 192 : cut_b + (j + 1) * 192, :] = down[:, j * B : (j + 1) * B]

            return pl.pallas_call(
                fill,
                out_shape=sds((cut_b + 384, B), BF),
                grid_spec=pltpu.PrefetchScalarGridSpec(
                    num_scalar_prefetch=1,
                    grid=(1,),
                    in_specs=[pl.BlockSpec((wrows, HEAD), aligned(i, k)) for _ in range(2) for i in range(2) for k in range(2)]
                    + [pl.BlockSpec((192, width // 2), lambda _, w: (w[0], w[1]))],
                    out_specs=pl.BlockSpec((cut_b + 384, B), lambda _, w: (0, 0)),
                ),
                compiler_params=pltpu.CompilerParams(vmem_limit_bytes=VMEM_LIMIT),
            )(where, *[stay(w_gate)] * 4, *[stay(w_up)] * 4, stay(w_down))

        def both(a):
            return [a, swap(a, "c")] if halves else [a]

        def rows_to_chip(got, cut):
            blocks = plane.exchange(lambda i: lax.dynamic_slice_in_dim(got, i, 1, 0)[0, cut:])
            return arrange(plane, t, blocks, cb)

        got_a = lax.all_gather(pick([w_query, w_key, w_value], w_out), "shard", axis=0, tiled=False)

        seg_rows = jnp.pad(segment_ids.astype(BF), ((0, 15), (0, width - length)))
        tok = plane.gather(tokens[:half], jnp.concatenate([tokens[half:], seg_rows], 0))
        cot_own, w_gate, w_up, w_down, tok[1], tok[n - 2] = tie((cotangent, w_gate, w_up, w_down, tok[1], tok[n - 2]))
        cot = plane.gather(cot_own[:half], cot_own[half:])
        piece_b = pick_spread() if spread else pick([w_gate, w_up], w_down)
        prep, _ = over_blocks(
            functools.partial(prep_block, length), [gain_in, freq], tok,
            [[hbm((length, width), BF), hbm((length, HEAD), F32), hbm((length, HEAD), F32), hbm((length, length), F32)]] * n,
            0,
        )
        got_a, prep, piece_b, cot = tie((got_a, prep, piece_b, cot))
        nin, tables = [a[0] for a in prep], [a[1:] for a in prep]
        got_b = lax.all_gather(piece_b, "shard", axis=0, tiled=False)
        wo = rows_to_chip(got_a, cut_a)
        wa, wo = both(got_a), both(wo)

        def term_type(r):
            return sds((rows, width), F32 if r == 0 and plane.square else BF)

        def run(block, shared, ins, outs, flops, order, total=None):
            got, totals = {}, []
            for group in order:
                mine = [ins[r] for r in group]
                res, tot = over_blocks(block, shared, mine, [outs(r) for r in group], flops, total)
                got.update(zip(group, res))
                totals.append(tot)
            return [{r: got[r][i] for r in got} for i in range(len(outs(0)))], totals

        (lin, vals, mixed, partial), _ = run(
            functools.partial(attend_block, parts, wrows), [qg, kg, wa, wo],
            [[stay(a) for a in (nin[r], *tables[r])] for r in range(n)],
            lambda r: [hbm((length, parts * 3 * HEAD), F32), hbm((length, parts * HEAD), BF),
                       hbm((length, parts * GROUP * HEAD), BF), term_type(r)],
            2 * length * width * parts * 6 * HEAD, three,
        )
        lin, vals, mixed, partial = ([a[r] for r in range(n)] for a in (lin, vals, mixed, partial))
        terms = plane.scatter(partial)
        hidden, nm0, nm1 = kernel_call(
            mid_kernel,
            [hbm((rows, width), F32), sds((half, width), BF), sds((half, width), BF)],
            [tokens, gain_mid, *terms],
        )
        nm = plane.gather(nm0, nm1)
        got_b, nm[1], nm[n - 2] = tie((got_b, nm[1], nm[n - 2]))
        wgu, wd = both(got_b), [] if spread else both(rows_to_chip(got_b, cut_b))

        (product, dgu, partial, d_mid), _ = run(
            functools.partial(mlp_block, spread, parts, wrows, ff), [core, wgu, wd],
            [[*nm[r], *[stay(a) for a in cot[r]]] for r in range(n)],
            lambda r: [sds((rows, parts * ff), BF), sds((rows, parts * 2 * ff), BF),
                       hbm((rows, width), term_type(r).dtype), term_type(r)],
            2 * length * width * parts * 7 * ff, one_by_one,
        )
        product, dgu, partial, d_mid = ([a[r] for r in range(n)] for a in (product, dgu, partial, d_mid))
        terms_mid = plane.scatter(d_mid)
        product, terms_mid[-1] = tie((product, terms_mid[-1]))

        def pair(make, between=lambda a: a):
            if halves:
                return make(0, swap(between(make(1, None)), "c"))
            return lax.psum(make(0, None), "c")

        dgu = [[a] for a in dgu]
        if spread:
            down = grad_down(core, product, cot, swap(grad_down(core, product, cot, None, size, ff), "c"), size, ff)
        else:
            down = pair(lambda h, o: grad_rows(product, cot, half, h, ff, n, o))
        terms_mid, down = tie((terms_mid, down))
        d_hidden, dh0, dh1, mlp_grad = kernel_call(
            mid_back_kernel,
            [hbm((rows, width), F32), sds((half, width), BF), sds((half, width), BF), sds((1, width), F32)],
            [hidden, cotangent, gain_mid, *terms_mid],
        )
        dh = plane.gather_near(dh0, dh1)
        dgu, _ = tie((dgu, dh0))
        gu_other = grad_columns(plane, t, nm, dgu, 1, 2 * ff, size, None) if halves else None
        dh[0], gu_other = tie((dh[0], gu_other))

        def back(order, dh):
            return run(
                functools.partial(attend_back_block, parts, wrows), [qg, kg, wa, wo],
                {r: [*dh[r], *[stay(a) for a in (*tok[r], lin[r], vals[r], *tables[r])]] for g in order for r in g},
                lambda r: [hbm((rows, parts * 4 * HEAD), BF), term_type(r)],
                2 * length * width * parts * 6 * HEAD, order, sds((1, width + 2 * HEAD), F32),
            )

        own_back, gains = back([[0]], dh)
        dh = plane.gather_far(dh, own_back)
        gu_other, own_back, dh[1:-1] = tie((gu_other, own_back, dh[1:-1]))

        def exchanged(low):
            return plane.exchange(lambda i: lax.dynamic_index_in_dim(low, i, 0, keepdims=False))

        def merged(lhs, rhs, width_, other, low):
            if halves:
                return grad_columns(plane, t, lhs, rhs, 0, width_, size, swap(other, "c"), low)
            a = grad_columns(plane, t, lhs, rhs, 0, width_, size, None)
            return jnp.concatenate([lax.psum(a, "c"), jnp.stack(low, 0)], 1)

        grads_b = merged(nm, dgu, 2 * ff, gu_other, down if spread else exchanged(down))
        partial, grads_b = tie((partial, grads_b))
        grads_b = lax.psum_scatter(grads_b.reshape(-1, B), "shard", scatter_dimension=0, tiled=True)
        terms_out = plane.scatter(partial)
        out = pair(lambda h, o: grad_rows(
            [stay(a) for a in mixed], [[stay(a) for a in b] for b in dh], half, h, GROUP * HEAD, n, o))
        far_back, more = back([[n - 1]], dh)
        dh[1:-1], far_back, out = tie((dh[1:-1], far_back, out))
        out = exchanged(out)
        near_back, last = back([[r] for r in range(1, n - 2)], dh)
        dh[n - 2], near_back, terms_out = tie((dh[n - 2], near_back, terms_out))
        near2_back, last2 = back([[n - 2]], dh)
        near_back = [{**a, **b} for a, b in zip(near_back, near2_back)]
        gains = gains + more + last + last2
        dqkv, d_in = ({**a, **b, **c} for a, b, c in zip(own_back, far_back, near_back))
        dqkv, d_in = ([a[r] for r in range(n)] for a in (dqkv, d_in))
        terms_in = plane.scatter(d_in)
        dqkv = [[a] for a in dqkv]
        lhs = [[a] for a in nin]
        dqkv, terms_in[-1] = tie((dqkv, terms_in[-1]))
        qkv_other = grad_columns(plane, t, lhs, dqkv, 1, 4 * HEAD, size, None) if halves else None
        qkv_other, terms_in[:-1] = tie((qkv_other, terms_in[:-1]))
        grads_a = merged(lhs, dqkv, 4 * HEAD, qkv_other, out)
        gains = jnp.concatenate([functools.reduce(jnp.add, gains), mlp_grad], 1)
        grads_a, grads_b, gains = tie((grads_a, grads_b, gains))
        grads_a = lax.psum_scatter(grads_a.reshape(-1, B), "shard", scatter_dimension=0, tiled=True)
        if plane.square and size == 4:
            for axis in ("c", "x", "y"):
                gains = gains + swap(gains, axis)
            gains, grads_b = tie((gains, grads_b))
            for k in (1, 2):
                gains = gains + lax.ppermute(gains, "shard", [(i, i ^ k) for i in range(4)])
        else:
            gains = lax.psum(gains, ("shard", "y", "x", "c"))
        grads_b = plane.gather_whole(grads_b)
        activations = kernel_call(
            out_kernel, [sds((rows, width), BF)], [hidden, *terms_out],
        )[0]
        grads_a, grads_b, gains = tie((grads_a, grads_b, gains))
        gains = gains[0]
        input_grad = kernel_call(
            last_kernel, [sds((rows, width), BF)], [tokens, d_hidden, gain_in, *terms_in],
        )[0]


        def assemble(mine, outs, write):
            got = [(r, 0, a) for r, a in enumerate(mine)]
            if halves:
                got += [(r, 1, swap(a, "c")) for r, a in enumerate(mine)]

            def body(where, *refs):
                for (r, other, _), ref in zip(got, refs):
                    core = jnp.bitwise_xor(where[1], other) if halves else 0
                    write(ref, plane.place(where[0], r), core, refs[len(got) :])

            if write is write_spread:
                body = lambda where, *refs: write(where, refs[: len(got)], refs[len(got) :])
            where = jnp.stack([t, c]).astype(jnp.int32)
            return kernel_call(body, outs, [where] + [a for _, _, a in got], scalars=1)

        def write_cols(ref, j, todo, src, core):
            a = ref[j * wrows : (j + 1) * wrows, :].astype(F32)
            for lo, hi, out, per, at in todo:
                start = pl.multiple_of((src * parts + core) * per + at, HEAD)
                out[:, pl.ds(start, hi - lo)] = a[:, lo:hi]

        def write_rows(ref, base, q, src, core, out):
            start = pl.multiple_of((core * n + src) * q, 16)
            for j in range(cb):
                a = ref[base + j * q : base + (j + 1) * q, :].astype(F32)
                out[pl.ds(start, q), j * B : (j + 1) * B] = a

        def write_b(ref, src, core, outs):
            gate, up, down = outs
            for j in range(2 * ff // B):
                todo = []
                for out, lo in ((gate, 0), (up, ff)):
                    a, b = max(j * B, lo), min((j + 1) * B, lo + ff)
                    if a < b:
                        todo.append((a - j * B, b - j * B, out, ff, a - lo))
                write_cols(ref, j, todo, src, core)
            write_rows(ref, cut_b, down_rows, src, core, down)

        def write_spread(where, refs, outs):
            gate, up, down = outs
            odd = jnp.full((wrows, HEAD), where[0] % 2) == 1
            low = lax.broadcasted_iota(jnp.int32, (wrows, HEAD), 1) < HEAD // 2
            for other in range(2):
                core = jnp.bitwise_xor(where[1], other)
                mine = refs[other * n : (other + 1) * n]
                for r, ref in enumerate(mine):
                    for j in range(2):
                        down[pl.ds(pl.multiple_of(plane.place(where[0], r) * 192, 64), 192),
                             pl.ds(pl.multiple_of((2 * core + j) * B, B), B)] = (
                            ref[cut_b + j * 192 : cut_b + (j + 1) * 192, :].astype(F32))
                for k in range(2):
                    one, two = mine[2 * k], mine[2 * k + 1]
                    pair_at = jnp.bitwise_xor(where[0] // 2, k)
                    for m, out in enumerate((gate, up)):
                        def block(ref, j):
                            j = 3 * m + j
                            return ref[j // 2 * wrows : (j // 2 + 1) * wrows, j % 2 * HEAD : (j % 2 + 1) * HEAD].astype(F32)

                        pairs = [(block(one, j), block(two, j)) for j in range(3)]
                        even = [jnp.where(odd, b, a) for a, b in pairs]
                        odds = [jnp.where(odd, a, b) for a, b in pairs]
                        for i in range(2):
                            at = pl.multiple_of(768 * (2 * core + i) + 384 * pair_at, HEAD)
                            rolled = half_roll(odds[i])
                            rest_even = even[2] if i == 0 else half_roll(even[2])
                            rest_odd = half_roll(odds[2]) if i == 0 else odds[2]
                            out[:, pl.ds(at, HEAD)] = even[i]
                            out[:, pl.ds(at + HEAD, HEAD)] = jnp.where(low, rest_even, rolled)
                            out[:, pl.ds(at + 2 * HEAD, HEAD)] = jnp.where(low, rolled, rest_odd)

        def write_a(ref, src, core, outs):
            q, k, v, out = outs
            write_cols(ref, 0, [(0, B, q, B, 0)], src, core)
            write_cols(ref, 1, [(0, HEAD, k, HEAD, 0), (HEAD, B, v, HEAD, 0)], src, core)
            write_rows(ref, cut_a, out_rows, src, core, out)

        like = lambda w: sds(w.shape, F32)
        gate_g, up_g, down_g = assemble(grads_b, [like(w_gate), like(w_up), like(w_down)], write_spread if spread else write_b)
        grads_a = plane.gather_whole(grads_a)
        grads_a, gate_g, up_g, down_g, activations, input_grad = tie(
            (grads_a, gate_g, up_g, down_g, activations, input_grad))
        query_g, key_g, value_g, out_g = assemble(
            grads_a, [like(w_query), like(w_key), like(w_value), like(w_out)], write_a)

        return (
            activations,
            input_grad,
            gains[:width],
            query_g,
            key_g,
            value_g,
            gains[width : width + HEAD],
            gains[width + HEAD : width + 2 * HEAD],
            out_g,
            gains[width + 2 * HEAD :],
            gate_g,
            up_g,
            down_g,
        )

    return body


def solution(mesh):
    size, replicas = mesh.shape["shard"], mesh.shape["replica"]
    ny, nx = replicas // 4, 2
    assert size == ny * nx
    plane = Plane(ny, nx)
    fine = Mesh(mesh.devices.reshape(size, ny, nx, 2), ("shard", "y", "x", "c"))
    halves = KV_HEADS % (2 * plane.n) == 0
    every = P(("shard", "y", "x", "c"), None)
    shard, copy = P("shard", None), P()
    return jax.shard_map(
        make_body(size, plane, halves),
        mesh=fine,
        in_specs=(every, every, copy, shard, shard, shard, copy, copy, shard, copy, shard, shard, shard, every),
        out_specs=(every, every, copy, shard, shard, shard, copy, copy, shard, copy, shard, shard, shard),
        check_vma=False,
    )
```

```python
import functools
import math

import jax
import jax.numpy as jnp
from jax import lax
from jax.experimental import pallas as pl
from jax.experimental.pallas import tpu as pltpu
from jax.sharding import Mesh
from jax.sharding import PartitionSpec as P

HEADS = 16
KV_HEADS = 8
HEAD = 128
GROUP = HEADS // KV_HEADS

EPS = 1e-06
ROPE_BASE = 1000000.0
MASKED = -1e30
SCALE = HEAD ** (-0.5)
BF = jnp.bfloat16
F32 = jnp.float32
SWAP = [(0, 1), (1, 0)]
VMEM_LIMIT = 24 * 1024 * 1024
B = 256


def dot(a, b):
    return jnp.dot(a, b, preferred_element_type=F32)


def dot_nt(a, b):
    return lax.dot_general(a, b, (((1,), (1,)), ((), ())), preferred_element_type=F32)


def dot_tn(a, b):
    return lax.dot_general(a, b, (((0,), (0,)), ((), ())), preferred_element_type=F32)


def swap(a, axis):
    return lax.ppermute(a, axis, SWAP)


tie = lax.optimization_barrier


def stay(a):
    return pltpu.with_memory_space_constraint(a, pltpu.HBM)


def sds(shape, dtype):
    return jax.ShapeDtypeStruct(shape, dtype)


def hbm(shape, dtype):
    return pltpu.HBM(shape, dtype)


VM = pl.BlockSpec(memory_space=pltpu.VMEM)
SM = pl.BlockSpec(memory_space=pltpu.SMEM)


def cost(flops, moved):
    return pl.CostEstimate(flops=int(flops), bytes_accessed=int(moved), transcendentals=0)


def kernel_call(body, outs, args, flops=0, scalars=0, **kw):
    moved = sum(a.size * a.dtype.itemsize for a in args) + sum(math.prod(o.shape) * o.dtype.itemsize for o in outs)
    if "grid" not in kw:
        kw = dict(in_specs=[SM] * scalars + [VM] * (len(args) - scalars), out_specs=[VM] * len(outs))
    return pl.pallas_call(
        body,
        out_shape=outs,
        compiler_params=pltpu.CompilerParams(vmem_limit_bytes=VMEM_LIMIT),
        cost_estimate=cost(flops, moved),
        **kw,
    )(*args)


class Plane:
    def __init__(self, ny, nx):
        self.ny, self.nx, self.n = ny, nx, ny * nx
        self.square = ny == 2 and nx == 2
        self.axes = ("y", "x")

    def index(self):
        return lax.axis_index("y") * self.nx + lax.axis_index("x")

    def place(self, t, r):
        return jnp.bitwise_xor(t, r) if self.square else r

    def gather(self, top, low):
        return self.gather_far(self.gather_near(top, low))

    def gather_near(self, top, low):
        if not self.square:
            g, h = (lax.all_gather(a, self.axes, axis=0, tiled=False) for a in (top, low))
            return [[g[i], h[i]] for i in range(self.n)]
        ty, lx = swap(top, "y"), swap(low, "x")
        tx, ly = swap(top, "x"), swap(low, "y")
        return [[top, low], [tx, lx], [ty, ly]]

    def gather_far(self, near, *after):
        if not self.square:
            return near
        (ty, lx), _ = tie(([near[2][0], near[1][1]], after))
        return near + [[swap(ty, "x"), swap(lx, "y")]]

    def near(self, a):
        if not self.square:
            g = lax.all_gather(a, self.axes, axis=0, tiled=False)
            return [g[i] for i in range(self.n)]
        return [a, swap(a, "x"), swap(a, "y")]

    def far(self, a, near):
        if not self.square:
            return near
        return near + [lax.ppermute(a, self.axes, [(i, 3 - i) for i in range(4)])]

    def far_halves(self, near):
        if not self.square:
            return near
        k = near[0].shape[0] // 2
        return near + [jnp.concatenate([swap(near[2][:k], "x"), swap(near[1][k:], "y")], 0)]

    def gather_whole(self, a):
        return self.far(a, self.near(a))

    def send_far(self, blocks):
        return lax.ppermute(blocks[3], self.axes, [(i, 3 - i) for i in range(4)]) if self.square else blocks[-1]

    def scatter(self, blocks, far=None):
        if not self.square:
            a = lax.psum_scatter(jnp.concatenate(blocks, 0), self.axes, scatter_dimension=0, tiled=True)
            return [a]
        far = self.send_far(blocks) if far is None else far
        return [blocks[0], swap(blocks[1], "x"), swap(blocks[2], "y"), far]

    def exchange(self, slice_for):
        if not self.square:
            a = jnp.stack([slice_for(i) for i in range(self.n)], 0)
            a = lax.all_to_all(a, self.axes, split_axis=0, concat_axis=0, tiled=True)
            return [a[i] for i in range(self.n)]
        t = self.index()
        return [
            slice_for(t),
            swap(slice_for(jnp.bitwise_xor(t, 1)), "x"),
            swap(slice_for(jnp.bitwise_xor(t, 2)), "y"),
            lax.ppermute(slice_for(jnp.bitwise_xor(t, 3)), self.axes, [(i, 3 - i) for i in range(4)]),
        ]


def columns(ref, lo, count, rows):
    s = ref.shape[0]
    got = [ref[:, (lo + j) * rows : (lo + j + 1) * rows, :].reshape(s * rows, B) for j in range(count)]
    return got[0] if count == 1 else jnp.concatenate(got, 1)


def split(ref):
    return jnp.concatenate([ref[0][...], ref[1][...]], 0)


def rsq(v):
    return lax.rsqrt(jnp.mean(v * v, axis=-1, keepdims=True) + EPS)


def norm_back(v, r, gain, d):
    dg = d * gain
    return r * (dg - v * (r * r) * jnp.mean(dg * v, axis=-1, keepdims=True))


def half_roll(u):
    return pltpu.roll(u, HEAD // 2, 1)


def token_rows(top, low):
    return jnp.concatenate([top[...], low[: top.shape[0], :]], 0).astype(F32)


def prep_block(length, gain, freq, tok0, tok1, nin, cos, sin, mask):
    half = length // 2
    x = token_rows(tok0, tok1)
    nin[...] = (x * rsq(x) * gain[...]).astype(BF)
    row = tok1[half : half + 16, :length].astype(F32)[:1]
    row = jnp.broadcast_to(row, (length, length))
    col = row.T
    start = jnp.sum(jnp.where(row < col, 1.0, 0.0), axis=-1, keepdims=True)
    i = lax.broadcasted_iota(jnp.int32, (length, length), 0)
    j = lax.broadcasted_iota(jnp.int32, (length, length), 1)
    mask[...] = jnp.where((j <= i) & (row == col), 1.0, 0.0)
    pos = lax.broadcasted_iota(jnp.int32, (length, HEAD), 0).astype(F32) - start
    ang = pos * freq[...]
    lane = lax.broadcasted_iota(jnp.int32, (length, HEAD), 1)
    s = jnp.sin(ang)
    cos[...] = jnp.cos(ang)
    sin[...] = jnp.where(lane < HEAD // 2, -s, s)


def ones(rows, value=1.0):
    return jnp.full((rows, HEAD), value, BF)


def twice(a):
    return jnp.concatenate([a, a], 1)


def head_mean(v):
    return dot(v.astype(BF), ones(HEAD, 1.0 / HEAD))


def head_rsq(v):
    return lax.rsqrt(head_mean(v * v) + EPS)


def head_back(v, r, gain, d):
    dg = d * gain
    return r * (dg - v * (r * r) * head_mean(dg * v))


def weights_of(qr, kr, keep):
    return jnp.where(keep, jnp.exp(dot_nt(qr, kr) * SCALE), 0.0)


def attend_block(parts, wrows, qg, kg, wa, wo, nin, cos, sin, mask, lin, vals, mixed, partial):
    keep = mask[...] > 0.0
    c, s = cos[...], sin[...]
    rot = lambda u: u * c + half_roll(u) * s
    n = nin[...]
    one = ones(n.shape[0])
    out = None
    for h in range(parts):
        q = dot(n, columns(wa[h], 0, 1, wrows))
        kv = dot(n, columns(wa[h], 1, 1, wrows))
        k, v = kv[:, :HEAD], kv[:, HEAD:].astype(BF)
        lin[:, h * 3 * HEAD : h * 3 * HEAD + 2 * HEAD] = q
        lin[:, h * 3 * HEAD + 2 * HEAD : (h + 1) * 3 * HEAD] = k
        vals[:, h * HEAD : (h + 1) * HEAD] = v
        kr = rot(k * head_rsq(k) * kg[...]).astype(BF)
        v1 = jnp.concatenate([v, one], 1)
        for g in range(GROUP):
            qh = q[:, g * HEAD : (g + 1) * HEAD]
            e = weights_of(rot(qh * head_rsq(qh) * qg[...]).astype(BF), kr, keep)
            m = dot(e.astype(BF), v1)
            at = h * GROUP * HEAD + g * HEAD
            mixed[:, at : at + HEAD] = (m[:, :HEAD] / m[:, HEAD:]).astype(BF)
        term = dot(mixed[:, h * GROUP * HEAD : (h + 1) * GROUP * HEAD], wo[h][...])
        out = term if out is None else out + term
    partial[...] = out.astype(partial.dtype)


def down_rows_of(ref, base, s0):
    def piece(s, lo, hi):
        return jnp.concatenate([ref[s, base + j * 192 + lo : base + j * 192 + hi, :] for j in range(2)], 1)

    return jnp.concatenate([piece(s0, 0, 128), piece(s0 + 1, 0, 128), piece(s0, 128, 192), piece(s0 + 1, 128, 192)], 0)


def mlp_block(spread, parts, wrows, ff, core, wgu, wd, nm0, nm1, cot0, cot1, product, dgu, partial, d_mid):
    n = split((nm0, nm1))
    blocks = 2 * ff // B
    width = n.shape[1]
    side = width // 2
    out, dm = {}, None
    for h in range(parts):
        w = columns(wgu[h], 0, blocks, wrows)
        if spread:
            s0 = 2 * jnp.bitwise_xor(core[0], h)
            where = [pl.multiple_of(jnp.bitwise_xor(core[0], j) * side, side) for j in range(2)]
            d = [(pl.ds(where[j], side), down_rows_of(wgu[j], blocks * wrows, s0)) for j in range(2)]
        else:
            d = [(slice(None), wd[h][...])]
        gu = dot(n, w)
        gate, up = gu[:, :ff], gu[:, ff:]
        sg = jax.nn.sigmoid(gate)
        act = gate * sg
        pr = (act * up).astype(BF)
        product[:, h * ff : (h + 1) * ff] = pr
        dp = None
        for at, rows in d:
            term = dot_nt(jnp.concatenate([cot0[:, at], cot1[:, at]], 0), rows)
            dp = term if dp is None else dp + term
        d_gate = (dp * up * (sg + act * (1.0 - sg))).astype(BF)
        d_up = (dp * act).astype(BF)
        at = h * 2 * ff
        dgu[:, at : at + ff] = d_gate
        dgu[:, at + ff : at + 2 * ff] = d_up
        for j, (_, rows) in enumerate(d):
            term = dot(pr, rows)
            out[j] = out[j] + term if j in out else term
        term = dot_nt(dgu[:, at : at + 2 * ff], w)
        dm = term if dm is None else dm + term
    for j, (at, _) in enumerate(d):
        partial[:, at] = out[j].astype(partial.dtype)
    d_mid[...] = dm.astype(d_mid.dtype)


def attend_back_block(parts, wrows, qg, kg, wa, wo, dh0, dh1, tok0, tok1, lin, vals, cos, sin, mask, dqkv, d_in, gains):
    keep = mask[...] > 0.0
    c, s = cos[...], sin[...]
    rot = lambda u: u * c + half_roll(u) * s
    rot_back = lambda u: u * c - half_roll(u) * s
    d = split((dh0, dh1))
    one = ones(d.shape[0])
    din, qgain, kgain = None, 0.0, 0.0
    for h in range(parts):
        dm = dot_nt(d, wo[h][...]).astype(BF)
        base = h * 3 * HEAD
        k = lin[:, base + 2 * HEAD : base + 3 * HEAD]
        v = vals[:, h * HEAD : (h + 1) * HEAD]
        rk = head_rsq(k)
        kr = rot(k * rk * kg[...]).astype(BF)
        ps, dss, qrs, dms = [], [], [], []
        at = h * 4 * HEAD
        for g in range(GROUP):
            q = lin[:, base + g * HEAD : base + (g + 1) * HEAD]
            rq = head_rsq(q)
            qr = rot(q * rq * qg[...]).astype(BF)
            e = weights_of(qr, kr, keep)
            p = e * twice(1.0 / dot(e.astype(BF), one))
            dmh = dm[:, g * HEAD : (g + 1) * HEAD]
            pd = p * dot_nt(dmh, v)
            ds = (pd - p * twice(dot(pd.astype(BF), one))).astype(BF)
            ps.append(p.astype(BF))
            dss.append(ds)
            qrs.append(qr)
            dms.append(dmh)
            dq = rot_back(dot(ds, kr) * SCALE)
            qgain = qgain + jnp.sum(dq * q * rq, axis=0, keepdims=True)
            dqkv[:, at + g * HEAD : at + (g + 1) * HEAD] = head_back(q, rq, qg[...], dq).astype(BF)
        dv = dot_tn(jnp.concatenate(ps, 0), jnp.concatenate(dms, 0))
        dk = rot_back(dot_tn(jnp.concatenate(dss, 0), jnp.concatenate(qrs, 0)) * SCALE)
        kgain = kgain + jnp.sum(dk * k * rk, axis=0, keepdims=True)
        dqkv[:, at + 2 * HEAD : at + 3 * HEAD] = head_back(k, rk, kg[...], dk).astype(BF)
        dqkv[:, at + 3 * HEAD : at + 4 * HEAD] = dv.astype(BF)
        term = dot_nt(dqkv[:, at : at + 4 * HEAD], columns(wa[h], 0, 2, wrows))
        din = term if din is None else din + term
    d_in[...] = din.astype(d_in.dtype)
    x = token_rows(tok0, tok1)
    width = x.shape[1]
    gains[:, :width] += jnp.sum(din * (x * rsq(x)), axis=0, keepdims=True)
    gains[:, width : width + HEAD] += qgain
    gains[:, width + HEAD :] += kgain


def added(refs):
    total = refs[0][...].astype(F32)
    for r in refs[1:]:
        total = total + r[...].astype(F32)
    return total


def mid_kernel(tokens, gain, *refs):
    terms, (hidden, nm0, nm1) = refs[:-3], refs[-3:]
    h = tokens[...].astype(F32) + added(terms)
    hidden[...] = h
    nm = (h * rsq(h) * gain[...]).astype(BF)
    nm0[...] = nm[: nm0.shape[0]]
    nm1[...] = nm[nm0.shape[0] :]


def mid_back_kernel(hidden, cot, gain, *refs):
    terms, (d_hidden, low0, low1, ggrad) = refs[:-4], refs[-4:]
    d = added(terms)
    h = hidden[...]
    r = rsq(h)
    out = cot[...].astype(F32) + norm_back(h, r, gain[...], d)
    d_hidden[...] = out
    low0[...] = out[: low0.shape[0]].astype(BF)
    low1[...] = out[low0.shape[0] :].astype(BF)
    ggrad[...] = jnp.sum(d * h * r, axis=0, keepdims=True)


def last_kernel(tokens, d_hidden, gain, *refs):
    terms, (out,) = refs[:-1], refs[-1:]
    x = tokens[...].astype(F32)
    out[...] = (d_hidden[...] + norm_back(x, rsq(x), gain[...], added(terms))).astype(BF)


def gain_lines(mlp_grad, parts):
    total = parts[0][...]
    for p in parts[1:]:
        total = total + p[...]
    width = mlp_grad.shape[1]
    vectors = [total[:, :width], mlp_grad[...], total[:, width:]]
    lines = [v[:, i : i + B] for v in vectors for i in range(0, v.shape[1], B)]
    row = lax.broadcasted_iota(jnp.int32, (16, B), 0)
    block = jnp.zeros((16, B), F32)
    for i, line in enumerate(lines):
        block = jnp.where(row == i, line, block)
    return block


def out_kernel(hidden, *refs):
    refs[-1][...] = (hidden[...] + added(refs[:-1])).astype(BF)


def arrange(plane, t, blocks, cb):
    q = blocks[0].shape[0] // cb

    def body(where, *refs):
        for r, ref in enumerate(refs[:-1]):
            start = pl.multiple_of(plane.place(where[0], r) * q, 16)
            for j in range(cb):
                refs[-1][pl.ds(start, q), j * B : (j + 1) * B] = ref[j * q : (j + 1) * q, :]

    return kernel_call(body, [sds((len(blocks) * q, cb * B), BF)], [t.astype(jnp.int32)[None], *blocks], scalars=1)[0]


def grad_columns(plane, t, lhs, rhs, half, width, size, other, below=None, gains=()):
    nblk = width // B
    flat_l, flat_r = sum(lhs, []), sum(rhs, [])
    nl, nr = len(flat_l), len(flat_r)
    rows = flat_l[0].shape[1] // size
    ready = below is not None and not isinstance(below, list)
    more = 0 if below is None else below.shape[1] if ready else below[0].shape[0]

    def body(where, *refs):
        left = jnp.concatenate([r[...] for r in refs[:nl]], 0)
        right = jnp.concatenate([r[...] for r in refs[nl : nl + nr]], 0)
        gain_refs, rest, out = refs[nl + nr : nl + nr + ng], refs[nl + nr + ng : -1], refs[-1]
        if ng:
            out[0, nblk * rows + more :, :] = gain_lines(gain_refs[0], gain_refs[1:]).astype(BF)
        got = dot_tn(left, right)
        for j in range(nblk):
            part = got[:, j * B : (j + 1) * B]
            if other is not None:
                part = part + rest[0][0, j * rows : (j + 1) * rows, :].astype(F32)
            out[0, j * rows : (j + 1) * rows, :] = part.astype(BF)
        if ready:
            out[0, nblk * rows : nblk * rows + more, :] = rest[-1][0]
        elif more:
            z = pl.program_id(0)
            for r in range(plane.n):
                @pl.when(plane.place(where[0], r) == z)
                def _():
                    out[0, nblk * rows : nblk * rows + more, :] = rest[-plane.n + r][...]

    ng = len(gains)
    tail = 16 if ng else 0
    tall = lambda k: pl.BlockSpec((1, k, B), lambda z, w: (z, 0, 0))
    in_specs = [pl.BlockSpec((a.shape[0], rows), lambda z, w: (0, z)) for a in flat_l]
    in_specs += [pl.BlockSpec((a.shape[0], width), lambda z, w: (0, half)) for a in flat_r]
    in_specs += [pl.BlockSpec(a.shape, lambda z, w: (0, 0)) for a in gains]
    args = flat_l + flat_r + list(gains)
    if other is not None:
        in_specs.append(tall(nblk * rows))
        args = args + [other]
    if ready:
        in_specs.append(tall(more))
        args = args + [below]
    elif more:
        in_specs += [pl.BlockSpec((more, B), lambda z, w: (0, 0))] * plane.n
        args = args + below
    tokens = sum(a.shape[0] for a in flat_l)
    out = sds((size, nblk * rows + more + tail, B), BF)
    return pl.pallas_call(
        body,
        out_shape=out,
        grid_spec=pltpu.PrefetchScalarGridSpec(
            num_scalar_prefetch=1, grid=(size,), in_specs=in_specs, out_specs=tall(nblk * rows + more + tail)
        ),
        compiler_params=pltpu.CompilerParams(vmem_limit_bytes=VMEM_LIMIT),
        cost_estimate=cost(
            2 * tokens * rows * size * width, sum(a.size * 2 for a in args) + math.prod(out.shape) * 2
        ),
    )(t.astype(jnp.int32)[None], *args)


def grad_rows(lhs, rhs, tokens_each, half, width, n, other):
    flat_l, flat_r = lhs, sum(rhs, [])
    nl = len(flat_l)
    cb = flat_r[0].shape[1] // B
    q = width // n

    def body(*refs):
        left = jnp.concatenate([r[...] for r in refs[:nl]], 0)
        right = jnp.concatenate([r[...] for r in refs[nl : nl + len(flat_r)]], 0)
        got = dot_tn(left, right).reshape(n, q, B)
        if other is not None:
            got = got + refs[-2][...].astype(F32)
        refs[-1][...] = got.astype(BF)

    spec = pl.BlockSpec((n, q, B), lambda j: (0, j, 0))
    in_specs = [pl.BlockSpec((a.shape[0], width), lambda j: (0, half)) for a in flat_l]
    in_specs += [pl.BlockSpec((tokens_each, B), lambda j: (0, j)) for a in flat_r]
    args = flat_l + flat_r
    if other is not None:
        in_specs.append(spec)
        args = args + [other]
    tokens = sum(a.shape[0] for a in flat_l)
    return kernel_call(
        body, [sds((n, cb * q, B), BF)], args, flops=2 * tokens * width * cb * B,
        grid=(cb,), in_specs=in_specs, out_specs=[spec],
    )[0]


def grad_mlp(core, nm, dgu, product, cot, other, size, ff):
    mine = other is not None
    groups = [sum(nm, []), dgu, product, sum(cot, [])]
    counts = [len(g) for g in groups]
    width = groups[0][0].shape[1]
    rows, blocks, side = width // size, 2 * ff // B, width // 2
    low = blocks * rows

    def body(where, *refs):
        at, parts = 0, []
        for k in counts:
            parts.append(refs[at : at + k])
            at += k
        rest, out = refs[at:-1], refs[-1]

        def add(part, s, lo):
            hi = lo + part.shape[0]
            if mine:
                part = part + rest[0][s, lo:hi, :].astype(F32)
            out[s, lo:hi, :] = part.astype(BF)

        lefts, rights, prods, cots = parts
        right = jnp.concatenate([r[...] for r in rights], 0)
        for z in range(size):
            got = dot_tn(jnp.concatenate([r[:, z * rows : (z + 1) * rows] for r in lefts], 0), right)
            for j in range(blocks):
                add(got[:, j * B : (j + 1) * B], z, j * rows)
        left = jnp.concatenate([r[...] for r in prods], 0)
        for j in range(2):
            got = dot_tn(left, jnp.concatenate([r[:, j * B : (j + 1) * B] for r in cots], 0))
            for h in range(2):
                for i in range(2):
                    s = 2 * jnp.bitwise_xor(where[0], h) + i
                    p = h * ff
                    part = [got[p + i * 128 : p + (i + 1) * 128], got[p + 256 + i * 64 : p + 256 + (i + 1) * 64]]
                    add(jnp.concatenate(part, 0), s, low + j * 192)

    whole_of = lambda a: pl.BlockSpec(a.shape, lambda i, w: (0,) * a.ndim)
    in_specs = [whole_of(a) for a in groups[0]]
    in_specs += [pl.BlockSpec((a.shape[0], 2 * ff), lambda i, w: (0, 0 if mine else 1)) for a in dgu]
    in_specs += [whole_of(a) for a in product]
    in_specs += [pl.BlockSpec((a.shape[0], side), lambda i, w: (0, jnp.bitwise_xor(w[0], 0 if mine else 1))) for a in groups[3]]
    args = sum(groups, []) + ([other] if mine else [])
    out = sds((size, low + 384, B), BF)
    return pl.pallas_call(
        body,
        out_shape=out,
        grid_spec=pltpu.PrefetchScalarGridSpec(
            num_scalar_prefetch=1, grid=(1,), in_specs=in_specs + [whole_of(out)] * mine, out_specs=whole_of(out)
        ),
        compiler_params=pltpu.CompilerParams(vmem_limit_bytes=VMEM_LIMIT),
        cost_estimate=cost(6 * 1024 * width * 2 * ff, sum(a.size * 2 for a in args)),
    )(core, *args)


def over_blocks(block, shared, per_block, outs, flops, total=False):
    flat = []
    shape = []
    for a in shared:
        shape.append(len(a) if isinstance(a, list) else None)
        flat += a if isinstance(a, list) else [a]
    nb, k, o = len(per_block), len(per_block[0]), len(outs[0])
    scalars = sum(1 for a in flat if a.dtype == jnp.int32)
    args = flat + sum(per_block, [])
    out_shapes = sum(outs, []) + ([total] if total else [])

    def body(*refs):
        at, head = 0, []
        for m in shape:
            head.append(refs[at] if m is None else refs[at : at + m])
            at += 1 if m is None else m
        ins, results = refs[at : at + nb * k], refs[at + nb * k :]
        tail = ()
        if total:
            results[-1][...] = jnp.zeros_like(results[-1])
            tail = (results[-1],)
        for b in range(nb):
            block(*head, *ins[b * k : (b + 1) * k], *results[b * o : (b + 1) * o], *tail)

    got = kernel_call(body, out_shapes, args, flops=flops * nb, scalars=scalars)
    return [got[b * o : (b + 1) * o] for b in range(nb)], (got[-1] if total else None)


def make_body(size, plane, halves):
    n = plane.n
    parts = 2 if halves else 1
    one_by_one = [[r] for r in (n - 1, *range(1, n - 1), 0)]
    three = [[n - 1], list(range(1, n - 1)), [0]]

    def body(tokens, segment_ids, attn_gain, w_query, w_key, w_value, query_gain, key_gain,
             w_out, mlp_gain, w_gate, w_up, w_down, cotangent):
        t = plane.index()
        c = lax.axis_index("c") if halves else 0
        rows, width = tokens.shape
        length = segment_ids.shape[1]
        assert rows == length
        half = rows // 2
        cb = width // B
        wrows = w_query.shape[0]
        cut_a, cut_b = 2 * wrows, 2 * w_gate.shape[1] // n // parts // B * wrows
        out_rows, down_rows = w_out.shape[0] // parts // n, w_down.shape[0] // parts // n
        ff = n * down_rows
        spread = plane.square and halves and size == 4 and ff == 384 and width == 1024
        core = jnp.stack([c]).astype(jnp.int32)
        gain_in, gain_mid = attn_gain[None, :], mlp_gain[None, :]
        qg, kg = query_gain[None, :], key_gain[None, :]
        freq = ROPE_BASE ** (-2.0 * (jnp.arange(HEAD) % (HEAD // 2)).astype(F32) / HEAD)[None, :]

        def pick(col_weights, row_weight):
            each = [w.shape[1] // n // parts for w in col_weights]
            total = sum(each)
            high = total // B * wrows
            q = row_weight.shape[0] // parts // n if row_weight is not None else 0
            where = jnp.stack([t * parts + c, c * n + t]).astype(jnp.int32)

            def fill(_, *refs):
                a = [r[...] for r in refs[: len(each)]]
                if a:
                    a = jnp.concatenate(a, 1)
                for j in range(total // B):
                    refs[-1][j * wrows : (j + 1) * wrows, :] = a[:, j * B : (j + 1) * B]
                for j in range(cb if q else 0):
                    refs[-1][high + j * q : high + (j + 1) * q, :] = refs[-2][:, j * B : (j + 1) * B]

            rows_of = [row_weight] if q else []
            return pl.pallas_call(
                fill,
                out_shape=sds((high + cb * q, B), BF),
                grid_spec=pltpu.PrefetchScalarGridSpec(
                    num_scalar_prefetch=1,
                    grid=(1,),
                    in_specs=[pl.BlockSpec((wrows, k), lambda i, at: (0, at[0])) for k in each]
                    + [pl.BlockSpec((q, width), lambda i, at: (at[1], 0)) for _ in rows_of],
                    out_specs=pl.BlockSpec((high + cb * q, B), lambda i, at: (0, 0)),
                ),
                compiler_params=pltpu.CompilerParams(vmem_limit_bytes=VMEM_LIMIT),
            )(where, *[pltpu.with_memory_space_constraint(w, pltpu.HBM) for w in (*col_weights, *rows_of)])

        def pick_spread():
            where = jnp.stack([t, c]).astype(jnp.int32)
            aligned = lambda i, k: lambda _, w: (0, 6 * (2 * w[1] + i) + (3 * w[0]) // 2 + k)

            def fill(w, *refs):
                odd = jnp.full((wrows, HEAD), w[0] % 2) == 1
                low = lax.broadcasted_iota(jnp.int32, (wrows, HEAD), 1) < HEAD // 2
                cols = []
                for m in range(2):
                    full, rest = [], []
                    for i in range(2):
                        w0, w1 = (refs[4 * m + 2 * i + k][...].astype(F32) for k in range(2))
                        r0, r1 = half_roll(w0), half_roll(w1)
                        full.append(jnp.where(odd, jnp.where(low, r0, r1), w0))
                        rest.append(jnp.where(odd, r1, w1) if i == 0 else jnp.where(odd, w1, r1))
                    cols += [*full, jnp.where(low, *rest)]
                out, down = refs[-1], refs[-2]
                for j, a in enumerate(cols):
                    out[j // 2 * wrows : (j // 2 + 1) * wrows, j % 2 * HEAD : (j % 2 + 1) * HEAD] = a.astype(BF)
                for j in range(2):
                    out[cut_b + j * 192 : cut_b + (j + 1) * 192, :] = down[:, j * B : (j + 1) * B]

            return pl.pallas_call(
                fill,
                out_shape=sds((cut_b + 384, B), BF),
                grid_spec=pltpu.PrefetchScalarGridSpec(
                    num_scalar_prefetch=1,
                    grid=(1,),
                    in_specs=[pl.BlockSpec((wrows, HEAD), aligned(i, k)) for _ in range(2) for i in range(2) for k in range(2)]
                    + [pl.BlockSpec((192, width // 2), lambda _, w: (w[0], w[1]))],
                    out_specs=pl.BlockSpec((cut_b + 384, B), lambda _, w: (0, 0)),
                ),
                compiler_params=pltpu.CompilerParams(vmem_limit_bytes=VMEM_LIMIT),
            )(where, *[stay(w_gate)] * 4, *[stay(w_up)] * 4, stay(w_down))

        def both(a):
            return [a, swap(a, "c")] if halves else [a]

        def rows_to_chip(got, cut):
            blocks = plane.exchange(lambda i: lax.dynamic_slice_in_dim(got, i, 1, 0)[0, cut:])
            return arrange(plane, t, blocks, cb)

        got_a = lax.all_gather(pick([w_query, w_key, w_value], w_out), "shard", axis=0, tiled=False)

        seg_rows = jnp.pad(segment_ids.astype(BF), ((0, 15), (0, width - length)))
        tok = plane.gather(tokens[:half], jnp.concatenate([tokens[half:], seg_rows], 0))
        cot_own, w_gate, w_up, w_down, tok[1], tok[n - 2] = tie((cotangent, w_gate, w_up, w_down, tok[1], tok[n - 2]))
        cot = plane.gather(cot_own[:half], cot_own[half:])
        piece_b = pick_spread() if spread else pick([w_gate, w_up], w_down)
        prep, _ = over_blocks(
            functools.partial(prep_block, length), [gain_in, freq], tok,
            [[hbm((length, width), BF), hbm((length, HEAD), F32), hbm((length, HEAD), F32), hbm((length, length), F32)]] * n,
            0,
        )
        got_a, prep, piece_b, cot = tie((got_a, prep, piece_b, cot))
        nin, tables = [a[0] for a in prep], [a[1:] for a in prep]
        got_b = lax.all_gather(piece_b, "shard", axis=0, tiled=False)
        wo = rows_to_chip(got_a, cut_a)
        wa, wo = both(got_a), both(wo)

        def term_type(r):
            return sds((rows, width), F32 if r == 0 and plane.square else BF)

        def run(block, shared, ins, outs, flops, order, total=None):
            got, totals = {}, []
            for group in order:
                mine = [ins[r] for r in group]
                res, tot = over_blocks(block, shared, mine, [outs(r) for r in group], flops, total)
                got.update(zip(group, res))
                totals.append(tot)
            return [{r: got[r][i] for r in got} for i in range(len(outs(0)))], totals

        (lin, vals, mixed, partial), _ = run(
            functools.partial(attend_block, parts, wrows), [qg, kg, wa, wo],
            [[stay(a) for a in (nin[r], *tables[r])] for r in range(n)],
            lambda r: [hbm((length, parts * 3 * HEAD), F32), hbm((length, parts * HEAD), BF),
                       hbm((length, parts * GROUP * HEAD), BF), term_type(r)],
            2 * length * width * parts * 6 * HEAD, three,
        )
        lin, vals, mixed, partial = ([a[r] for r in range(n)] for a in (lin, vals, mixed, partial))
        terms = plane.scatter(partial)
        hidden, nm0, nm1 = kernel_call(
            mid_kernel,
            [hbm((rows, width), F32), sds((half, width), BF), sds((half, width), BF)],
            [tokens, gain_mid, *terms],
        )
        nm = plane.gather(nm0, nm1)
        got_b, nm[1], nm[n - 2] = tie((got_b, nm[1], nm[n - 2]))
        wgu, wd = both(got_b), [] if spread else both(rows_to_chip(got_b, cut_b))

        def mlp(order):
            return run(
                functools.partial(mlp_block, spread, parts, wrows, ff), [core, wgu, wd],
                {r: [*nm[r], *[stay(a) for a in cot[r]]] for g in order for r in g},
                lambda r: [sds((rows, parts * ff), BF), sds((rows, parts * 2 * ff), BF),
                           hbm((rows, width), term_type(r).dtype), term_type(r)],
                2 * length * width * parts * 7 * ff, order,
            )[0]

        blocks = mlp([[n - 1], list(range(1, n - 1)), [0]])
        product, dgu, partial, d_mid = ([a[r] for r in range(n)] for a in blocks)
        terms_mid = plane.scatter(d_mid)

        def pair(make, between=lambda a: a):
            if halves:
                return make(0, swap(between(make(1, None)), "c"))
            return lax.psum(make(0, None), "c")

        def exchanged(low):
            return plane.exchange(lambda i: lax.dynamic_index_in_dim(low, i, 0, keepdims=False))

        def merged(lhs, rhs, width_, other, low, gains=()):
            if halves:
                return grad_columns(plane, t, lhs, rhs, 0, width_, size, swap(other, "c"), low, gains)
            a = grad_columns(plane, t, lhs, rhs, 0, width_, size, None)
            return jnp.concatenate([lax.psum(a, "c"), jnp.stack(low, 0)], 1)

        d_hidden, dh0, dh1, mlp_grad = kernel_call(
            mid_back_kernel,
            [hbm((rows, width), F32), sds((half, width), BF), sds((half, width), BF), sds((1, width), F32)],
            [hidden, cotangent, gain_mid, *terms_mid],
        )
        dh = plane.gather_near(dh0, dh1)
        if spread:
            make_b = lambda other: grad_mlp(core, nm, dgu, product, cot, other, size, ff)
            dgu, product, _ = tie((dgu, product, dh0))
            grads_b = make_b(swap(make_b(None), "c"))
        else:
            dgu = [[a] for a in dgu]
            gu_other = grad_columns(plane, t, nm, dgu, 1, 2 * ff, size, None) if halves else None
            grads_b = merged(nm, dgu, 2 * ff, gu_other, exchanged(pair(lambda h, o: grad_rows(product, cot, half, h, ff, n, o))))
        dh[1], dh[n - 2], grads_b, dh[0] = tie((dh[1], dh[n - 2], grads_b, dh[0]))
        grads_b = lax.psum_scatter(grads_b.reshape(-1, B), "shard", scatter_dimension=0, tiled=True)

        def back(order, dh):
            return run(
                functools.partial(attend_back_block, parts, wrows), [qg, kg, wa, wo],
                {r: [*([stay(a) for a in dh[r]] if r == 0 else dh[r]), *[stay(a) for a in (*tok[r], lin[r], vals[r], *tables[r])]]
                 for g in order for r in g},
                lambda r: [hbm((rows, parts * 4 * HEAD), BF), hbm((rows, width), term_type(r).dtype)],
                2 * length * width * parts * 6 * HEAD, order, sds((1, width + 2 * HEAD), F32),
            )

        own_back, gains = back([[0]], dh)
        dh = plane.gather_far(dh)
        dh[n - 1], own_back = tie((dh[n - 1], own_back))
        out = pair(lambda h, o: grad_rows(
            [stay(a) for a in mixed], [[stay(a) for a in b] for b in dh], half, h, GROUP * HEAD, n, o))
        dh[1:], partial, out = tie((dh[1:], partial, out))
        out = exchanged(out)
        far_out = plane.send_far(partial)
        near_back, more = back([list(range(1, n - 1))], dh)
        dh[n - 1], out, far_out, near_back, partial = tie((dh[n - 1], out, far_out, near_back, partial))
        terms_out = plane.scatter(partial, far_out)
        far_back, last = back([[n - 1]], dh)
        gains = gains + more + last
        far_back, grads_b, terms_out = tie((far_back, grads_b, terms_out))
        grads_b = plane.near(grads_b)
        dqkv, d_in = ([{**a, **b, **c}[r] for r in range(n)] for a, b, c in zip(own_back, near_back, far_back))
        dqkv = [[stay(a)] for a in dqkv]
        lhs = [[stay(a)] for a in nin]
        qkv_other = grad_columns(plane, t, lhs, dqkv, 1, 4 * HEAD, size, None) if halves else None
        if halves:
            qkv_other, grads_b = tie((qkv_other, grads_b))
        grads_a = merged(lhs, dqkv, 4 * HEAD, qkv_other, out, [mlp_grad, *gains] if halves else [])
        grads_b, _ = tie((grads_b, grads_a))
        grads_b = plane.far_halves(grads_b)
        d_in, grads_b = tie((d_in, grads_b))
        grads_a = lax.psum_scatter(grads_a.reshape(-1, B), "shard", scatter_dimension=0, tiled=True)
        terms_in = plane.scatter(d_in)
        activations = kernel_call(out_kernel, [sds((rows, width), BF)], [hidden, *terms_out])[0]

        def assemble(mine, outs, write):
            got = [(r, 0, a) for r, a in enumerate(mine)]
            if halves:
                got += [(r, 1, swap(a, "c")) for r, a in enumerate(mine)]

            def body(where, *refs):
                if len(outs) == 5:
                    refs[-1][...] = jnp.zeros_like(refs[-1])
                for (r, other, _), ref in zip(got, refs):
                    core = jnp.bitwise_xor(where[1], other) if halves else 0
                    write(ref, plane.place(where[0], r), core, refs[len(got) :])

            if write is write_spread:
                body = lambda where, *refs: write(where, refs[: len(got)], refs[len(got) :])
            where = jnp.stack([t, c]).astype(jnp.int32)
            return kernel_call(body, outs, [where] + [a for _, _, a in got], scalars=1)

        def write_cols(ref, j, todo, src, core):
            a = ref[j * wrows : (j + 1) * wrows, :].astype(F32)
            for lo, hi, out, per, at in todo:
                start = pl.multiple_of((src * parts + core) * per + at, HEAD)
                out[:, pl.ds(start, hi - lo)] = a[:, lo:hi]

        def write_rows(ref, base, q, src, core, out):
            start = pl.multiple_of((core * n + src) * q, 16)
            for j in range(cb):
                a = ref[base + j * q : base + (j + 1) * q, :].astype(F32)
                out[pl.ds(start, q), j * B : (j + 1) * B] = a

        def write_b(ref, src, core, outs):
            gate, up, down = outs
            for j in range(2 * ff // B):
                todo = []
                for out, lo in ((gate, 0), (up, ff)):
                    a, b = max(j * B, lo), min((j + 1) * B, lo + ff)
                    if a < b:
                        todo.append((a - j * B, b - j * B, out, ff, a - lo))
                write_cols(ref, j, todo, src, core)
            write_rows(ref, cut_b, down_rows, src, core, down)

        def write_spread(where, refs, outs):
            gate, up, down = outs
            odd = jnp.full((wrows, HEAD), where[0] % 2) == 1
            low = lax.broadcasted_iota(jnp.int32, (wrows, HEAD), 1) < HEAD // 2
            for other in range(2):
                core = jnp.bitwise_xor(where[1], other)
                mine = refs[other * n : (other + 1) * n]
                for r, ref in enumerate(mine):
                    for j in range(2):
                        down[pl.ds(pl.multiple_of(plane.place(where[0], r) * 192, 64), 192),
                             pl.ds(pl.multiple_of((2 * core + j) * B, B), B)] = (
                            ref[cut_b + j * 192 : cut_b + (j + 1) * 192, :].astype(F32))
                for k in range(2):
                    one, two = mine[2 * k], mine[2 * k + 1]
                    pair_at = jnp.bitwise_xor(where[0] // 2, k)
                    for m, out in enumerate((gate, up)):
                        def block(ref, j):
                            j = 3 * m + j
                            return ref[j // 2 * wrows : (j // 2 + 1) * wrows, j % 2 * HEAD : (j % 2 + 1) * HEAD].astype(F32)

                        pairs = [(block(one, j), block(two, j)) for j in range(3)]
                        even = [jnp.where(odd, b, a) for a, b in pairs]
                        odds = [jnp.where(odd, a, b) for a, b in pairs]
                        for i in range(2):
                            at = pl.multiple_of(768 * (2 * core + i) + 384 * pair_at, HEAD)
                            rolled = half_roll(odds[i])
                            rest_even = even[2] if i == 0 else half_roll(even[2])
                            rest_odd = half_roll(odds[2]) if i == 0 else odds[2]
                            out[:, pl.ds(at, HEAD)] = even[i]
                            out[:, pl.ds(at + HEAD, HEAD)] = jnp.where(low, rest_even, rolled)
                            out[:, pl.ds(at + 2 * HEAD, HEAD)] = jnp.where(low, rolled, rest_odd)

        def write_a(ref, src, core, outs):
            q, k, v, out = outs[:4]
            write_cols(ref, 0, [(0, B, q, B, 0)], src, core)
            write_cols(ref, 1, [(0, HEAD, k, HEAD, 0), (HEAD, B, v, HEAD, 0)], src, core)
            write_rows(ref, cut_a, out_rows, src, core, out)
            if halves:
                outs[4][...] += ref[cut_a + cb * out_rows :, :].astype(F32)

        like = lambda w: sds(w.shape, F32)
        gate_g, up_g, down_g = assemble(grads_b, [like(w_gate), like(w_up), like(w_down)], write_spread if spread else write_b)
        grads_a, gate_g, up_g, down_g, activations, terms_in = tie(
            (grads_a, gate_g, up_g, down_g, activations, terms_in))
        input_grad = kernel_call(
            last_kernel, [sds((rows, width), BF)], [tokens, d_hidden, gain_in, *terms_in])[0]
        grads_a, input_grad = tie((plane.gather_whole(grads_a), input_grad))
        outs_a = [like(w_query), like(w_key), like(w_value), like(w_out)]
        if halves:
            query_g, key_g, value_g, out_g, gains = assemble(grads_a, outs_a + [sds((16, B), F32)], write_a)
            gains = gains[: (2 * width + 2 * HEAD) // B].reshape(-1)
            gains = [gains[:width], gains[width : 2 * width], gains[2 * width :]]
        else:
            query_g, key_g, value_g, out_g = assemble(grads_a, outs_a, write_a)
            gains = functools.reduce(jnp.add, gains)
            gains = [gains[:, :width], mlp_grad, gains[:, width:]]
            gains = [g[0] for g in lax.psum(gains, ("shard", "y", "x", "c"))]

        return (
            activations,
            input_grad,
            gains[0],
            query_g,
            key_g,
            value_g,
            gains[2][:HEAD],
            gains[2][HEAD:],
            out_g,
            gains[1],
            gate_g,
            up_g,
            down_g,
        )

    return body


def solution(mesh):
    size, replicas = mesh.shape["shard"], mesh.shape["replica"]
    ny, nx = replicas // 4, 2
    assert size == ny * nx
    plane = Plane(ny, nx)
    fine = Mesh(mesh.devices.reshape(size, ny, nx, 2), ("shard", "y", "x", "c"))
    halves = KV_HEADS % (2 * plane.n) == 0
    every = P(("shard", "y", "x", "c"), None)
    shard, copy = P("shard", None), P()
    return jax.shard_map(
        make_body(size, plane, halves),
        mesh=fine,
        in_specs=(every, every, copy, shard, shard, shard, copy, copy, shard, copy, shard, shard, shard, every),
        out_specs=(every, every, copy, shard, shard, shard, copy, copy, shard, copy, shard, shard, shard),
        check_vma=False,
    )
```

```python
import functools
import math

import jax
import jax.numpy as jnp
from jax import lax
from jax.experimental import pallas as pl
from jax.experimental.pallas import tpu as pltpu
from jax.sharding import Mesh
from jax.sharding import PartitionSpec as P

HEADS = 16
KV_HEADS = 8
HEAD = 128
GROUP = HEADS // KV_HEADS

EPS = 1e-06
ROPE_BASE = 1000000.0
MASKED = -1e30
SCALE = HEAD ** (-0.5)
BF = jnp.bfloat16
F32 = jnp.float32
SWAP = [(0, 1), (1, 0)]
VMEM_LIMIT = 24 * 1024 * 1024
B = 256


def dot(a, b):
    return jnp.dot(a, b, preferred_element_type=F32)


def dot_nt(a, b):
    return lax.dot_general(a, b, (((1,), (1,)), ((), ())), preferred_element_type=F32)


def dot_tn(a, b):
    return lax.dot_general(a, b, (((0,), (0,)), ((), ())), preferred_element_type=F32)


def swap(a, axis):
    return lax.ppermute(a, axis, SWAP)


tie = lax.optimization_barrier


def stay(a):
    return pltpu.with_memory_space_constraint(a, pltpu.HBM)


def sds(shape, dtype):
    return jax.ShapeDtypeStruct(shape, dtype)


def hbm(shape, dtype):
    return pltpu.HBM(shape, dtype)


VM = pl.BlockSpec(memory_space=pltpu.VMEM)
SM = pl.BlockSpec(memory_space=pltpu.SMEM)


def cost(flops, moved):
    return pl.CostEstimate(flops=int(flops), bytes_accessed=int(moved), transcendentals=0)


def kernel_call(body, outs, args, flops=0, scalars=0, **kw):
    moved = sum(a.size * a.dtype.itemsize for a in args) + sum(math.prod(o.shape) * o.dtype.itemsize for o in outs)
    if "grid" not in kw:
        kw = dict(in_specs=[SM] * scalars + [VM] * (len(args) - scalars), out_specs=[VM] * len(outs))
    return pl.pallas_call(
        body,
        out_shape=outs,
        compiler_params=pltpu.CompilerParams(vmem_limit_bytes=VMEM_LIMIT),
        cost_estimate=cost(flops, moved),
        **kw,
    )(*args)


class Plane:
    def __init__(self, ny, nx):
        self.ny, self.nx, self.n = ny, nx, ny * nx
        self.square = ny == 2 and nx == 2
        self.axes = ("y", "x")

    def index(self):
        return lax.axis_index("y") * self.nx + lax.axis_index("x")

    def place(self, t, r):
        return jnp.bitwise_xor(t, r) if self.square else r

    def gather(self, top, low):
        return self.gather_far(self.gather_near(top, low))

    def gather_near(self, top, low):
        if not self.square:
            g, h = (lax.all_gather(a, self.axes, axis=0, tiled=False) for a in (top, low))
            return [[g[i], h[i]] for i in range(self.n)]
        ty, lx = swap(top, "y"), swap(low, "x")
        tx, ly = swap(top, "x"), swap(low, "y")
        return [[top, low], [tx, lx], [ty, ly]]

    def gather_far(self, near, *after):
        if not self.square:
            return near
        (ty, lx), _ = tie(([near[2][0], near[1][1]], after))
        return near + [[swap(ty, "x"), swap(lx, "y")]]

    def near(self, a):
        if not self.square:
            g = lax.all_gather(a, self.axes, axis=0, tiled=False)
            return [g[i] for i in range(self.n)]
        return [a, swap(a, "x"), swap(a, "y")]

    def far(self, a, near):
        if not self.square:
            return near
        return near + [lax.ppermute(a, self.axes, [(i, 3 - i) for i in range(4)])]

    def far_halves(self, near):
        if not self.square:
            return near
        k = near[0].shape[0] // 2
        return near + [jnp.concatenate([swap(near[2][:k], "x"), swap(near[1][k:], "y")], 0)]

    def gather_whole(self, a):
        return self.far(a, self.near(a))

    def send_far(self, blocks):
        return lax.ppermute(blocks[3], self.axes, [(i, 3 - i) for i in range(4)]) if self.square else blocks[-1]

    def send_near(self, blocks):
        return [swap(blocks[1], "x"), swap(blocks[2], "y")] if self.square else []

    def scatter(self, blocks, far=None):
        if not self.square:
            a = lax.psum_scatter(jnp.concatenate(blocks, 0), self.axes, scatter_dimension=0, tiled=True)
            return [a]
        far = self.send_far(blocks) if far is None else far
        return [blocks[0], swap(blocks[1], "x"), swap(blocks[2], "y"), far]

    def exchange(self, slice_for):
        if not self.square:
            a = jnp.stack([slice_for(i) for i in range(self.n)], 0)
            a = lax.all_to_all(a, self.axes, split_axis=0, concat_axis=0, tiled=True)
            return [a[i] for i in range(self.n)]
        t = self.index()
        return [
            slice_for(t),
            swap(slice_for(jnp.bitwise_xor(t, 1)), "x"),
            swap(slice_for(jnp.bitwise_xor(t, 2)), "y"),
            lax.ppermute(slice_for(jnp.bitwise_xor(t, 3)), self.axes, [(i, 3 - i) for i in range(4)]),
        ]


def columns(ref, lo, count, rows):
    s = ref.shape[0]
    got = [ref[:, (lo + j) * rows : (lo + j + 1) * rows, :].reshape(s * rows, B) for j in range(count)]
    return got[0] if count == 1 else jnp.concatenate(got, 1)


def split(ref):
    return jnp.concatenate([ref[0][...], ref[1][...]], 0)


def rsq(v):
    return lax.rsqrt(jnp.mean(v * v, axis=-1, keepdims=True) + EPS)


def norm_back(v, r, gain, d):
    dg = d * gain
    return r * (dg - v * (r * r) * jnp.mean(dg * v, axis=-1, keepdims=True))


def half_roll(u):
    return pltpu.roll(u, HEAD // 2, 1)


def token_rows(top, low):
    return jnp.concatenate([top[...], low[: top.shape[0], :]], 0).astype(F32)


def prep_block(length, gain, freq, tok0, tok1, nin, cos, sin, mask):
    half = length // 2
    x = token_rows(tok0, tok1)
    nin[...] = (x * rsq(x) * gain[...]).astype(BF)
    row = tok1[half : half + 16, :length].astype(F32)[:1]
    row = jnp.broadcast_to(row, (length, length))
    col = row.T
    start = jnp.sum(jnp.where(row < col, 1.0, 0.0), axis=-1, keepdims=True)
    i = lax.broadcasted_iota(jnp.int32, (length, length), 0)
    j = lax.broadcasted_iota(jnp.int32, (length, length), 1)
    mask[...] = jnp.where((j <= i) & (row == col), 1.0, 0.0)
    pos = lax.broadcasted_iota(jnp.int32, (length, HEAD), 0).astype(F32) - start
    ang = pos * freq[...]
    lane = lax.broadcasted_iota(jnp.int32, (length, HEAD), 1)
    s = jnp.sin(ang)
    cos[...] = jnp.cos(ang)
    sin[...] = jnp.where(lane < HEAD // 2, -s, s)


def ones(rows, value=1.0):
    return jnp.full((rows, HEAD), value, BF)


def twice(a):
    return jnp.concatenate([a, a], 1)


def head_mean(v):
    return dot(v.astype(BF), ones(HEAD, 1.0 / HEAD))


def head_rsq(v):
    return lax.rsqrt(head_mean(v * v) + EPS)


def head_back(v, r, gain, d):
    dg = d * gain
    return r * (dg - v * (r * r) * head_mean(dg * v))


def weights_of(qr, kr, keep):
    return jnp.where(keep, jnp.exp(dot_nt(qr, kr) * SCALE), 0.0)


def attend_block(parts, wrows, qg, kg, wa, wo, nin, cos, sin, mask, lin, vals, mixed, partial):
    keep = mask[...] > 0.0
    c, s = cos[...], sin[...]
    rot = lambda u: u * c + half_roll(u) * s
    n = nin[...]
    one = ones(n.shape[0])
    out = None
    for h in range(parts):
        q = dot(n, columns(wa[h], 0, 1, wrows))
        kv = dot(n, columns(wa[h], 1, 1, wrows))
        k, v = kv[:, :HEAD], kv[:, HEAD:].astype(BF)
        lin[:, h * 3 * HEAD : h * 3 * HEAD + 2 * HEAD] = q
        lin[:, h * 3 * HEAD + 2 * HEAD : (h + 1) * 3 * HEAD] = k
        vals[:, h * HEAD : (h + 1) * HEAD] = v
        kr = rot(k * head_rsq(k) * kg[...]).astype(BF)
        v1 = jnp.concatenate([v, one], 1)
        for g in range(GROUP):
            qh = q[:, g * HEAD : (g + 1) * HEAD]
            e = weights_of(rot(qh * head_rsq(qh) * qg[...]).astype(BF), kr, keep)
            m = dot(e.astype(BF), v1)
            at = h * GROUP * HEAD + g * HEAD
            mixed[:, at : at + HEAD] = (m[:, :HEAD] / m[:, HEAD:]).astype(BF)
        term = dot(mixed[:, h * GROUP * HEAD : (h + 1) * GROUP * HEAD], wo[h][...])
        out = term if out is None else out + term
    partial[...] = out.astype(partial.dtype)


def down_rows_of(ref, base, s0):
    def piece(s, lo, hi):
        return jnp.concatenate([ref[s, base + j * 192 + lo : base + j * 192 + hi, :] for j in range(2)], 1)

    return jnp.concatenate([piece(s0, 0, 128), piece(s0 + 1, 0, 128), piece(s0, 128, 192), piece(s0 + 1, 128, 192)], 0)


def mlp_block(spread, parts, wrows, ff, core, wgu, wd, nm0, nm1, cot0, cot1, product, dgu, partial, d_mid):
    n = split((nm0, nm1))
    blocks = 2 * ff // B
    width = n.shape[1]
    side = width // 2
    out, dm = {}, None
    for h in range(parts):
        w = columns(wgu[h], 0, blocks, wrows)
        if spread:
            s0 = 2 * jnp.bitwise_xor(core[0], h)
            where = [pl.multiple_of(jnp.bitwise_xor(core[0], j) * side, side) for j in range(2)]
            d = [(pl.ds(where[j], side), down_rows_of(wgu[j], blocks * wrows, s0)) for j in range(2)]
        else:
            d = [(slice(None), wd[h][...])]
        gu = dot(n, w)
        gate, up = gu[:, :ff], gu[:, ff:]
        sg = jax.nn.sigmoid(gate)
        act = gate * sg
        pr = (act * up).astype(BF)
        product[:, h * ff : (h + 1) * ff] = pr
        dp = None
        for at, rows in d:
            term = dot_nt(jnp.concatenate([cot0[:, at], cot1[:, at]], 0), rows)
            dp = term if dp is None else dp + term
        d_gate = (dp * up * (sg + act * (1.0 - sg))).astype(BF)
        d_up = (dp * act).astype(BF)
        at = h * 2 * ff
        dgu[:, at : at + ff] = d_gate
        dgu[:, at + ff : at + 2 * ff] = d_up
        for j, (_, rows) in enumerate(d):
            term = dot(pr, rows)
            out[j] = out[j] + term if j in out else term
        term = dot_nt(dgu[:, at : at + 2 * ff], w)
        dm = term if dm is None else dm + term
    for j, (at, _) in enumerate(d):
        partial[:, at] = out[j].astype(partial.dtype)
    d_mid[...] = dm.astype(d_mid.dtype)


def attend_back_block(parts, wrows, qg, kg, wa, wo, dh0, dh1, tok0, tok1, lin, vals, cos, sin, mask, dqkv, d_in, gains):
    keep = mask[...] > 0.0
    c, s = cos[...], sin[...]
    rot = lambda u: u * c + half_roll(u) * s
    rot_back = lambda u: u * c - half_roll(u) * s
    d = split((dh0, dh1))
    one = ones(d.shape[0])
    din, qgain, kgain = None, 0.0, 0.0
    for h in range(parts):
        dm = dot_nt(d, wo[h][...]).astype(BF)
        base = h * 3 * HEAD
        k = lin[:, base + 2 * HEAD : base + 3 * HEAD]
        v = vals[:, h * HEAD : (h + 1) * HEAD]
        rk = head_rsq(k)
        kr = rot(k * rk * kg[...]).astype(BF)
        ps, dss, qrs, dms = [], [], [], []
        at = h * 4 * HEAD
        for g in range(GROUP):
            q = lin[:, base + g * HEAD : base + (g + 1) * HEAD]
            rq = head_rsq(q)
            qr = rot(q * rq * qg[...]).astype(BF)
            e = weights_of(qr, kr, keep)
            p = e * twice(1.0 / dot(e.astype(BF), one))
            dmh = dm[:, g * HEAD : (g + 1) * HEAD]
            pd = p * dot_nt(dmh, v)
            ds = (pd - p * twice(dot(pd.astype(BF), one))).astype(BF)
            ps.append(p.astype(BF))
            dss.append(ds)
            qrs.append(qr)
            dms.append(dmh)
            dq = rot_back(dot(ds, kr) * SCALE)
            qgain = qgain + jnp.sum(dq * q * rq, axis=0, keepdims=True)
            dqkv[:, at + g * HEAD : at + (g + 1) * HEAD] = head_back(q, rq, qg[...], dq).astype(BF)
        dv = dot_tn(jnp.concatenate(ps, 0), jnp.concatenate(dms, 0))
        dk = rot_back(dot_tn(jnp.concatenate(dss, 0), jnp.concatenate(qrs, 0)) * SCALE)
        kgain = kgain + jnp.sum(dk * k * rk, axis=0, keepdims=True)
        dqkv[:, at + 2 * HEAD : at + 3 * HEAD] = head_back(k, rk, kg[...], dk).astype(BF)
        dqkv[:, at + 3 * HEAD : at + 4 * HEAD] = dv.astype(BF)
        term = dot_nt(dqkv[:, at : at + 4 * HEAD], columns(wa[h], 0, 2, wrows))
        din = term if din is None else din + term
    d_in[...] = din.astype(d_in.dtype)
    x = token_rows(tok0, tok1)
    width = x.shape[1]
    gains[:, :width] += jnp.sum(din * (x * rsq(x)), axis=0, keepdims=True)
    gains[:, width : width + HEAD] += qgain
    gains[:, width + HEAD :] += kgain


def added(refs):
    total = refs[0][...].astype(F32)
    for r in refs[1:]:
        total = total + r[...].astype(F32)
    return total


def mid_kernel(tokens, gain, *refs):
    terms, (hidden, nm0, nm1) = refs[:-3], refs[-3:]
    h = tokens[...].astype(F32) + added(terms)
    hidden[...] = h
    nm = (h * rsq(h) * gain[...]).astype(BF)
    nm0[...] = nm[: nm0.shape[0]]
    nm1[...] = nm[nm0.shape[0] :]


def mid_back_kernel(hidden, cot, gain, *refs):
    terms, (d_hidden, low0, low1, ggrad) = refs[:-4], refs[-4:]
    d = added(terms)
    h = hidden[...]
    r = rsq(h)
    out = cot[...].astype(F32) + norm_back(h, r, gain[...], d)
    d_hidden[...] = out
    low0[...] = out[: low0.shape[0]].astype(BF)
    low1[...] = out[low0.shape[0] :].astype(BF)
    ggrad[...] = jnp.sum(d * h * r, axis=0, keepdims=True)


def last_kernel(tokens, d_hidden, gain, *refs):
    terms, (out,) = refs[:-1], refs[-1:]
    x = tokens[...].astype(F32)
    out[...] = (d_hidden[...] + norm_back(x, rsq(x), gain[...], added(terms))).astype(BF)


def gain_lines(mlp_grad, parts):
    total = parts[0][...]
    for p in parts[1:]:
        total = total + p[...]
    width = mlp_grad.shape[1]
    vectors = [total[:, :width], mlp_grad[...], total[:, width:]]
    lines = [v[:, i : i + B] for v in vectors for i in range(0, v.shape[1], B)]
    row = lax.broadcasted_iota(jnp.int32, (16, B), 0)
    block = jnp.zeros((16, B), F32)
    for i, line in enumerate(lines):
        block = jnp.where(row == i, line, block)
    return block


def out_kernel(hidden, *refs):
    refs[-1][...] = (hidden[...] + added(refs[:-1])).astype(BF)


def arrange(plane, t, blocks, cb):
    q = blocks[0].shape[0] // cb

    def body(where, *refs):
        for r, ref in enumerate(refs[:-1]):
            start = pl.multiple_of(plane.place(where[0], r) * q, 16)
            for j in range(cb):
                refs[-1][pl.ds(start, q), j * B : (j + 1) * B] = ref[j * q : (j + 1) * q, :]

    return kernel_call(body, [sds((len(blocks) * q, cb * B), BF)], [t.astype(jnp.int32)[None], *blocks], scalars=1)[0]


def arrange_rows(plane, t, blocks):
    q, width = blocks[0].shape

    def body(where, *refs):
        for r, ref in enumerate(refs[:-1]):
            refs[-1][pl.ds(pl.multiple_of(plane.place(where[0], r) * q, 16), q), :] = ref[...]

    return kernel_call(body, [sds((len(blocks) * q, width), BF)], [t.astype(jnp.int32)[None], *blocks], scalars=1)[0]


def grad_columns(plane, t, lhs, rhs, half, width, size, other, below=None, gains=()):
    nblk = width // B
    flat_l, flat_r = sum(lhs, []), sum(rhs, [])
    nl, nr = len(flat_l), len(flat_r)
    rows = flat_l[0].shape[1] // size
    ready = below is not None and not isinstance(below, list)
    more = 0 if below is None else below.shape[1] if ready else below[0].shape[0]

    def body(where, *refs):
        left = jnp.concatenate([r[...] for r in refs[:nl]], 0)
        right = jnp.concatenate([r[...] for r in refs[nl : nl + nr]], 0)
        gain_refs, rest, out = refs[nl + nr : nl + nr + ng], refs[nl + nr + ng : -1], refs[-1]
        if ng:
            out[0, nblk * rows + more :, :] = gain_lines(gain_refs[0], gain_refs[1:]).astype(BF)
        got = dot_tn(left, right)
        for j in range(nblk):
            part = got[:, j * B : (j + 1) * B]
            if other is not None:
                part = part + rest[0][0, j * rows : (j + 1) * rows, :].astype(F32)
            out[0, j * rows : (j + 1) * rows, :] = part.astype(BF)
        if ready:
            out[0, nblk * rows : nblk * rows + more, :] = rest[-1][0]
        elif more:
            z = pl.program_id(0)
            for r in range(plane.n):
                @pl.when(plane.place(where[0], r) == z)
                def _():
                    out[0, nblk * rows : nblk * rows + more, :] = rest[-plane.n + r][...]

    ng = len(gains)
    tail = 16 if ng else 0
    tall = lambda k: pl.BlockSpec((1, k, B), lambda z, w: (z, 0, 0))
    in_specs = [pl.BlockSpec((a.shape[0], rows), lambda z, w: (0, z)) for a in flat_l]
    in_specs += [pl.BlockSpec((a.shape[0], width), lambda z, w: (0, half)) for a in flat_r]
    in_specs += [pl.BlockSpec(a.shape, lambda z, w: (0, 0)) for a in gains]
    args = flat_l + flat_r + list(gains)
    if other is not None:
        in_specs.append(tall(nblk * rows))
        args = args + [other]
    if ready:
        in_specs.append(tall(more))
        args = args + [below]
    elif more:
        in_specs += [pl.BlockSpec((more, B), lambda z, w: (0, 0))] * plane.n
        args = args + below
    tokens = sum(a.shape[0] for a in flat_l)
    out = sds((size, nblk * rows + more + tail, B), BF)
    return pl.pallas_call(
        body,
        out_shape=out,
        grid_spec=pltpu.PrefetchScalarGridSpec(
            num_scalar_prefetch=1, grid=(size,), in_specs=in_specs, out_specs=tall(nblk * rows + more + tail)
        ),
        compiler_params=pltpu.CompilerParams(vmem_limit_bytes=VMEM_LIMIT),
        cost_estimate=cost(
            2 * tokens * rows * size * width, sum(a.size * 2 for a in args) + math.prod(out.shape) * 2
        ),
    )(t.astype(jnp.int32)[None], *args)


def grad_rows(lhs, rhs, tokens_each, half, width, n, other):
    flat_l, flat_r = lhs, sum(rhs, [])
    nl = len(flat_l)
    cb = flat_r[0].shape[1] // B
    q = width // n

    def body(*refs):
        left = jnp.concatenate([r[...] for r in refs[:nl]], 0)
        right = jnp.concatenate([r[...] for r in refs[nl : nl + len(flat_r)]], 0)
        got = dot_tn(left, right).reshape(n, q, B)
        if other is not None:
            got = got + refs[-2][...].astype(F32)
        refs[-1][...] = got.astype(BF)

    spec = pl.BlockSpec((n, q, B), lambda j: (0, j, 0))
    in_specs = [pl.BlockSpec((a.shape[0], width), lambda j: (0, half)) for a in flat_l]
    in_specs += [pl.BlockSpec((tokens_each, B), lambda j: (0, j)) for a in flat_r]
    args = flat_l + flat_r
    if other is not None:
        in_specs.append(spec)
        args = args + [other]
    tokens = sum(a.shape[0] for a in flat_l)
    return kernel_call(
        body, [sds((n, cb * q, B), BF)], args, flops=2 * tokens * width * cb * B,
        grid=(cb,), in_specs=in_specs, out_specs=[spec],
    )[0]


def grad_mlp(core, nm, dgu, product, cot, other, size, ff):
    mine = other is not None
    groups = [sum(nm, []), dgu, product, sum(cot, [])]
    counts = [len(g) for g in groups]
    width = groups[0][0].shape[1]
    rows, blocks, side = width // size, 2 * ff // B, width // 2
    low = blocks * rows

    def body(where, *refs):
        at, parts = 0, []
        for k in counts:
            parts.append(refs[at : at + k])
            at += k
        rest, out = refs[at:-1], refs[-1]

        def add(part, s, lo):
            hi = lo + part.shape[0]
            if mine:
                part = part + rest[0][s, lo:hi, :].astype(F32)
            out[s, lo:hi, :] = part.astype(BF)

        lefts, rights, prods, cots = parts
        right = jnp.concatenate([r[...] for r in rights], 0)
        for z in range(size):
            got = dot_tn(jnp.concatenate([r[:, z * rows : (z + 1) * rows] for r in lefts], 0), right)
            for j in range(blocks):
                add(got[:, j * B : (j + 1) * B], z, j * rows)
        left = jnp.concatenate([r[...] for r in prods], 0)
        for j in range(2):
            got = dot_tn(left, jnp.concatenate([r[:, j * B : (j + 1) * B] for r in cots], 0))
            for h in range(2):
                for i in range(2):
                    s = 2 * jnp.bitwise_xor(where[0], h) + i
                    p = h * ff
                    part = [got[p + i * 128 : p + (i + 1) * 128], got[p + 256 + i * 64 : p + 256 + (i + 1) * 64]]
                    add(jnp.concatenate(part, 0), s, low + j * 192)

    whole_of = lambda a: pl.BlockSpec(a.shape, lambda i, w: (0,) * a.ndim)
    in_specs = [whole_of(a) for a in groups[0]]
    in_specs += [pl.BlockSpec((a.shape[0], 2 * ff), lambda i, w: (0, 0 if mine else 1)) for a in dgu]
    in_specs += [whole_of(a) for a in product]
    in_specs += [pl.BlockSpec((a.shape[0], side), lambda i, w: (0, jnp.bitwise_xor(w[0], 0 if mine else 1))) for a in groups[3]]
    args = sum(groups, []) + ([other] if mine else [])
    out = sds((size, low + 384, B), BF)
    return pl.pallas_call(
        body,
        out_shape=out,
        grid_spec=pltpu.PrefetchScalarGridSpec(
            num_scalar_prefetch=1, grid=(1,), in_specs=in_specs + [whole_of(out)] * mine, out_specs=whole_of(out)
        ),
        compiler_params=pltpu.CompilerParams(vmem_limit_bytes=VMEM_LIMIT),
        cost_estimate=cost(6 * 1024 * width * 2 * ff, sum(a.size * 2 for a in args)),
    )(core, *args)


def over_blocks(block, shared, per_block, outs, flops, total=False):
    flat = []
    shape = []
    for a in shared:
        shape.append(len(a) if isinstance(a, list) else None)
        flat += a if isinstance(a, list) else [a]
    nb, k, o = len(per_block), len(per_block[0]), len(outs[0])
    scalars = sum(1 for a in flat if a.dtype == jnp.int32)
    args = flat + sum(per_block, [])
    out_shapes = sum(outs, []) + ([total] if total else [])

    def body(*refs):
        at, head = 0, []
        for m in shape:
            head.append(refs[at] if m is None else refs[at : at + m])
            at += 1 if m is None else m
        ins, results = refs[at : at + nb * k], refs[at + nb * k :]
        tail = ()
        if total:
            results[-1][...] = jnp.zeros_like(results[-1])
            tail = (results[-1],)
        for b in range(nb):
            block(*head, *ins[b * k : (b + 1) * k], *results[b * o : (b + 1) * o], *tail)

    got = kernel_call(body, out_shapes, args, flops=flops * nb, scalars=scalars)
    return [got[b * o : (b + 1) * o] for b in range(nb)], (got[-1] if total else None)


def make_body(size, plane, halves):
    n = plane.n
    parts = 2 if halves else 1
    one_by_one = [[r] for r in (n - 1, *range(1, n - 1), 0)]
    three = [[n - 1], list(range(1, n - 1)), [0]]

    def body(tokens, segment_ids, attn_gain, w_query, w_key, w_value, query_gain, key_gain,
             w_out, mlp_gain, w_gate, w_up, w_down, cotangent):
        t = plane.index()
        c = lax.axis_index("c") if halves else 0
        rows, width = tokens.shape
        length = segment_ids.shape[1]
        assert rows == length
        half = rows // 2
        cb = width // B
        wrows = w_query.shape[0]
        cut_a, cut_b = 2 * wrows, 2 * w_gate.shape[1] // n // parts // B * wrows
        out_rows, down_rows = w_out.shape[0] // parts // n, w_down.shape[0] // parts // n
        ff = n * down_rows
        spread = plane.square and halves and size == 4 and ff == 384 and width == 1024
        core = jnp.stack([c]).astype(jnp.int32)
        gain_in, gain_mid = attn_gain[None, :], mlp_gain[None, :]
        qg, kg = query_gain[None, :], key_gain[None, :]
        freq = ROPE_BASE ** (-2.0 * (jnp.arange(HEAD) % (HEAD // 2)).astype(F32) / HEAD)[None, :]

        def pick(col_weights, row_weight):
            each = [w.shape[1] // n // parts for w in col_weights]
            total = sum(each)
            high = total // B * wrows
            q = row_weight.shape[0] // parts // n if row_weight is not None else 0
            where = jnp.stack([t * parts + c, c * n + t]).astype(jnp.int32)

            def fill(_, *refs):
                a = [r[...] for r in refs[: len(each)]]
                if a:
                    a = jnp.concatenate(a, 1)
                for j in range(total // B):
                    refs[-1][j * wrows : (j + 1) * wrows, :] = a[:, j * B : (j + 1) * B]
                for j in range(cb if q else 0):
                    refs[-1][high + j * q : high + (j + 1) * q, :] = refs[-2][:, j * B : (j + 1) * B]

            rows_of = [row_weight] if q else []
            return pl.pallas_call(
                fill,
                out_shape=sds((high + cb * q, B), BF),
                grid_spec=pltpu.PrefetchScalarGridSpec(
                    num_scalar_prefetch=1,
                    grid=(1,),
                    in_specs=[pl.BlockSpec((wrows, k), lambda i, at: (0, at[0])) for k in each]
                    + [pl.BlockSpec((q, width), lambda i, at: (at[1], 0)) for _ in rows_of],
                    out_specs=pl.BlockSpec((high + cb * q, B), lambda i, at: (0, 0)),
                ),
                compiler_params=pltpu.CompilerParams(vmem_limit_bytes=VMEM_LIMIT),
            )(where, *[pltpu.with_memory_space_constraint(w, pltpu.HBM) for w in (*col_weights, *rows_of)])

        def pick_spread():
            where = jnp.stack([t, c]).astype(jnp.int32)
            aligned = lambda i, k: lambda _, w: (0, 6 * (2 * w[1] + i) + (3 * w[0]) // 2 + k)

            def fill(w, *refs):
                odd = jnp.full((wrows, HEAD), w[0] % 2) == 1
                low = lax.broadcasted_iota(jnp.int32, (wrows, HEAD), 1) < HEAD // 2
                cols = []
                for m in range(2):
                    full, rest = [], []
                    for i in range(2):
                        w0, w1 = (refs[4 * m + 2 * i + k][...].astype(F32) for k in range(2))
                        r0, r1 = half_roll(w0), half_roll(w1)
                        full.append(jnp.where(odd, jnp.where(low, r0, r1), w0))
                        rest.append(jnp.where(odd, r1, w1) if i == 0 else jnp.where(odd, w1, r1))
                    cols += [*full, jnp.where(low, *rest)]
                out, down = refs[-1], refs[-2]
                for j, a in enumerate(cols):
                    out[j // 2 * wrows : (j // 2 + 1) * wrows, j % 2 * HEAD : (j % 2 + 1) * HEAD] = a.astype(BF)
                for j in range(2):
                    out[cut_b + j * 192 : cut_b + (j + 1) * 192, :] = down[:, j * B : (j + 1) * B]

            return pl.pallas_call(
                fill,
                out_shape=sds((cut_b + 384, B), BF),
                grid_spec=pltpu.PrefetchScalarGridSpec(
                    num_scalar_prefetch=1,
                    grid=(1,),
                    in_specs=[pl.BlockSpec((wrows, HEAD), aligned(i, k)) for _ in range(2) for i in range(2) for k in range(2)]
                    + [pl.BlockSpec((192, width // 2), lambda _, w: (w[0], w[1]))],
                    out_specs=pl.BlockSpec((cut_b + 384, B), lambda _, w: (0, 0)),
                ),
                compiler_params=pltpu.CompilerParams(vmem_limit_bytes=VMEM_LIMIT),
            )(where, *[stay(w_gate)] * 4, *[stay(w_up)] * 4, stay(w_down))

        def both(a):
            return [a, swap(a, "c")] if halves else [a]

        def rows_to_chip(got, cut):
            blocks = plane.exchange(lambda i: lax.dynamic_slice_in_dim(got, i, 1, 0)[0, cut:])
            return arrange(plane, t, blocks, cb)

        got_a = lax.all_gather(pick([w_query, w_key, w_value], w_out), "shard", axis=0, tiled=False)

        seg_rows = jnp.pad(segment_ids.astype(BF), ((0, 15), (0, width - length)))
        tok = plane.gather(tokens[:half], jnp.concatenate([tokens[half:], seg_rows], 0))
        cot_own, w_gate, w_up, w_down, tok[1], tok[n - 2] = tie((cotangent, w_gate, w_up, w_down, tok[1], tok[n - 2]))
        cot = plane.gather(cot_own[:half], cot_own[half:])
        piece_b = pick_spread() if spread else pick([w_gate, w_up], w_down)
        prep, _ = over_blocks(
            functools.partial(prep_block, length), [gain_in, freq], tok,
            [[hbm((length, width), BF), hbm((length, HEAD), F32), hbm((length, HEAD), F32), hbm((length, length), F32)]] * n,
            0,
        )
        got_a, prep, piece_b, cot = tie((got_a, prep, piece_b, cot))
        nin, tables = [a[0] for a in prep], [a[1:] for a in prep]
        got_b = lax.all_gather(piece_b, "shard", axis=0, tiled=False)
        wo = rows_to_chip(got_a, cut_a)
        wa, wo = both(got_a), both(wo)

        def term_type(r):
            return sds((rows, width), F32 if r == 0 and plane.square else BF)

        def run(block, shared, ins, outs, flops, order, total=None):
            got, totals = {}, []
            for group in [g[i : i + 2] for g in order for i in range(0, len(g), 2)]:
                mine = [ins[r] for r in group]
                res, tot = over_blocks(block, shared, mine, [outs(r) for r in group], flops, total)
                got.update(zip(group, res))
                totals.append(tot)
            return [{r: got[r][i] for r in got} for i in range(len(outs(0)))], totals

        (lin, vals, mixed, partial), _ = run(
            functools.partial(attend_block, parts, wrows), [qg, kg, wa, wo],
            [[stay(a) for a in (nin[r], *tables[r])] for r in range(n)],
            lambda r: [hbm((length, parts * 3 * HEAD), F32), hbm((length, parts * HEAD), BF),
                       hbm((length, parts * GROUP * HEAD), BF), term_type(r)],
            2 * length * width * parts * 6 * HEAD, three,
        )
        lin, vals, mixed, partial = ([a[r] for r in range(n)] for a in (lin, vals, mixed, partial))
        terms = plane.scatter(partial)
        hidden, nm0, nm1 = kernel_call(
            mid_kernel,
            [hbm((rows, width), F32), sds((half, width), BF), sds((half, width), BF)],
            [tokens, gain_mid, *terms],
        )
        nm = plane.gather(nm0, nm1)
        got_b, nm[1][1], nm[n - 2][0] = tie((got_b, nm[1][1], nm[n - 2][0]))
        wgu, wd = both(got_b), [] if spread else both(rows_to_chip(got_b, cut_b))

        def mlp(order):
            return run(
                functools.partial(mlp_block, spread, parts, wrows, ff), [core, wgu, wd],
                {r: [*nm[r], *[stay(a) for a in cot[r]]] for g in order for r in g},
                lambda r: [sds((rows, parts * ff), BF), sds((rows, parts * 2 * ff), BF),
                           hbm((rows, width), term_type(r).dtype), term_type(r)],
                2 * length * width * parts * 7 * ff, order,
            )[0]

        blocks = mlp([[0], [n - 1], list(range(1, n - 1))])
        product, dgu, partial, d_mid = ([a[r] for r in range(n)] for a in blocks)
        terms_mid = plane.scatter(d_mid)

        def pair(make, between=lambda a: a):
            if halves:
                return make(0, swap(between(make(1, None)), "c"))
            return lax.psum(make(0, None), "c")

        def exchanged(low):
            return plane.exchange(lambda i: lax.dynamic_index_in_dim(low, i, 0, keepdims=False))

        def merged(lhs, rhs, width_, other, low, gains=()):
            if halves:
                return grad_columns(plane, t, lhs, rhs, 0, width_, size, swap(other, "c"), low, gains)
            a = grad_columns(plane, t, lhs, rhs, 0, width_, size, None)
            return jnp.concatenate([lax.psum(a, "c"), jnp.stack(low, 0)], 1)

        if spread:
            make_b = lambda other: grad_mlp(core, nm, dgu, product, cot, other, size, ff)
            product, terms_mid[-1] = tie((product, terms_mid[-1]))
            other_b = make_b(None)
            terms_mid, other_b = tie((terms_mid, other_b))
        d_hidden, dh0, dh1, mlp_grad = kernel_call(
            mid_back_kernel,
            [hbm((rows, width), F32), sds((half, width), BF), sds((half, width), BF), sds((1, width), F32)],
            [hidden, cotangent, gain_mid, *terms_mid],
        )
        dh = plane.gather_near(dh0, dh1)
        if spread:
            grads_b = make_b(swap(other_b, "c"))
        else:
            dgu = [[a] for a in dgu]
            gu_other = grad_columns(plane, t, nm, dgu, 1, 2 * ff, size, None) if halves else None
            grads_b = merged(nm, dgu, 2 * ff, gu_other, exchanged(pair(lambda h, o: grad_rows(product, cot, half, h, ff, n, o))))
        dh[1], dh[n - 2], grads_b, dh[0] = tie((dh[1], dh[n - 2], grads_b, dh[0]))
        grads_b = lax.psum_scatter(grads_b.reshape(-1, B), "shard", scatter_dimension=0, tiled=True)

        def back(order, dh):
            return run(
                functools.partial(attend_back_block, parts, wrows), [qg, kg, wa, [stay(a) for a in wo]],
                {r: [*[stay(a) for a in dh[r]], *[stay(a) for a in (*tok[r], lin[r], vals[r], *tables[r])]]
                 for g in order for r in g},
                lambda r: [hbm((rows, parts * 4 * HEAD), BF), hbm((rows, width), term_type(r).dtype)],
                2 * length * width * parts * 6 * HEAD, order, sds((1, width + 2 * HEAD), F32),
            )

        own_back, gains = back([[0]], dh)
        dh = plane.gather_far(dh)
        dh[n - 1], own_back, partial = tie((dh[n - 1], own_back, partial))
        near_out = plane.send_near(partial)
        out = pair(lambda h, o: grad_rows(
            [stay(a) for a in mixed], [[stay(a) for a in b] for b in dh], half, h, GROUP * HEAD, n, o))
        dh[1:], partial, out, near_out = tie((dh[1:], partial, out, near_out))
        out = exchanged(out)
        far_out = plane.send_far(partial)
        near_back, more = back([list(range(1, n - 1))], dh)
        dh[n - 1], out, far_out, near_back, partial = tie((dh[n - 1], out, far_out, near_back, partial))
        terms_out = [partial[0], *near_out, far_out] if plane.square else plane.scatter(partial)
        near_in = plane.send_near(near_back[1])
        separate = plane.square and halves and size == n
        if separate:
            dh[n - 1], out = tie((dh[n - 1], arrange_rows(plane, t, out)))
            out = lax.psum_scatter(out, "shard", scatter_dimension=0, tiled=True)
        far_back, last = back([[n - 1]], dh)
        gains = gains + more + last
        far_back, grads_b, terms_out, near_in = tie((far_back, grads_b, terms_out, near_in))
        grads_b = plane.near(grads_b)
        dqkv, d_in = ([{**a, **b, **c}[r] for r in range(n)] for a, b, c in zip(own_back, near_back, far_back))
        dqkv = [[stay(a)] for a in dqkv]
        lhs = [[stay(a)] for a in nin]
        qkv_other = grad_columns(plane, t, lhs, dqkv, 1, 4 * HEAD, size, None) if halves else None
        if halves:
            qkv_other, grads_b, out = tie((qkv_other, grads_b, out))
        if separate:
            grads_a = merged(lhs, dqkv, 4 * HEAD, qkv_other, None, [mlp_grad, *gains])
            grads_b, grads_a = tie((grads_b, grads_a))
            grads_b = plane.far_halves(grads_b)
            d_in[n - 1], grads_b = tie((d_in[n - 1], grads_b))
            terms_in = [d_in[0], *near_in, plane.send_far(d_in)]
        else:
            grads_a = merged(lhs, dqkv, 4 * HEAD, qkv_other, out)
            grads_b = plane.far_halves(grads_b)
            terms_in = plane.scatter(d_in)
        grads_a = lax.psum_scatter(grads_a.reshape(-1, B), "shard", scatter_dimension=0, tiled=True)
        if separate:
            grads_a = jnp.concatenate([grads_a, out], 0)
        activations = kernel_call(out_kernel, [sds((rows, width), BF)], [hidden, *terms_out])[0]

        def assemble(mine, outs, write):
            got = [(r, 0, a) for r, a in enumerate(mine)]
            if halves:
                got += [(r, 1, swap(a, "c")) for r, a in enumerate(mine)]

            def body(where, *refs):
                total = 0.0
                for (r, other, _), ref in zip(got, refs):
                    core = jnp.bitwise_xor(where[1], other) if halves else 0
                    lines = write(ref, plane.place(where[0], r), core, refs[len(got) :])
                    total = total + lines if separate and write is write_a else total
                if separate and write is write_a:
                    i = 0
                    for out in refs[len(got) + 4 :]:
                        for j in range(0, out.shape[1], B):
                            k = min(B, out.shape[1])
                            at = 0 if out.shape[1] > HEAD else HEAD * (i % 2)
                            line = i if out.shape[1] > HEAD else 2 * width // B
                            out[:, j : j + k] = total[line : line + 1, at : at + k]
                            i += 1

            if write is write_spread:
                body = lambda where, *refs: write(where, refs[: len(got)], refs[len(got) :])
            where = jnp.stack([t, c]).astype(jnp.int32)
            return kernel_call(body, outs, [where] + [a for _, _, a in got], scalars=1)

        def write_cols(ref, j, todo, src, core):
            a = ref[j * wrows : (j + 1) * wrows, :].astype(F32)
            for lo, hi, out, per, at in todo:
                start = pl.multiple_of((src * parts + core) * per + at, HEAD)
                out[:, pl.ds(start, hi - lo)] = a[:, lo:hi]

        def write_rows(ref, base, q, src, core, out):
            start = pl.multiple_of((core * n + src) * q, 16)
            for j in range(cb):
                a = ref[base + j * q : base + (j + 1) * q, :].astype(F32)
                out[pl.ds(start, q), j * B : (j + 1) * B] = a

        def write_b(ref, src, core, outs):
            gate, up, down = outs
            for j in range(2 * ff // B):
                todo = []
                for out, lo in ((gate, 0), (up, ff)):
                    a, b = max(j * B, lo), min((j + 1) * B, lo + ff)
                    if a < b:
                        todo.append((a - j * B, b - j * B, out, ff, a - lo))
                write_cols(ref, j, todo, src, core)
            write_rows(ref, cut_b, down_rows, src, core, down)

        def write_spread(where, refs, outs):
            gate, up, down = outs
            odd = jnp.full((wrows, HEAD), where[0] % 2) == 1
            low = lax.broadcasted_iota(jnp.int32, (wrows, HEAD), 1) < HEAD // 2
            for other in range(2):
                core = jnp.bitwise_xor(where[1], other)
                mine = refs[other * n : (other + 1) * n]
                for r, ref in enumerate(mine):
                    for j in range(2):
                        down[pl.ds(pl.multiple_of(plane.place(where[0], r) * 192, 64), 192),
                             pl.ds(pl.multiple_of((2 * core + j) * B, B), B)] = (
                            ref[cut_b + j * 192 : cut_b + (j + 1) * 192, :].astype(F32))
                for k in range(2):
                    one, two = mine[2 * k], mine[2 * k + 1]
                    pair_at = jnp.bitwise_xor(where[0] // 2, k)
                    for m, out in enumerate((gate, up)):
                        def block(ref, j):
                            j = 3 * m + j
                            return ref[j // 2 * wrows : (j // 2 + 1) * wrows, j % 2 * HEAD : (j % 2 + 1) * HEAD].astype(F32)

                        pairs = [(block(one, j), block(two, j)) for j in range(3)]
                        even = [jnp.where(odd, b, a) for a, b in pairs]
                        odds = [jnp.where(odd, a, b) for a, b in pairs]
                        for i in range(2):
                            at = pl.multiple_of(768 * (2 * core + i) + 384 * pair_at, HEAD)
                            rolled = half_roll(odds[i])
                            rest_even = even[2] if i == 0 else half_roll(even[2])
                            rest_odd = half_roll(odds[2]) if i == 0 else odds[2]
                            out[:, pl.ds(at, HEAD)] = even[i]
                            out[:, pl.ds(at + HEAD, HEAD)] = jnp.where(low, rest_even, rolled)
                            out[:, pl.ds(at + 2 * HEAD, HEAD)] = jnp.where(low, rolled, rest_odd)

        def write_a(ref, src, core, outs):
            q, k, v, out = outs[:4]
            write_cols(ref, 0, [(0, B, q, B, 0)], src, core)
            write_cols(ref, 1, [(0, HEAD, k, HEAD, 0), (HEAD, B, v, HEAD, 0)], src, core)
            write_rows(ref, cut_a + (16 if separate else 0), out_rows, src, core, out)
            return ref[cut_a : cut_a + 16, :].astype(F32)

        like = lambda w: sds(w.shape, F32)
        gate_g, up_g, down_g = assemble(grads_b, [like(w_gate), like(w_up), like(w_down)], write_spread if spread else write_b)
        grads_a, gate_g, up_g, down_g, activations, terms_in = tie(
            (grads_a, gate_g, up_g, down_g, activations, terms_in))
        input_grad = kernel_call(
            last_kernel, [sds((rows, width), BF)], [tokens, d_hidden, gain_in, *terms_in])[0]
        grads_a, input_grad = tie((plane.gather_whole(grads_a), input_grad))
        outs_a = [like(w_query), like(w_key), like(w_value), like(w_out)]
        if separate:
            gain_outs = [sds((1, k), F32) for k in (width, width, HEAD, HEAD)]
            query_g, key_g, value_g, out_g, *gains = assemble(grads_a, outs_a + gain_outs, write_a)
            gains = [g[0] for g in gains]
        else:
            query_g, key_g, value_g, out_g = assemble(grads_a, outs_a, write_a)
            gains = functools.reduce(jnp.add, gains)
            gains = [gains[:, :width], mlp_grad, gains[:, width : width + HEAD], gains[:, width + HEAD :]]
            gains = [g[0] for g in lax.psum(gains, ("shard", "y", "x", "c"))]

        return (
            activations,
            input_grad,
            gains[0],
            query_g,
            key_g,
            value_g,
            gains[2],
            gains[3],
            out_g,
            gains[1],
            gate_g,
            up_g,
            down_g,
        )

    return body


def solution(mesh):
    size, replicas = mesh.shape["shard"], mesh.shape["replica"]
    ny, nx = replicas // 4, 2
    assert size == ny * nx
    plane = Plane(ny, nx)
    fine = Mesh(mesh.devices.reshape(size, ny, nx, 2), ("shard", "y", "x", "c"))
    halves = KV_HEADS % (2 * plane.n) == 0
    every = P(("shard", "y", "x", "c"), None)
    shard, copy = P("shard", None), P()
    return jax.shard_map(
        make_body(size, plane, halves),
        mesh=fine,
        in_specs=(every, every, copy, shard, shard, shard, copy, copy, shard, copy, shard, shard, shard, every),
        out_specs=(every, every, copy, shard, shard, shard, copy, copy, shard, copy, shard, shard, shard),
        check_vma=False,
    )
```

```python
import functools
import math

import jax
import jax.numpy as jnp
from jax import lax
from jax.experimental import pallas as pl
from jax.experimental.pallas import tpu as pltpu
from jax.sharding import Mesh
from jax.sharding import PartitionSpec as P

HEADS = 16
KV_HEADS = 8
HEAD = 128
GROUP = HEADS // KV_HEADS

EPS = 1e-06
ROPE_BASE = 1000000.0
MASKED = -1e30
SCALE = HEAD ** (-0.5)
BF = jnp.bfloat16
F32 = jnp.float32
SWAP = [(0, 1), (1, 0)]
VMEM_LIMIT = 24 * 1024 * 1024
B = 256


def dot(a, b):
    return jnp.dot(a, b, preferred_element_type=F32)


def dot_nt(a, b):
    return lax.dot_general(a, b, (((1,), (1,)), ((), ())), preferred_element_type=F32)


def dot_tn(a, b):
    return lax.dot_general(a, b, (((0,), (0,)), ((), ())), preferred_element_type=F32)


def swap(a, axis):
    return lax.ppermute(a, axis, SWAP)


tie = lax.optimization_barrier


def stay(a):
    return pltpu.with_memory_space_constraint(a, pltpu.HBM)


def sds(shape, dtype):
    return jax.ShapeDtypeStruct(shape, dtype)


def hbm(shape, dtype):
    return pltpu.HBM(shape, dtype)


VM = pl.BlockSpec(memory_space=pltpu.VMEM)
SM = pl.BlockSpec(memory_space=pltpu.SMEM)


def cost(flops, moved):
    return pl.CostEstimate(flops=int(flops), bytes_accessed=int(moved), transcendentals=0)


def kernel_call(body, outs, args, flops=0, scalars=0, **kw):
    moved = sum(a.size * a.dtype.itemsize for a in args) + sum(math.prod(o.shape) * o.dtype.itemsize for o in outs)
    if "grid" not in kw:
        kw = dict(in_specs=[SM] * scalars + [VM] * (len(args) - scalars), out_specs=[VM] * len(outs))
    return pl.pallas_call(
        body,
        out_shape=outs,
        compiler_params=pltpu.CompilerParams(vmem_limit_bytes=VMEM_LIMIT),
        cost_estimate=cost(flops, moved),
        **kw,
    )(*args)


class Plane:
    def __init__(self, ny, nx):
        self.ny, self.nx, self.n = ny, nx, ny * nx
        self.square = ny == 2 and nx == 2
        self.axes = ("y", "x")

    def index(self):
        return lax.axis_index("y") * self.nx + lax.axis_index("x")

    def place(self, t, r):
        return jnp.bitwise_xor(t, r) if self.square else r

    def gather(self, top, low):
        return self.gather_far(self.gather_near(top, low))

    def gather_near(self, top, low):
        if not self.square:
            g, h = (lax.all_gather(a, self.axes, axis=0, tiled=False) for a in (top, low))
            return [[g[i], h[i]] for i in range(self.n)]
        ty, lx = swap(top, "y"), swap(low, "x")
        tx, ly = swap(top, "x"), swap(low, "y")
        return [[top, low], [tx, lx], [ty, ly]]

    def gather_far(self, near, *after):
        if not self.square:
            return near
        (ty, lx), _ = tie(([near[2][0], near[1][1]], after))
        return near + [[swap(ty, "x"), swap(lx, "y")]]

    def near(self, a):
        if not self.square:
            g = lax.all_gather(a, self.axes, axis=0, tiled=False)
            return [g[i] for i in range(self.n)]
        return [a, swap(a, "x"), swap(a, "y")]

    def far(self, a, near):
        if not self.square:
            return near
        return near + [lax.ppermute(a, self.axes, [(i, 3 - i) for i in range(4)])]

    def far_halves(self, near):
        if not self.square:
            return near
        k = near[0].shape[0] // 32 * 16
        return near + [jnp.concatenate([swap(near[2][:k], "x"), swap(near[1][k:], "y")], 0)]

    def gather_whole(self, a):
        return self.far(a, self.near(a))

    def send_far(self, blocks):
        return lax.ppermute(blocks[3], self.axes, [(i, 3 - i) for i in range(4)]) if self.square else blocks[-1]

    def send_near(self, blocks):
        return [swap(blocks[1], "x"), swap(blocks[2], "y")] if self.square else []

    def scatter(self, blocks, far=None):
        if not self.square:
            a = lax.psum_scatter(jnp.concatenate(blocks, 0), self.axes, scatter_dimension=0, tiled=True)
            return [a]
        far = self.send_far(blocks) if far is None else far
        return [blocks[0], swap(blocks[1], "x"), swap(blocks[2], "y"), far]

    def exchange(self, slice_for):
        if not self.square:
            a = jnp.stack([slice_for(i) for i in range(self.n)], 0)
            a = lax.all_to_all(a, self.axes, split_axis=0, concat_axis=0, tiled=True)
            return [a[i] for i in range(self.n)]
        t = self.index()
        return [
            slice_for(t),
            swap(slice_for(jnp.bitwise_xor(t, 1)), "x"),
            swap(slice_for(jnp.bitwise_xor(t, 2)), "y"),
            lax.ppermute(slice_for(jnp.bitwise_xor(t, 3)), self.axes, [(i, 3 - i) for i in range(4)]),
        ]


def columns(ref, lo, count, rows):
    s = ref.shape[0]
    got = [ref[:, (lo + j) * rows : (lo + j + 1) * rows, :].reshape(s * rows, B) for j in range(count)]
    return got[0] if count == 1 else jnp.concatenate(got, 1)


def split(ref):
    return jnp.concatenate([ref[0][...], ref[1][...]], 0)


def rsq(v):
    return lax.rsqrt(jnp.mean(v * v, axis=-1, keepdims=True) + EPS)


def norm_back(v, r, gain, d):
    dg = d * gain
    return r * (dg - v * (r * r) * jnp.mean(dg * v, axis=-1, keepdims=True))


def half_roll(u):
    return pltpu.roll(u, HEAD // 2, 1)


def token_rows(top, low):
    return jnp.concatenate([top[...], low[: top.shape[0], :]], 0).astype(F32)


def prep_block(length, gain, freq, tok0, tok1, nin, cos, sin, mask):
    half = length // 2
    x = token_rows(tok0, tok1)
    nin[...] = (x * rsq(x) * gain[...]).astype(BF)
    row = tok1[half : half + 16, :length].astype(F32)[:1]
    row = jnp.broadcast_to(row, (length, length))
    col = row.T
    start = jnp.sum(jnp.where(row < col, 1.0, 0.0), axis=-1, keepdims=True)
    i = lax.broadcasted_iota(jnp.int32, (length, length), 0)
    j = lax.broadcasted_iota(jnp.int32, (length, length), 1)
    mask[...] = jnp.where((j <= i) & (row == col), 1.0, 0.0)
    pos = lax.broadcasted_iota(jnp.int32, (length, HEAD), 0).astype(F32) - start
    ang = pos * freq[...]
    lane = lax.broadcasted_iota(jnp.int32, (length, HEAD), 1)
    s = jnp.sin(ang)
    cos[...] = jnp.cos(ang)
    sin[...] = jnp.where(lane < HEAD // 2, -s, s)


def ones(rows, value=1.0):
    return jnp.full((rows, HEAD), value, BF)


def twice(a):
    return jnp.concatenate([a, a], 1)


def head_mean(v):
    return dot(v.astype(BF), ones(HEAD, 1.0 / HEAD))


def head_rsq(v):
    return lax.rsqrt(head_mean(v * v) + EPS)


def head_back(v, r, gain, d):
    dg = d * gain
    return r * (dg - v * (r * r) * head_mean(dg * v))


def weights_of(qr, kr, keep):
    return jnp.where(keep, jnp.exp(dot_nt(qr, kr) * SCALE), 0.0)


def heads_below(a):
    return jnp.concatenate([a[:, g * HEAD : (g + 1) * HEAD] for g in range(GROUP)], 0)


def heads_beside(a):
    rows = a.shape[0] // GROUP
    return jnp.concatenate([a[g * rows : (g + 1) * rows] for g in range(GROUP)], 1)


def repeat(a):
    return jnp.concatenate([a] * GROUP, 0)


def attend_block(parts, wrows, qg, kg, wa, wo, nin, cos, sin, mask, lin, vals, mixed, partial):
    keep = repeat(mask[...]) > 0.0
    c, s = cos[...], sin[...]
    c2, s2 = repeat(c), repeat(s)
    n = nin[...]
    one = ones(n.shape[0])
    out = None
    for h in range(parts):
        q = dot(n, columns(wa[h], 0, 1, wrows))
        kv = dot(n, columns(wa[h], 1, 1, wrows))
        k, v = kv[:, :HEAD], kv[:, HEAD:].astype(BF)
        lin[:, h * 3 * HEAD : h * 3 * HEAD + 2 * HEAD] = q
        lin[:, h * 3 * HEAD + 2 * HEAD : (h + 1) * 3 * HEAD] = k
        vals[:, h * HEAD : (h + 1) * HEAD] = v
        kn = k * head_rsq(k) * kg[...]
        kr = (kn * c + half_roll(kn) * s).astype(BF)
        q = heads_below(q)
        qn = q * head_rsq(q) * qg[...]
        e = weights_of((qn * c2 + half_roll(qn) * s2).astype(BF), kr, keep)
        m = dot(e.astype(BF), jnp.concatenate([v, one], 1))
        m = heads_beside((m[:, :HEAD] / m[:, HEAD:]).astype(BF))
        mixed[:, h * GROUP * HEAD : (h + 1) * GROUP * HEAD] = m
        term = dot(m, wo[h][...])
        out = term if out is None else out + term
    partial[...] = out.astype(partial.dtype)


def down_rows_of(ref, base, s0):
    def piece(s, lo, hi):
        return jnp.concatenate([ref[s, base + j * 192 + lo : base + j * 192 + hi, :] for j in range(2)], 1)

    return jnp.concatenate([piece(s0, 0, 128), piece(s0 + 1, 0, 128), piece(s0, 128, 192), piece(s0 + 1, 128, 192)], 0)


def mlp_block(spread, parts, wrows, ff, core, wgu, wd, nm0, nm1, cot0, cot1, product, dgu, partial, d_mid):
    n = split((nm0, nm1))
    blocks = 2 * ff // B
    width = n.shape[1]
    side = width // 2
    out, dm = {}, None
    for h in range(parts):
        w = columns(wgu[h], 0, blocks, wrows)
        if spread:
            s0 = 2 * jnp.bitwise_xor(core[0], h)
            where = [pl.multiple_of(jnp.bitwise_xor(core[0], j) * side, side) for j in range(2)]
            d = [(pl.ds(where[j], side), down_rows_of(wgu[j], blocks * wrows, s0)) for j in range(2)]
        else:
            d = [(slice(None), wd[h][...])]
        gu = dot(n, w)
        gate, up = gu[:, :ff], gu[:, ff:]
        sg = jax.nn.sigmoid(gate)
        act = gate * sg
        pr = (act * up).astype(BF)
        product[:, h * ff : (h + 1) * ff] = pr
        dp = None
        for at, rows in d:
            term = dot_nt(jnp.concatenate([cot0[:, at], cot1[:, at]], 0), rows)
            dp = term if dp is None else dp + term
        d_gate = (dp * up * (sg + act * (1.0 - sg))).astype(BF)
        d_up = (dp * act).astype(BF)
        at = h * 2 * ff
        dgu[:, at : at + ff] = d_gate
        dgu[:, at + ff : at + 2 * ff] = d_up
        for j, (_, rows) in enumerate(d):
            term = dot(pr, rows)
            out[j] = out[j] + term if j in out else term
        term = dot_nt(dgu[:, at : at + 2 * ff], w)
        dm = term if dm is None else dm + term
    for j, (at, _) in enumerate(d):
        partial[:, at] = out[j].astype(partial.dtype)
    d_mid[...] = dm.astype(d_mid.dtype)


def attend_back_block(parts, wrows, qg, kg, wa, wo, dh0, dh1, tok0, tok1, lin, vals, cos, sin, mask, dqkv, d_in, gains):
    keep = repeat(mask[...]) > 0.0
    c, s = cos[...], sin[...]
    c2, s2 = repeat(c), repeat(s)
    d = split((dh0, dh1))
    one = ones(d.shape[0])
    din, qgain, kgain = None, 0.0, 0.0
    for h in range(parts):
        dm = heads_below(dot_nt(d, wo[h][...]).astype(BF))
        base = h * 3 * HEAD
        k = lin[:, base + 2 * HEAD : base + 3 * HEAD]
        v = vals[:, h * HEAD : (h + 1) * HEAD]
        rk = head_rsq(k)
        kn = k * rk * kg[...]
        kr = (kn * c + half_roll(kn) * s).astype(BF)
        q = heads_below(lin[:, base : base + GROUP * HEAD])
        rq = head_rsq(q)
        qn = q * rq * qg[...]
        qr = (qn * c2 + half_roll(qn) * s2).astype(BF)
        e = weights_of(qr, kr, keep)
        p = e * twice(1.0 / dot(e.astype(BF), one))
        pd = p * dot_nt(dm, v)
        ds = (pd - p * twice(dot(pd.astype(BF), one))).astype(BF)
        dq = dot(ds, kr) * SCALE
        dk = dot_tn(ds, qr) * SCALE
        dv = dot_tn(p.astype(BF), dm)
        dq = dq * c2 - half_roll(dq) * s2
        dk = dk * c - half_roll(dk) * s
        qgain = qgain + jnp.sum(dq * q * rq, axis=0, keepdims=True)
        kgain = kgain + jnp.sum(dk * k * rk, axis=0, keepdims=True)
        dq = heads_beside(head_back(q, rq, qg[...], dq).astype(BF))
        dk = head_back(k, rk, kg[...], dk).astype(BF)
        both = jnp.concatenate([dq, dk, dv.astype(BF)], 1)
        dqkv[:, h * 4 * HEAD : (h + 1) * 4 * HEAD] = both
        term = dot_nt(both, columns(wa[h], 0, 2, wrows))
        din = term if din is None else din + term
    d_in[...] = din.astype(d_in.dtype)
    x = token_rows(tok0, tok1)
    width = x.shape[1]
    gains[:, :width] += jnp.sum(din * (x * rsq(x)), axis=0, keepdims=True)
    gains[:, width : width + HEAD] += qgain
    gains[:, width + HEAD :] += kgain


def added(refs):
    total = refs[0][...].astype(F32)
    for r in refs[1:]:
        total = total + r[...].astype(F32)
    return total


def mid_kernel(tokens, gain, *refs):
    terms, (hidden, nm0, nm1) = refs[:-3], refs[-3:]
    h = tokens[...].astype(F32) + added(terms)
    hidden[...] = h
    nm = (h * rsq(h) * gain[...]).astype(BF)
    nm0[...] = nm[: nm0.shape[0]]
    nm1[...] = nm[nm0.shape[0] :]


def mid_back_kernel(hidden, cot, gain, *refs):
    terms, (d_hidden, low0, low1, ggrad) = refs[:-4], refs[-4:]
    d = added(terms)
    h = hidden[...]
    r = rsq(h)
    out = cot[...].astype(F32) + norm_back(h, r, gain[...], d)
    d_hidden[...] = out
    low0[...] = out[: low0.shape[0]].astype(BF)
    low1[...] = out[low0.shape[0] :].astype(BF)
    ggrad[...] = jnp.sum(d * h * r, axis=0, keepdims=True)


def last_kernel(tokens, d_hidden, gain, *refs):
    terms, (out,) = refs[:-1], refs[-1:]
    x = tokens[...].astype(F32)
    out[...] = (d_hidden[...] + norm_back(x, rsq(x), gain[...], added(terms))).astype(BF)


def gain_lines(mlp_grad, parts):
    total = parts[0][...]
    for p in parts[1:]:
        total = total + p[...]
    width = mlp_grad.shape[1]
    vectors = [total[:, :width], mlp_grad[...], total[:, width:]]
    lines = [v[:, i : i + B] for v in vectors for i in range(0, v.shape[1], B)]
    row = lax.broadcasted_iota(jnp.int32, (16, B), 0)
    block = jnp.zeros((16, B), F32)
    for i, line in enumerate(lines):
        block = jnp.where(row == i, line, block)
    return block


def out_kernel(hidden, *refs):
    refs[-1][...] = (hidden[...] + added(refs[:-1])).astype(BF)


def arrange(plane, t, blocks, cb):
    q = blocks[0].shape[0] // cb

    def body(where, *refs):
        for r, ref in enumerate(refs[:-1]):
            start = pl.multiple_of(plane.place(where[0], r) * q, 16)
            for j in range(cb):
                refs[-1][pl.ds(start, q), j * B : (j + 1) * B] = ref[j * q : (j + 1) * q, :]

    return kernel_call(body, [sds((len(blocks) * q, cb * B), BF)], [t.astype(jnp.int32)[None], *blocks], scalars=1)[0]


def arrange_rows(plane, t, blocks):
    q, width = blocks[0].shape

    def body(where, *refs):
        for r, ref in enumerate(refs[:-1]):
            refs[-1][pl.ds(pl.multiple_of(plane.place(where[0], r) * q, 16), q), :] = ref[...]

    return kernel_call(body, [sds((len(blocks) * q, width), BF)], [t.astype(jnp.int32)[None], *blocks], scalars=1)[0]


def grad_columns(plane, t, lhs, rhs, half, width, size, other, below=None, gains=()):
    nblk = width // B
    flat_l, flat_r = sum(lhs, []), sum(rhs, [])
    nl, nr = len(flat_l), len(flat_r)
    rows = flat_l[0].shape[1] // size
    ready = below is not None and not isinstance(below, list)
    more = 0 if below is None else below.shape[1] if ready else below[0].shape[0]

    def body(where, *refs):
        left = jnp.concatenate([r[...] for r in refs[:nl]], 0)
        right = jnp.concatenate([r[...] for r in refs[nl : nl + nr]], 0)
        gain_refs, rest, out = refs[nl + nr : nl + nr + ng], refs[nl + nr + ng : -1], refs[-1]
        if ng:
            out[0, nblk * rows + more :, :] = gain_lines(gain_refs[0], gain_refs[1:]).astype(BF)
        got = dot_tn(left, right)
        for j in range(nblk):
            part = got[:, j * B : (j + 1) * B]
            if other is not None:
                part = part + rest[0][0, j * rows : (j + 1) * rows, :].astype(F32)
            out[0, j * rows : (j + 1) * rows, :] = part.astype(BF)
        if ready:
            out[0, nblk * rows : nblk * rows + more, :] = rest[-1][0]
        elif more:
            z = pl.program_id(0)
            for r in range(plane.n):
                @pl.when(plane.place(where[0], r) == z)
                def _():
                    out[0, nblk * rows : nblk * rows + more, :] = rest[-plane.n + r][...]

    ng = len(gains)
    tail = 16 if ng else 0
    tall = lambda k: pl.BlockSpec((1, k, B), lambda z, w: (z, 0, 0))
    in_specs = [pl.BlockSpec((a.shape[0], rows), lambda z, w: (0, z)) for a in flat_l]
    in_specs += [pl.BlockSpec((a.shape[0], width), lambda z, w: (0, half)) for a in flat_r]
    in_specs += [pl.BlockSpec(a.shape, lambda z, w: (0, 0)) for a in gains]
    args = flat_l + flat_r + list(gains)
    if other is not None:
        in_specs.append(tall(nblk * rows))
        args = args + [other]
    if ready:
        in_specs.append(tall(more))
        args = args + [below]
    elif more:
        in_specs += [pl.BlockSpec((more, B), lambda z, w: (0, 0))] * plane.n
        args = args + below
    tokens = sum(a.shape[0] for a in flat_l)
    out = sds((size, nblk * rows + more + tail, B), BF)
    return pl.pallas_call(
        body,
        out_shape=out,
        grid_spec=pltpu.PrefetchScalarGridSpec(
            num_scalar_prefetch=1, grid=(size,), in_specs=in_specs, out_specs=tall(nblk * rows + more + tail)
        ),
        compiler_params=pltpu.CompilerParams(vmem_limit_bytes=VMEM_LIMIT),
        cost_estimate=cost(
            2 * tokens * rows * size * width, sum(a.size * 2 for a in args) + math.prod(out.shape) * 2
        ),
    )(t.astype(jnp.int32)[None], *args)


def grad_rows(lhs, rhs, tokens_each, half, width, n, other):
    flat_l, flat_r = lhs, sum(rhs, [])
    nl = len(flat_l)
    cb = flat_r[0].shape[1] // B
    q = width // n

    def body(*refs):
        left = jnp.concatenate([r[...] for r in refs[:nl]], 0)
        right = jnp.concatenate([r[...] for r in refs[nl : nl + len(flat_r)]], 0)
        got = dot_tn(left, right).reshape(n, q, B)
        if other is not None:
            got = got + refs[-2][...].astype(F32)
        refs[-1][...] = got.astype(BF)

    spec = pl.BlockSpec((n, q, B), lambda j: (0, j, 0))
    in_specs = [pl.BlockSpec((a.shape[0], width), lambda j: (0, half)) for a in flat_l]
    in_specs += [pl.BlockSpec((tokens_each, B), lambda j: (0, j)) for a in flat_r]
    args = flat_l + flat_r
    if other is not None:
        in_specs.append(spec)
        args = args + [other]
    tokens = sum(a.shape[0] for a in flat_l)
    return kernel_call(
        body, [sds((n, cb * q, B), BF)], args, flops=2 * tokens * width * cb * B,
        grid=(cb,), in_specs=in_specs, out_specs=[spec],
    )[0]


def grad_rows_twice(lhs, rhs, tokens_each, width, n):
    flat_r = sum(rhs, [])
    nl = len(lhs)
    cb = flat_r[0].shape[1] // B
    q = width // n

    def body(*refs):
        left = jnp.concatenate([r[...] for r in refs[:nl]], 0)
        right = jnp.concatenate([r[...] for r in refs[nl : nl + len(flat_r)]], 0)
        got = dot_tn(left, right).astype(BF)
        for h in range(2):
            refs[h - 2][...] = got[h * width : (h + 1) * width].reshape(n, q, B)

    spec = pl.BlockSpec((n, q, B), lambda j: (0, j, 0))
    in_specs = [pl.BlockSpec(a.shape, lambda j: (0, 0)) for a in lhs]
    in_specs += [pl.BlockSpec((tokens_each, B), lambda j: (0, j)) for a in flat_r]
    tokens = sum(a.shape[0] for a in lhs)
    return kernel_call(
        body, [sds((n, cb * q, B), BF)] * 2, lhs + flat_r, flops=4 * tokens * width * cb * B,
        grid=(cb,), in_specs=in_specs, out_specs=[spec] * 2,
    )


def grad_mlp(core, nm, dgu, product, cot, other, size, ff):
    mine = other is not None
    groups = [sum(nm, []), dgu, product, sum(cot, [])]
    counts = [len(g) for g in groups]
    width = groups[0][0].shape[1]
    rows, blocks, side = width // size, 2 * ff // B, width // 2
    low = blocks * rows

    def body(where, *refs):
        at, parts = 0, []
        for k in counts:
            parts.append(refs[at : at + k])
            at += k
        rest, out = refs[at:-1], refs[-1]

        def add(part, s, lo):
            hi = lo + part.shape[0]
            if mine:
                part = part + rest[0][s, lo:hi, :].astype(F32)
            out[s, lo:hi, :] = part.astype(BF)

        lefts, rights, prods, cots = parts
        right = jnp.concatenate([r[...] for r in rights], 0)
        for z in range(size):
            got = dot_tn(jnp.concatenate([r[:, z * rows : (z + 1) * rows] for r in lefts], 0), right)
            for j in range(blocks):
                add(got[:, j * B : (j + 1) * B], z, j * rows)
        left = jnp.concatenate([r[...] for r in prods], 0)
        for j in range(2):
            got = dot_tn(left, jnp.concatenate([r[:, j * B : (j + 1) * B] for r in cots], 0))
            for h in range(2):
                for i in range(2):
                    s = 2 * jnp.bitwise_xor(where[0], h) + i
                    p = h * ff
                    part = [got[p + i * 128 : p + (i + 1) * 128], got[p + 256 + i * 64 : p + 256 + (i + 1) * 64]]
                    add(jnp.concatenate(part, 0), s, low + j * 192)

    whole_of = lambda a: pl.BlockSpec(a.shape, lambda i, w: (0,) * a.ndim)
    in_specs = [whole_of(a) for a in groups[0]]
    in_specs += [pl.BlockSpec((a.shape[0], 2 * ff), lambda i, w: (0, 0 if mine else 1)) for a in dgu]
    in_specs += [whole_of(a) for a in product]
    in_specs += [pl.BlockSpec((a.shape[0], side), lambda i, w: (0, jnp.bitwise_xor(w[0], 0 if mine else 1))) for a in groups[3]]
    args = sum(groups, []) + ([other] if mine else [])
    out = sds((size, low + 384, B), BF)
    return pl.pallas_call(
        body,
        out_shape=out,
        grid_spec=pltpu.PrefetchScalarGridSpec(
            num_scalar_prefetch=1, grid=(1,), in_specs=in_specs + [whole_of(out)] * mine, out_specs=whole_of(out)
        ),
        compiler_params=pltpu.CompilerParams(vmem_limit_bytes=VMEM_LIMIT),
        cost_estimate=cost(6 * 1024 * width * 2 * ff, sum(a.size * 2 for a in args)),
    )(core, *args)


def over_blocks(block, shared, per_block, outs, flops, total=False):
    flat = []
    shape = []
    for a in shared:
        shape.append(len(a) if isinstance(a, list) else None)
        flat += a if isinstance(a, list) else [a]
    nb, k, o = len(per_block), len(per_block[0]), len(outs[0])
    scalars = sum(1 for a in flat if a.dtype == jnp.int32)
    args = flat + sum(per_block, [])
    out_shapes = sum(outs, []) + ([total] if total else [])

    def body(*refs):
        at, head = 0, []
        for m in shape:
            head.append(refs[at] if m is None else refs[at : at + m])
            at += 1 if m is None else m
        ins, results = refs[at : at + nb * k], refs[at + nb * k :]
        tail = ()
        if total:
            results[-1][...] = jnp.zeros_like(results[-1])
            tail = (results[-1],)
        for b in range(nb):
            block(*head, *ins[b * k : (b + 1) * k], *results[b * o : (b + 1) * o], *tail)

    got = kernel_call(body, out_shapes, args, flops=flops * nb, scalars=scalars)
    return [got[b * o : (b + 1) * o] for b in range(nb)], (got[-1] if total else None)


def make_body(size, plane, halves):
    n = plane.n
    parts = 2 if halves else 1
    one_by_one = [[r] for r in (n - 1, *range(1, n - 1), 0)]
    three = [[n - 1], list(range(1, n - 1)), [0]]

    def body(tokens, segment_ids, attn_gain, w_query, w_key, w_value, query_gain, key_gain,
             w_out, mlp_gain, w_gate, w_up, w_down, cotangent):
        t = plane.index()
        c = lax.axis_index("c") if halves else 0
        rows, width = tokens.shape
        length = segment_ids.shape[1]
        assert rows == length
        half = rows // 2
        cb = width // B
        wrows = w_query.shape[0]
        cut_a, cut_b = 2 * wrows, 2 * w_gate.shape[1] // n // parts // B * wrows
        out_rows, down_rows = w_out.shape[0] // parts // n, w_down.shape[0] // parts // n
        ff = n * down_rows
        spread = plane.square and halves and size == 4 and ff == 384 and width == 1024
        core = jnp.stack([c]).astype(jnp.int32)
        gain_in, gain_mid = attn_gain[None, :], mlp_gain[None, :]
        qg, kg = query_gain[None, :], key_gain[None, :]
        freq = ROPE_BASE ** (-2.0 * (jnp.arange(HEAD) % (HEAD // 2)).astype(F32) / HEAD)[None, :]

        def pick(col_weights, row_weight):
            each = [w.shape[1] // n // parts for w in col_weights]
            total = sum(each)
            high = total // B * wrows
            q = row_weight.shape[0] // parts // n if row_weight is not None else 0
            where = jnp.stack([t * parts + c, c * n + t]).astype(jnp.int32)

            def fill(_, *refs):
                a = [r[...] for r in refs[: len(each)]]
                if a:
                    a = jnp.concatenate(a, 1)
                for j in range(total // B):
                    refs[-1][j * wrows : (j + 1) * wrows, :] = a[:, j * B : (j + 1) * B]
                for j in range(cb if q else 0):
                    refs[-1][high + j * q : high + (j + 1) * q, :] = refs[-2][:, j * B : (j + 1) * B]

            rows_of = [row_weight] if q else []
            return pl.pallas_call(
                fill,
                out_shape=sds((high + cb * q, B), BF),
                grid_spec=pltpu.PrefetchScalarGridSpec(
                    num_scalar_prefetch=1,
                    grid=(1,),
                    in_specs=[pl.BlockSpec((wrows, k), lambda i, at: (0, at[0])) for k in each]
                    + [pl.BlockSpec((q, width), lambda i, at: (at[1], 0)) for _ in rows_of],
                    out_specs=pl.BlockSpec((high + cb * q, B), lambda i, at: (0, 0)),
                ),
                compiler_params=pltpu.CompilerParams(vmem_limit_bytes=VMEM_LIMIT),
            )(where, *[pltpu.with_memory_space_constraint(w, pltpu.HBM) for w in (*col_weights, *rows_of)])

        def pick_spread():
            where = jnp.stack([t, c]).astype(jnp.int32)
            aligned = lambda i, k: lambda _, w: (0, 6 * (2 * w[1] + i) + (3 * w[0]) // 2 + k)

            def fill(w, *refs):
                odd = jnp.full((wrows, HEAD), w[0] % 2) == 1
                low = lax.broadcasted_iota(jnp.int32, (wrows, HEAD), 1) < HEAD // 2
                cols = []
                for m in range(2):
                    full, rest = [], []
                    for i in range(2):
                        w0, w1 = (refs[4 * m + 2 * i + k][...].astype(F32) for k in range(2))
                        r0, r1 = half_roll(w0), half_roll(w1)
                        full.append(jnp.where(odd, jnp.where(low, r0, r1), w0))
                        rest.append(jnp.where(odd, r1, w1) if i == 0 else jnp.where(odd, w1, r1))
                    cols += [*full, jnp.where(low, *rest)]
                out, down = refs[-1], refs[-2]
                for j, a in enumerate(cols):
                    out[j // 2 * wrows : (j // 2 + 1) * wrows, j % 2 * HEAD : (j % 2 + 1) * HEAD] = a.astype(BF)
                for j in range(2):
                    out[cut_b + j * 192 : cut_b + (j + 1) * 192, :] = down[:, j * B : (j + 1) * B]

            return pl.pallas_call(
                fill,
                out_shape=sds((cut_b + 384, B), BF),
                grid_spec=pltpu.PrefetchScalarGridSpec(
                    num_scalar_prefetch=1,
                    grid=(1,),
                    in_specs=[pl.BlockSpec((wrows, HEAD), aligned(i, k)) for _ in range(2) for i in range(2) for k in range(2)]
                    + [pl.BlockSpec((192, width // 2), lambda _, w: (w[0], w[1]))],
                    out_specs=pl.BlockSpec((cut_b + 384, B), lambda _, w: (0, 0)),
                ),
                compiler_params=pltpu.CompilerParams(vmem_limit_bytes=VMEM_LIMIT),
            )(where, *[stay(w_gate)] * 4, *[stay(w_up)] * 4, stay(w_down))

        def both(a):
            return [a, swap(a, "c")] if halves else [a]

        def rows_to_chip(got, cut):
            blocks = plane.exchange(lambda i: lax.dynamic_slice_in_dim(got, i, 1, 0)[0, cut:])
            return arrange(plane, t, blocks, cb)

        got_a = lax.all_gather(pick([w_query, w_key, w_value], w_out), "shard", axis=0, tiled=False)

        seg_rows = jnp.pad(segment_ids.astype(BF), ((0, 15), (0, width - length)))
        tok = plane.gather(tokens[:half], jnp.concatenate([tokens[half:], seg_rows], 0))
        cot_own, w_gate, w_up, w_down, tok[1], tok[n - 2] = tie((cotangent, w_gate, w_up, w_down, tok[1], tok[n - 2]))
        cot = plane.gather(cot_own[:half], cot_own[half:])
        piece_b = pick_spread() if spread else pick([w_gate, w_up], w_down)
        prep, _ = over_blocks(
            functools.partial(prep_block, length), [gain_in, freq], tok,
            [[hbm((length, width), BF), hbm((length, HEAD), F32), hbm((length, HEAD), F32), hbm((length, length), F32)]] * n,
            0,
        )
        got_a, prep, piece_b, cot = tie((got_a, prep, piece_b, cot))
        nin, tables = [a[0] for a in prep], [a[1:] for a in prep]
        got_b = lax.all_gather(piece_b, "shard", axis=0, tiled=False)
        wo = rows_to_chip(got_a, cut_a)
        wa, wo = both(got_a), both(wo)

        def term_type(r):
            return sds((rows, width), F32 if r == 0 and plane.square else BF)

        def run(block, shared, ins, outs, flops, order, total=None):
            got, totals = {}, []
            for group in [g[i : i + 2] for g in order for i in range(0, len(g), 2)]:
                mine = [ins[r] for r in group]
                res, tot = over_blocks(block, shared, mine, [outs(r) for r in group], flops, total)
                got.update(zip(group, res))
                totals.append(tot)
            return [{r: got[r][i] for r in got} for i in range(len(outs(0)))], totals

        (lin, vals, mixed, partial), _ = run(
            functools.partial(attend_block, parts, wrows), [qg, kg, wa, wo],
            [[stay(a) for a in (nin[r], *tables[r])] for r in range(n)],
            lambda r: [hbm((length, parts * 3 * HEAD), F32), hbm((length, parts * HEAD), BF),
                       hbm((length, parts * GROUP * HEAD), BF), term_type(r)],
            2 * length * width * parts * 6 * HEAD, three,
        )
        lin, vals, mixed, partial = ([a[r] for r in range(n)] for a in (lin, vals, mixed, partial))
        terms = plane.scatter(partial)
        hidden, nm0, nm1 = kernel_call(
            mid_kernel,
            [hbm((rows, width), F32), sds((half, width), BF), sds((half, width), BF)],
            [tokens, gain_mid, *terms],
        )
        nm = plane.gather(nm0, nm1)
        got_b, nm[1][1], nm[n - 2][0] = tie((got_b, nm[1][1], nm[n - 2][0]))
        wgu, wd = both(got_b), [] if spread else both(rows_to_chip(got_b, cut_b))

        def mlp(order):
            return run(
                functools.partial(mlp_block, spread, parts, wrows, ff), [core, wgu, wd],
                {r: [*nm[r], *[stay(a) for a in cot[r]]] for g in order for r in g},
                lambda r: [sds((rows, parts * ff), BF), sds((rows, parts * 2 * ff), BF),
                           hbm((rows, width), term_type(r).dtype), term_type(r)],
                2 * length * width * parts * 7 * ff, order,
            )[0]

        blocks = mlp([[0], [n - 1], list(range(1, n - 1))])
        product, dgu, partial, d_mid = ([a[r] for r in range(n)] for a in blocks)
        terms_mid = plane.scatter(d_mid)

        def pair(make, between=lambda a: a):
            if halves:
                return make(0, swap(between(make(1, None)), "c"))
            return lax.psum(make(0, None), "c")

        def exchanged(low):
            return plane.exchange(lambda i: lax.dynamic_index_in_dim(low, i, 0, keepdims=False))

        def merged(lhs, rhs, width_, other, low, gains=()):
            if halves:
                return grad_columns(plane, t, lhs, rhs, 0, width_, size, swap(other, "c"), low, gains)
            a = grad_columns(plane, t, lhs, rhs, 0, width_, size, None)
            return jnp.concatenate([lax.psum(a, "c"), jnp.stack(low, 0)], 1)

        if spread:
            make_b = lambda other: grad_mlp(core, nm, dgu, product, cot, other, size, ff)
            product, terms_mid[-1] = tie((product, terms_mid[-1]))
            other_b = make_b(None)
            terms_mid, other_b = tie((terms_mid, other_b))
        d_hidden, dh0, dh1, mlp_grad = kernel_call(
            mid_back_kernel,
            [hbm((rows, width), F32), sds((half, width), BF), sds((half, width), BF), sds((1, width), F32)],
            [hidden, cotangent, gain_mid, *terms_mid],
        )
        dh = plane.gather_near(dh0, dh1)
        if spread:
            grads_b = make_b(swap(other_b, "c"))
        else:
            dgu = [[a] for a in dgu]
            gu_other = grad_columns(plane, t, nm, dgu, 1, 2 * ff, size, None) if halves else None
            grads_b = merged(nm, dgu, 2 * ff, gu_other, exchanged(pair(lambda h, o: grad_rows(product, cot, half, h, ff, n, o))))
        dh[1], dh[n - 2], grads_b, dh[0] = tie((dh[1], dh[n - 2], grads_b, dh[0]))
        grads_b = lax.psum_scatter(grads_b.reshape(-1, B), "shard", scatter_dimension=0, tiled=True)

        def back(order, dh):
            return run(
                functools.partial(attend_back_block, parts, wrows), [qg, kg, wa, [stay(a) for a in wo]],
                {r: [*[stay(a) for a in dh[r]], *[stay(a) for a in (*tok[r], lin[r], vals[r], *tables[r])]]
                 for g in order for r in g},
                lambda r: [hbm((rows, parts * 4 * HEAD), BF), hbm((rows, width), term_type(r).dtype)],
                2 * length * width * parts * 6 * HEAD, order, sds((1, width + 2 * HEAD), F32),
            )

        own_back, gains = back([[0]], dh)
        dh = plane.gather_far(dh)
        dh[n - 1], own_back, partial = tie((dh[n - 1], own_back, partial))
        near_out = plane.send_near(partial)
        if halves:
            out, other = grad_rows_twice(
                [stay(a) for a in mixed], [[stay(a) for a in b] for b in dh], half, GROUP * HEAD, n)
            out = (out.astype(F32) + swap(other, "c").astype(F32)).astype(BF)
        else:
            out = pair(lambda h, o: grad_rows(mixed, dh, half, h, GROUP * HEAD, n, o))
        dh[1:], partial, out = tie((dh[1:], partial, out))
        out = exchanged(out)
        far_out = plane.send_far(partial)
        near_back, more = back([list(range(1, n - 1))], dh)
        dh[n - 1], out, far_out, near_back, partial, near_out = tie(
            (dh[n - 1], out, far_out, near_back, partial, near_out))
        terms_out = [partial[0], *near_out, far_out] if plane.square else plane.scatter(partial)
        near_in = plane.send_near(near_back[1])
        separate = plane.square and halves and size == n
        if separate:
            dh[n - 1], out = tie((dh[n - 1], arrange_rows(plane, t, out)))
            out = lax.psum_scatter(out, "shard", scatter_dimension=0, tiled=True)
        far_back, last = back([[n - 1]], dh)
        gains = gains + more + last
        far_back, grads_b, terms_out, near_in = tie((far_back, grads_b, terms_out, near_in))
        grads_b = plane.near(grads_b)
        dqkv, d_in = ([{**a, **b, **c}[r] for r in range(n)] for a, b, c in zip(own_back, near_back, far_back))
        dqkv = [[stay(a)] for a in dqkv]
        lhs = [[stay(a)] for a in nin]
        qkv_other = grad_columns(plane, t, lhs, dqkv, 1, 4 * HEAD, size, None) if halves else None
        if halves:
            qkv_other, grads_b, out = tie((qkv_other, grads_b, out))
        if separate:
            grads_a = merged(lhs, dqkv, 4 * HEAD, qkv_other, None, [mlp_grad, *gains])
            grads_b, grads_a = tie((grads_b, grads_a))
            grads_b = plane.far_halves(grads_b)
            d_in[n - 1], grads_b = tie((d_in[n - 1], grads_b))
            terms_in = [d_in[0], *near_in, plane.send_far(d_in)]
        else:
            grads_a = merged(lhs, dqkv, 4 * HEAD, qkv_other, out)
            grads_b = plane.far_halves(grads_b)
            terms_in = plane.scatter(d_in)
        grads_a = lax.psum_scatter(grads_a.reshape(-1, B), "shard", scatter_dimension=0, tiled=True)
        if separate:
            grads_a = jnp.concatenate([grads_a, out], 0)
        activations = kernel_call(out_kernel, [sds((rows, width), BF)], [hidden, *terms_out])[0]

        def assemble(mine, outs, write):
            got = [(r, 0, a) for r, a in enumerate(mine)]
            if halves:
                got += [(r, 1, swap(a, "c")) for r, a in enumerate(mine)]

            def body(where, *refs):
                total = 0.0
                for (r, other, _), ref in zip(got, refs):
                    core = jnp.bitwise_xor(where[1], other) if halves else 0
                    lines = write(ref, plane.place(where[0], r), core, refs[len(got) :])
                    total = total + lines if separate and write is write_a else total
                if separate and write is write_a:
                    i = 0
                    for out in refs[len(got) + 4 :]:
                        for j in range(0, out.shape[1], B):
                            k = min(B, out.shape[1])
                            at = 0 if out.shape[1] > HEAD else HEAD * (i % 2)
                            line = i if out.shape[1] > HEAD else 2 * width // B
                            out[:, j : j + k] = total[line : line + 1, at : at + k]
                            i += 1

            if write is write_spread:
                body = lambda where, *refs: write(where, refs[: len(got)], refs[len(got) :])
            where = jnp.stack([t, c]).astype(jnp.int32)
            return kernel_call(body, outs, [where] + [a for _, _, a in got], scalars=1)

        def write_cols(ref, j, todo, src, core):
            a = ref[j * wrows : (j + 1) * wrows, :].astype(F32)
            for lo, hi, out, per, at in todo:
                start = pl.multiple_of((src * parts + core) * per + at, HEAD)
                out[:, pl.ds(start, hi - lo)] = a[:, lo:hi]

        def write_rows(ref, base, q, src, core, out):
            start = pl.multiple_of((core * n + src) * q, 16)
            for j in range(cb):
                a = ref[base + j * q : base + (j + 1) * q, :].astype(F32)
                out[pl.ds(start, q), j * B : (j + 1) * B] = a

        def write_b(ref, src, core, outs):
            gate, up, down = outs
            for j in range(2 * ff // B):
                todo = []
                for out, lo in ((gate, 0), (up, ff)):
                    a, b = max(j * B, lo), min((j + 1) * B, lo + ff)
                    if a < b:
                        todo.append((a - j * B, b - j * B, out, ff, a - lo))
                write_cols(ref, j, todo, src, core)
            write_rows(ref, cut_b, down_rows, src, core, down)

        def write_spread(where, refs, outs):
            gate, up, down = outs
            odd = jnp.full((wrows, HEAD), where[0] % 2) == 1
            low = lax.broadcasted_iota(jnp.int32, (wrows, HEAD), 1) < HEAD // 2
            for other in range(2):
                core = jnp.bitwise_xor(where[1], other)
                mine = refs[other * n : (other + 1) * n]
                for r, ref in enumerate(mine):
                    for j in range(2):
                        down[pl.ds(pl.multiple_of(plane.place(where[0], r) * 192, 64), 192),
                             pl.ds(pl.multiple_of((2 * core + j) * B, B), B)] = (
                            ref[cut_b + j * 192 : cut_b + (j + 1) * 192, :].astype(F32))
                for k in range(2):
                    one, two = mine[2 * k], mine[2 * k + 1]
                    pair_at = jnp.bitwise_xor(where[0] // 2, k)
                    for m, out in enumerate((gate, up)):
                        def block(ref, j):
                            j = 3 * m + j
                            return ref[j // 2 * wrows : (j // 2 + 1) * wrows, j % 2 * HEAD : (j % 2 + 1) * HEAD].astype(F32)

                        pairs = [(block(one, j), block(two, j)) for j in range(3)]
                        even = [jnp.where(odd, b, a) for a, b in pairs]
                        odds = [jnp.where(odd, a, b) for a, b in pairs]
                        for i in range(2):
                            at = pl.multiple_of(768 * (2 * core + i) + 384 * pair_at, HEAD)
                            rolled = half_roll(odds[i])
                            rest_even = even[2] if i == 0 else half_roll(even[2])
                            rest_odd = half_roll(odds[2]) if i == 0 else odds[2]
                            out[:, pl.ds(at, HEAD)] = even[i]
                            out[:, pl.ds(at + HEAD, HEAD)] = jnp.where(low, rest_even, rolled)
                            out[:, pl.ds(at + 2 * HEAD, HEAD)] = jnp.where(low, rolled, rest_odd)

        def write_a(ref, src, core, outs):
            q, k, v, out = outs[:4]
            write_cols(ref, 0, [(0, B, q, B, 0)], src, core)
            write_cols(ref, 1, [(0, HEAD, k, HEAD, 0), (HEAD, B, v, HEAD, 0)], src, core)
            write_rows(ref, cut_a + (16 if separate else 0), out_rows, src, core, out)
            return ref[cut_a : cut_a + 16, :].astype(F32)

        like = lambda w: sds(w.shape, F32)
        gate_g, up_g, down_g = assemble(grads_b, [like(w_gate), like(w_up), like(w_down)], write_spread if spread else write_b)
        grads_a, gate_g, up_g, down_g, activations, terms_in = tie(
            (grads_a, gate_g, up_g, down_g, activations, terms_in))
        input_grad = kernel_call(
            last_kernel, [sds((rows, width), BF)], [tokens, d_hidden, gain_in, *terms_in])[0]
        grads_a, input_grad = tie((plane.far_halves(plane.near(grads_a)), input_grad))
        outs_a = [like(w_query), like(w_key), like(w_value), like(w_out)]
        if separate:
            gain_outs = [sds((1, k), F32) for k in (width, width, HEAD, HEAD)]
            query_g, key_g, value_g, out_g, *gains = assemble(grads_a, outs_a + gain_outs, write_a)
            gains = [g[0] for g in gains]
        else:
            query_g, key_g, value_g, out_g = assemble(grads_a, outs_a, write_a)
            gains = functools.reduce(jnp.add, gains)
            gains = [gains[:, :width], mlp_grad, gains[:, width : width + HEAD], gains[:, width + HEAD :]]
            gains = [g[0] for g in lax.psum(gains, ("shard", "y", "x", "c"))]

        return (
            activations,
            input_grad,
            gains[0],
            query_g,
            key_g,
            value_g,
            gains[2],
            gains[3],
            out_g,
            gains[1],
            gate_g,
            up_g,
            down_g,
        )

    return body


def solution(mesh):
    size, replicas = mesh.shape["shard"], mesh.shape["replica"]
    ny, nx = replicas // 4, 2
    assert size == ny * nx
    plane = Plane(ny, nx)
    fine = Mesh(mesh.devices.reshape(size, ny, nx, 2), ("shard", "y", "x", "c"))
    halves = KV_HEADS % (2 * plane.n) == 0
    every = P(("shard", "y", "x", "c"), None)
    shard, copy = P("shard", None), P()
    return jax.shard_map(
        make_body(size, plane, halves),
        mesh=fine,
        in_specs=(every, every, copy, shard, shard, shard, copy, copy, shard, copy, shard, shard, shard, every),
        out_specs=(every, every, copy, shard, shard, shard, copy, copy, shard, copy, shard, shard, shard),
        check_vma=False,
    )
```

```python
import functools
import math

import jax
import jax.numpy as jnp
from jax import lax
from jax.experimental import pallas as pl
from jax.experimental.pallas import tpu as pltpu
from jax.sharding import Mesh
from jax.sharding import PartitionSpec as P

HEADS = 16
KV_HEADS = 8
HEAD = 128
GROUP = HEADS // KV_HEADS

EPS = 1e-06
ROPE_BASE = 1000000.0
MASKED = -1e30
SCALE = HEAD ** (-0.5)
BF = jnp.bfloat16
F32 = jnp.float32
SWAP = [(0, 1), (1, 0)]
VMEM_LIMIT = 24 * 1024 * 1024
B = 256


def dot(a, b):
    return jnp.dot(a, b, preferred_element_type=F32)


def dot_nt(a, b):
    return lax.dot_general(a, b, (((1,), (1,)), ((), ())), preferred_element_type=F32)


def dot_tn(a, b):
    return lax.dot_general(a, b, (((0,), (0,)), ((), ())), preferred_element_type=F32)


def swap(a, axis):
    return lax.ppermute(a, axis, SWAP)


tie = lax.optimization_barrier


def stay(a):
    return pltpu.with_memory_space_constraint(a, pltpu.HBM)


def sds(shape, dtype):
    return jax.ShapeDtypeStruct(shape, dtype)


def hbm(shape, dtype):
    return pltpu.HBM(shape, dtype)


VM = pl.BlockSpec(memory_space=pltpu.VMEM)
SM = pl.BlockSpec(memory_space=pltpu.SMEM)


def cost(flops, moved):
    return pl.CostEstimate(flops=int(flops), bytes_accessed=int(moved), transcendentals=0)


def kernel_call(body, outs, args, flops=0, scalars=0, **kw):
    moved = sum(a.size * a.dtype.itemsize for a in args) + sum(math.prod(o.shape) * o.dtype.itemsize for o in outs)
    if "grid" not in kw:
        kw = dict(in_specs=[SM] * scalars + [VM] * (len(args) - scalars), out_specs=[VM] * len(outs))
    return pl.pallas_call(
        body,
        out_shape=outs,
        compiler_params=pltpu.CompilerParams(vmem_limit_bytes=VMEM_LIMIT),
        cost_estimate=cost(flops, moved),
        **kw,
    )(*args)


class Plane:
    def __init__(self, ny, nx):
        self.ny, self.nx, self.n = ny, nx, ny * nx
        self.square = ny == 2 and nx == 2
        self.axes = ("y", "x")

    def index(self):
        return lax.axis_index("y") * self.nx + lax.axis_index("x")

    def place(self, t, r):
        return jnp.bitwise_xor(t, r) if self.square else r

    def gather(self, top, low):
        return self.gather_far(self.gather_near(top, low))

    def gather_near(self, top, low):
        if not self.square:
            g, h = (lax.all_gather(a, self.axes, axis=0, tiled=False) for a in (top, low))
            return [[g[i], h[i]] for i in range(self.n)]
        ty, lx = swap(top, "y"), swap(low, "x")
        tx, ly = swap(top, "x"), swap(low, "y")
        return [[top, low], [tx, lx], [ty, ly]]

    def gather_far(self, near, *after):
        if not self.square:
            return near
        (ty, lx), _ = tie(([near[2][0], near[1][1]], after))
        return near + [[swap(ty, "x"), swap(lx, "y")]]

    def near(self, a):
        if not self.square:
            g = lax.all_gather(a, self.axes, axis=0, tiled=False)
            return [g[i] for i in range(self.n)]
        return [a, swap(a, "x"), swap(a, "y")]

    def far(self, a, near):
        if not self.square:
            return near
        return near + [lax.ppermute(a, self.axes, [(i, 3 - i) for i in range(4)])]

    def far_halves(self, near):
        if not self.square:
            return near
        k = near[0].shape[0] // 32 * 16
        return near + [jnp.concatenate([swap(near[2][:k], "x"), swap(near[1][k:], "y")], 0)]

    def gather_whole(self, a):
        return self.far(a, self.near(a))

    def send_far(self, blocks):
        return lax.ppermute(blocks[3], self.axes, [(i, 3 - i) for i in range(4)]) if self.square else blocks[-1]

    def send_near(self, blocks):
        return [swap(blocks[1], "x"), swap(blocks[2], "y")] if self.square else []

    def scatter(self, blocks, far=None):
        if not self.square:
            a = lax.psum_scatter(jnp.concatenate(blocks, 0), self.axes, scatter_dimension=0, tiled=True)
            return [a]
        far = self.send_far(blocks) if far is None else far
        return [blocks[0], swap(blocks[1], "x"), swap(blocks[2], "y"), far]

    def exchange(self, slice_for):
        if not self.square:
            a = jnp.stack([slice_for(i) for i in range(self.n)], 0)
            a = lax.all_to_all(a, self.axes, split_axis=0, concat_axis=0, tiled=True)
            return [a[i] for i in range(self.n)]
        t = self.index()
        return [
            slice_for(t),
            swap(slice_for(jnp.bitwise_xor(t, 1)), "x"),
            swap(slice_for(jnp.bitwise_xor(t, 2)), "y"),
            lax.ppermute(slice_for(jnp.bitwise_xor(t, 3)), self.axes, [(i, 3 - i) for i in range(4)]),
        ]


def columns(ref, lo, count, rows):
    s = ref.shape[0]
    got = [ref[:, (lo + j) * rows : (lo + j + 1) * rows, :].reshape(s * rows, B) for j in range(count)]
    return got[0] if count == 1 else jnp.concatenate(got, 1)


def split(ref):
    return jnp.concatenate([ref[0][...], ref[1][...]], 0)


def rsq(v):
    return lax.rsqrt(jnp.mean(v * v, axis=-1, keepdims=True) + EPS)


def norm_back(v, r, gain, d):
    dg = d * gain
    return r * (dg - v * (r * r) * jnp.mean(dg * v, axis=-1, keepdims=True))


def half_roll(u):
    return pltpu.roll(u, HEAD // 2, 1)


def token_rows(top, low):
    return jnp.concatenate([top[...], low[: top.shape[0], :]], 0).astype(F32)


def prep_block(length, gain, freq, tok0, tok1, nin, cos, sin, mask):
    half = length // 2
    x = token_rows(tok0, tok1)
    nin[...] = (x * rsq(x) * gain[...]).astype(BF)
    row = tok1[half : half + 16, :length].astype(F32)[:1]
    row = jnp.broadcast_to(row, (length, length))
    col = row.T
    start = jnp.sum(jnp.where(row < col, 1.0, 0.0), axis=-1, keepdims=True)
    i = lax.broadcasted_iota(jnp.int32, (length, length), 0)
    j = lax.broadcasted_iota(jnp.int32, (length, length), 1)
    mask[...] = jnp.where((j <= i) & (row == col), 1.0, 0.0)
    pos = lax.broadcasted_iota(jnp.int32, (length, HEAD), 0).astype(F32) - start
    ang = pos * freq[...]
    lane = lax.broadcasted_iota(jnp.int32, (length, HEAD), 1)
    s = jnp.sin(ang)
    cos[...] = jnp.cos(ang)
    sin[...] = jnp.where(lane < HEAD // 2, -s, s)


def ones(rows, value=1.0):
    return jnp.full((rows, HEAD), value, BF)


def twice(a):
    return jnp.concatenate([a, a], 1)


def head_mean(v):
    return dot(v.astype(BF), ones(HEAD, 1.0 / HEAD))


def head_rsq(v):
    return lax.rsqrt(head_mean(v * v) + EPS)


def head_back(v, r, gain, d):
    dg = d * gain
    return r * (dg - v * (r * r) * head_mean(dg * v))


def weights_of(qr, kr, keep):
    return jnp.where(keep, jnp.exp(dot_nt(qr, kr) * SCALE), 0.0)


def heads_below(a):
    return jnp.concatenate([a[:, g * HEAD : (g + 1) * HEAD] for g in range(GROUP)], 0)


def heads_beside(a):
    rows = a.shape[0] // GROUP
    return jnp.concatenate([a[g * rows : (g + 1) * rows] for g in range(GROUP)], 1)


def repeat(a):
    return jnp.concatenate([a] * GROUP, 0)


def attend_block(parts, wrows, qg, kg, wa, wo, nin, cos, sin, mask, lin, vals, mixed, partial):
    keep = repeat(mask[...]) > 0.0
    c, s = cos[...], sin[...]
    c2, s2 = repeat(c), repeat(s)
    n = nin[...]
    one = ones(n.shape[0])
    out = None
    for h in range(parts):
        q = dot(n, columns(wa[h], 0, 1, wrows))
        kv = dot(n, columns(wa[h], 1, 1, wrows))
        k, v = kv[:, :HEAD], kv[:, HEAD:].astype(BF)
        lin[:, h * 3 * HEAD : h * 3 * HEAD + 2 * HEAD] = q
        lin[:, h * 3 * HEAD + 2 * HEAD : (h + 1) * 3 * HEAD] = k
        vals[:, h * HEAD : (h + 1) * HEAD] = v
        kn = k * head_rsq(k) * kg[...]
        kr = (kn * c + half_roll(kn) * s).astype(BF)
        q = heads_below(q)
        qn = q * head_rsq(q) * qg[...]
        e = weights_of((qn * c2 + half_roll(qn) * s2).astype(BF), kr, keep)
        m = dot(e.astype(BF), jnp.concatenate([v, one], 1))
        m = heads_beside((m[:, :HEAD] / m[:, HEAD:]).astype(BF))
        mixed[:, h * GROUP * HEAD : (h + 1) * GROUP * HEAD] = m
        term = dot(m, wo[h][...])
        out = term if out is None else out + term
    partial[...] = out.astype(partial.dtype)


def down_rows_of(ref, base, s0):
    def piece(s, lo, hi):
        return jnp.concatenate([ref[s, base + j * 192 + lo : base + j * 192 + hi, :] for j in range(2)], 1)

    return jnp.concatenate([piece(s0, 0, 128), piece(s0 + 1, 0, 128), piece(s0, 128, 192), piece(s0 + 1, 128, 192)], 0)


def mlp_block(spread, parts, wrows, ff, core, wgu, wd, nm0, nm1, cot0, cot1, product, dgu, partial, d_mid):
    n = split((nm0, nm1))
    blocks = 2 * ff // B
    width = n.shape[1]
    side = width // 2
    out, dm = {}, None
    for h in range(parts):
        w = columns(wgu[h], 0, blocks, wrows)
        if spread:
            s0 = 2 * jnp.bitwise_xor(core[0], h)
            where = [pl.multiple_of(jnp.bitwise_xor(core[0], j) * side, side) for j in range(2)]
            d = [(pl.ds(where[j], side), down_rows_of(wgu[j], blocks * wrows, s0)) for j in range(2)]
        else:
            d = [(slice(None), wd[h][...])]
        gu = dot(n, w)
        gate, up = gu[:, :ff], gu[:, ff:]
        sg = jax.nn.sigmoid(gate)
        act = gate * sg
        pr = (act * up).astype(BF)
        product[:, h * ff : (h + 1) * ff] = pr
        dp = None
        for at, rows in d:
            term = dot_nt(jnp.concatenate([cot0[:, at], cot1[:, at]], 0), rows)
            dp = term if dp is None else dp + term
        d_gate = (dp * up * (sg + act * (1.0 - sg))).astype(BF)
        d_up = (dp * act).astype(BF)
        at = h * 2 * ff
        dgu[:, at : at + ff] = d_gate
        dgu[:, at + ff : at + 2 * ff] = d_up
        for j, (_, rows) in enumerate(d):
            term = dot(pr, rows)
            out[j] = out[j] + term if j in out else term
        term = dot_nt(dgu[:, at : at + 2 * ff], w)
        dm = term if dm is None else dm + term
    for j, (at, _) in enumerate(d):
        partial[:, at] = out[j].astype(partial.dtype)
    d_mid[...] = dm.astype(d_mid.dtype)


def attend_back_block(parts, wrows, qg, kg, wa, wo, dh0, dh1, tok0, tok1, lin, vals, cos, sin, mask, dqkv, d_in, gains):
    keep = repeat(mask[...]) > 0.0
    c, s = cos[...], sin[...]
    c2, s2 = repeat(c), repeat(s)
    d = split((dh0, dh1))
    one = ones(d.shape[0])
    din, qgain, kgain = None, 0.0, 0.0
    for h in range(parts):
        dm = heads_below(dot_nt(d, wo[h][...]).astype(BF))
        base = h * 3 * HEAD
        k = lin[:, base + 2 * HEAD : base + 3 * HEAD]
        v = vals[:, h * HEAD : (h + 1) * HEAD]
        rk = head_rsq(k)
        kn = k * rk * kg[...]
        kr = (kn * c + half_roll(kn) * s).astype(BF)
        q = heads_below(lin[:, base : base + GROUP * HEAD])
        rq = head_rsq(q)
        qn = q * rq * qg[...]
        qr = (qn * c2 + half_roll(qn) * s2).astype(BF)
        e = weights_of(qr, kr, keep)
        p = e * twice(1.0 / dot(e.astype(BF), one))
        pd = p * dot_nt(dm, v)
        ds = (pd - p * twice(dot(pd.astype(BF), one))).astype(BF)
        dq = dot(ds, kr) * SCALE
        dk = dot_tn(ds, qr) * SCALE
        dv = dot_tn(p.astype(BF), dm)
        dq = dq * c2 - half_roll(dq) * s2
        dk = dk * c - half_roll(dk) * s
        qgain = qgain + jnp.sum(dq * q * rq, axis=0, keepdims=True)
        kgain = kgain + jnp.sum(dk * k * rk, axis=0, keepdims=True)
        dq = heads_beside(head_back(q, rq, qg[...], dq).astype(BF))
        dk = head_back(k, rk, kg[...], dk).astype(BF)
        both = jnp.concatenate([dq, dk, dv.astype(BF)], 1)
        dqkv[:, h * 4 * HEAD : (h + 1) * 4 * HEAD] = both
        term = dot_nt(both, columns(wa[h], 0, 2, wrows))
        din = term if din is None else din + term
    d_in[...] = din.astype(d_in.dtype)
    x = token_rows(tok0, tok1)
    width = x.shape[1]
    gains[:, :width] += jnp.sum(din * (x * rsq(x)), axis=0, keepdims=True)
    gains[:, width : width + HEAD] += qgain
    gains[:, width + HEAD :] += kgain


def added(refs):
    total = refs[0][...].astype(F32)
    for r in refs[1:]:
        total = total + r[...].astype(F32)
    return total


def mid_kernel(tokens, gain, *refs):
    terms, (hidden, nm0, nm1) = refs[:-3], refs[-3:]
    h = tokens[...].astype(F32) + added(terms)
    hidden[...] = h
    nm = (h * rsq(h) * gain[...]).astype(BF)
    nm0[...] = nm[: nm0.shape[0]]
    nm1[...] = nm[nm0.shape[0] :]


def mid_back_kernel(hidden, cot, gain, *refs):
    terms, (d_hidden, low0, low1, ggrad) = refs[:-4], refs[-4:]
    d = added(terms)
    h = hidden[...]
    r = rsq(h)
    out = cot[...].astype(F32) + norm_back(h, r, gain[...], d)
    d_hidden[...] = out
    low0[...] = out[: low0.shape[0]].astype(BF)
    low1[...] = out[low0.shape[0] :].astype(BF)
    ggrad[...] = jnp.sum(d * h * r, axis=0, keepdims=True)


def last_kernel(tokens, d_hidden, gain, *refs):
    terms, (out,) = refs[:-1], refs[-1:]
    x = tokens[...].astype(F32)
    out[...] = (d_hidden[...] + norm_back(x, rsq(x), gain[...], added(terms))).astype(BF)


def gain_lines(mlp_grad, parts):
    total = parts[0][...]
    for p in parts[1:]:
        total = total + p[...]
    width = mlp_grad.shape[1]
    vectors = [total[:, :width], mlp_grad[...], total[:, width:]]
    lines = [v[:, i : i + B] for v in vectors for i in range(0, v.shape[1], B)]
    row = lax.broadcasted_iota(jnp.int32, (16, B), 0)
    block = jnp.zeros((16, B), F32)
    for i, line in enumerate(lines):
        block = jnp.where(row == i, line, block)
    return block


def out_kernel(hidden, *refs):
    refs[-1][...] = (hidden[...] + added(refs[:-1])).astype(BF)


def arrange(plane, t, blocks, cb):
    q = blocks[0].shape[0] // cb

    def body(where, *refs):
        for r, ref in enumerate(refs[:-1]):
            start = pl.multiple_of(plane.place(where[0], r) * q, 16)
            for j in range(cb):
                refs[-1][pl.ds(start, q), j * B : (j + 1) * B] = ref[j * q : (j + 1) * q, :]

    return kernel_call(body, [sds((len(blocks) * q, cb * B), BF)], [t.astype(jnp.int32)[None], *blocks], scalars=1)[0]


def arrange_rows(plane, t, blocks):
    q, width = blocks[0].shape

    def body(where, *refs):
        for r, ref in enumerate(refs[:-1]):
            refs[-1][pl.ds(pl.multiple_of(plane.place(where[0], r) * q, 16), q), :] = ref[...]

    return kernel_call(body, [sds((len(blocks) * q, width), BF)], [t.astype(jnp.int32)[None], *blocks], scalars=1)[0]


def grad_columns(plane, t, lhs, rhs, half, width, size, other, below=None, gains=()):
    nblk = width // B
    flat_l, flat_r = sum(lhs, []), sum(rhs, [])
    nl, nr = len(flat_l), len(flat_r)
    rows = flat_l[0].shape[1] // size
    ready = below is not None and not isinstance(below, list)
    more = 0 if below is None else below.shape[1] if ready else below[0].shape[0]

    def body(where, *refs):
        left = jnp.concatenate([r[...] for r in refs[:nl]], 0)
        right = jnp.concatenate([r[...] for r in refs[nl : nl + nr]], 0)
        gain_refs, rest, out = refs[nl + nr : nl + nr + ng], refs[nl + nr + ng : -1], refs[-1]
        if ng:
            out[0, nblk * rows + more :, :] = gain_lines(gain_refs[0], gain_refs[1:]).astype(BF)
        got = dot_tn(left, right)
        for j in range(nblk):
            part = got[:, j * B : (j + 1) * B]
            if other is not None:
                part = part + rest[0][0, j * rows : (j + 1) * rows, :].astype(F32)
            out[0, j * rows : (j + 1) * rows, :] = part.astype(BF)
        if ready:
            out[0, nblk * rows : nblk * rows + more, :] = rest[-1][0]
        elif more:
            z = pl.program_id(0)
            for r in range(plane.n):
                @pl.when(plane.place(where[0], r) == z)
                def _():
                    out[0, nblk * rows : nblk * rows + more, :] = rest[-plane.n + r][...]

    ng = len(gains)
    tail = 16 if ng else 0
    tall = lambda k: pl.BlockSpec((1, k, B), lambda z, w: (z, 0, 0))
    in_specs = [pl.BlockSpec((a.shape[0], rows), lambda z, w: (0, z)) for a in flat_l]
    in_specs += [pl.BlockSpec((a.shape[0], width), lambda z, w: (0, half)) for a in flat_r]
    in_specs += [pl.BlockSpec(a.shape, lambda z, w: (0, 0)) for a in gains]
    args = flat_l + flat_r + list(gains)
    if other is not None:
        in_specs.append(tall(nblk * rows))
        args = args + [other]
    if ready:
        in_specs.append(tall(more))
        args = args + [below]
    elif more:
        in_specs += [pl.BlockSpec((more, B), lambda z, w: (0, 0))] * plane.n
        args = args + below
    tokens = sum(a.shape[0] for a in flat_l)
    out = sds((size, nblk * rows + more + tail, B), BF)
    return pl.pallas_call(
        body,
        out_shape=out,
        grid_spec=pltpu.PrefetchScalarGridSpec(
            num_scalar_prefetch=1, grid=(size,), in_specs=in_specs, out_specs=tall(nblk * rows + more + tail)
        ),
        compiler_params=pltpu.CompilerParams(vmem_limit_bytes=VMEM_LIMIT),
        cost_estimate=cost(
            2 * tokens * rows * size * width, sum(a.size * 2 for a in args) + math.prod(out.shape) * 2
        ),
    )(t.astype(jnp.int32)[None], *args)


def grad_rows(lhs, rhs, tokens_each, half, width, n, other):
    flat_l, flat_r = lhs, sum(rhs, [])
    nl = len(flat_l)
    cb = flat_r[0].shape[1] // B
    q = width // n

    def body(*refs):
        left = jnp.concatenate([r[...] for r in refs[:nl]], 0)
        right = jnp.concatenate([r[...] for r in refs[nl : nl + len(flat_r)]], 0)
        got = dot_tn(left, right).reshape(n, q, B)
        if other is not None:
            got = got + refs[-2][...].astype(F32)
        refs[-1][...] = got.astype(BF)

    spec = pl.BlockSpec((n, q, B), lambda j: (0, j, 0))
    in_specs = [pl.BlockSpec((a.shape[0], width), lambda j: (0, half)) for a in flat_l]
    in_specs += [pl.BlockSpec((tokens_each, B), lambda j: (0, j)) for a in flat_r]
    args = flat_l + flat_r
    if other is not None:
        in_specs.append(spec)
        args = args + [other]
    tokens = sum(a.shape[0] for a in flat_l)
    return kernel_call(
        body, [sds((n, cb * q, B), BF)], args, flops=2 * tokens * width * cb * B,
        grid=(cb,), in_specs=in_specs, out_specs=[spec],
    )[0]


def grad_rows_twice(lhs, rhs, tokens_each, width, n):
    flat_r = sum(rhs, [])
    nl = len(lhs)
    cb = flat_r[0].shape[1] // B
    q = width // n

    def body(*refs):
        left = jnp.concatenate([r[...] for r in refs[:nl]], 0)
        right = jnp.concatenate([r[...] for r in refs[nl : nl + len(flat_r)]], 0)
        got = dot_tn(left, right).astype(BF)
        for h in range(2):
            refs[h - 2][...] = got[h * width : (h + 1) * width].reshape(n, q, B)

    spec = pl.BlockSpec((n, q, B), lambda j: (0, j, 0))
    in_specs = [pl.BlockSpec(a.shape, lambda j: (0, 0)) for a in lhs]
    in_specs += [pl.BlockSpec((tokens_each, B), lambda j: (0, j)) for a in flat_r]
    tokens = sum(a.shape[0] for a in lhs)
    return kernel_call(
        body, [sds((n, cb * q, B), BF)] * 2, lhs + flat_r, flops=4 * tokens * width * cb * B,
        grid=(cb,), in_specs=in_specs, out_specs=[spec] * 2,
    )


def grad_mlp(core, nm, dgu, product, cot, other, size, ff):
    mine = other is not None
    groups = [sum(nm, []), dgu, product, sum(cot, [])]
    counts = [len(g) for g in groups]
    width = groups[0][0].shape[1]
    rows, blocks, side = width // size, 2 * ff // B, width // 2
    low = blocks * rows

    def body(where, *refs):
        at, parts = 0, []
        for k in counts:
            parts.append(refs[at : at + k])
            at += k
        rest, out = refs[at:-1], refs[-1]

        def add(part, s, lo):
            hi = lo + part.shape[0]
            if mine:
                part = part + rest[0][s, lo:hi, :].astype(F32)
            out[s, lo:hi, :] = part.astype(BF)

        lefts, rights, prods, cots = parts
        right = jnp.concatenate([r[...] for r in rights], 0)
        for z in range(size):
            got = dot_tn(jnp.concatenate([r[:, z * rows : (z + 1) * rows] for r in lefts], 0), right)
            for j in range(blocks):
                add(got[:, j * B : (j + 1) * B], z, j * rows)
        left = jnp.concatenate([r[...] for r in prods], 0)
        for j in range(2):
            got = dot_tn(left, jnp.concatenate([r[:, j * B : (j + 1) * B] for r in cots], 0))
            for h in range(2):
                for i in range(2):
                    s = 2 * jnp.bitwise_xor(where[0], h) + i
                    p = h * ff
                    part = [got[p + i * 128 : p + (i + 1) * 128], got[p + 256 + i * 64 : p + 256 + (i + 1) * 64]]
                    add(jnp.concatenate(part, 0), s, low + j * 192)

    whole_of = lambda a: pl.BlockSpec(a.shape, lambda i, w: (0,) * a.ndim)
    in_specs = [whole_of(a) for a in groups[0]]
    in_specs += [pl.BlockSpec((a.shape[0], 2 * ff), lambda i, w: (0, 0 if mine else 1)) for a in dgu]
    in_specs += [whole_of(a) for a in product]
    in_specs += [pl.BlockSpec((a.shape[0], side), lambda i, w: (0, jnp.bitwise_xor(w[0], 0 if mine else 1))) for a in groups[3]]
    args = sum(groups, []) + ([other] if mine else [])
    out = sds((size, low + 384, B), BF)
    return pl.pallas_call(
        body,
        out_shape=out,
        grid_spec=pltpu.PrefetchScalarGridSpec(
            num_scalar_prefetch=1, grid=(1,), in_specs=in_specs + [whole_of(out)] * mine, out_specs=whole_of(out)
        ),
        compiler_params=pltpu.CompilerParams(vmem_limit_bytes=VMEM_LIMIT),
        cost_estimate=cost(6 * 1024 * width * 2 * ff, sum(a.size * 2 for a in args)),
    )(core, *args)


def over_blocks(block, shared, per_block, outs, flops, total=False):
    flat = []
    shape = []
    for a in shared:
        shape.append(len(a) if isinstance(a, list) else None)
        flat += a if isinstance(a, list) else [a]
    nb, k, o = len(per_block), len(per_block[0]), len(outs[0])
    scalars = sum(1 for a in flat if a.dtype == jnp.int32)
    args = flat + sum(per_block, [])
    out_shapes = sum(outs, []) + ([total] if total else [])

    def body(*refs):
        at, head = 0, []
        for m in shape:
            head.append(refs[at] if m is None else refs[at : at + m])
            at += 1 if m is None else m
        ins, results = refs[at : at + nb * k], refs[at + nb * k :]
        tail = ()
        if total:
            results[-1][...] = jnp.zeros_like(results[-1])
            tail = (results[-1],)
        for b in range(nb):
            block(*head, *ins[b * k : (b + 1) * k], *results[b * o : (b + 1) * o], *tail)

    got = kernel_call(body, out_shapes, args, flops=flops * nb, scalars=scalars)
    return [got[b * o : (b + 1) * o] for b in range(nb)], (got[-1] if total else None)


def make_body(size, plane, halves):
    n = plane.n
    parts = 2 if halves else 1
    one_by_one = [[r] for r in (n - 1, *range(1, n - 1), 0)]
    three = [[n - 1], list(range(1, n - 1)), [0]]

    def body(tokens, segment_ids, attn_gain, w_query, w_key, w_value, query_gain, key_gain,
             w_out, mlp_gain, w_gate, w_up, w_down, cotangent):
        t = plane.index()
        c = lax.axis_index("c") if halves else 0
        rows, width = tokens.shape
        length = segment_ids.shape[1]
        assert rows == length
        half = rows // 2
        cb = width // B
        wrows = w_query.shape[0]
        cut_a, cut_b = 2 * wrows, 2 * w_gate.shape[1] // n // parts // B * wrows
        out_rows, down_rows = w_out.shape[0] // parts // n, w_down.shape[0] // parts // n
        ff = n * down_rows
        spread = plane.square and halves and size == 4 and ff == 384 and width == 1024
        core = jnp.stack([c]).astype(jnp.int32)
        gain_in, gain_mid = attn_gain[None, :], mlp_gain[None, :]
        qg, kg = query_gain[None, :], key_gain[None, :]
        freq = ROPE_BASE ** (-2.0 * (jnp.arange(HEAD) % (HEAD // 2)).astype(F32) / HEAD)[None, :]

        def pick(col_weights, row_weight):
            each = [w.shape[1] // n // parts for w in col_weights]
            total = sum(each)
            high = total // B * wrows
            q = row_weight.shape[0] // parts // n if row_weight is not None else 0
            where = jnp.stack([t * parts + c, c * n + t]).astype(jnp.int32)

            def fill(_, *refs):
                a = [r[...] for r in refs[: len(each)]]
                if a:
                    a = jnp.concatenate(a, 1)
                for j in range(total // B):
                    refs[-1][j * wrows : (j + 1) * wrows, :] = a[:, j * B : (j + 1) * B]
                for j in range(cb if q else 0):
                    refs[-1][high + j * q : high + (j + 1) * q, :] = refs[-2][:, j * B : (j + 1) * B]

            rows_of = [row_weight] if q else []
            return pl.pallas_call(
                fill,
                out_shape=sds((high + cb * q, B), BF),
                grid_spec=pltpu.PrefetchScalarGridSpec(
                    num_scalar_prefetch=1,
                    grid=(1,),
                    in_specs=[pl.BlockSpec((wrows, k), lambda i, at: (0, at[0])) for k in each]
                    + [pl.BlockSpec((q, width), lambda i, at: (at[1], 0)) for _ in rows_of],
                    out_specs=pl.BlockSpec((high + cb * q, B), lambda i, at: (0, 0)),
                ),
                compiler_params=pltpu.CompilerParams(vmem_limit_bytes=VMEM_LIMIT),
            )(where, *[pltpu.with_memory_space_constraint(w, pltpu.HBM) for w in (*col_weights, *rows_of)])

        def pick_spread():
            where = jnp.stack([t, c]).astype(jnp.int32)
            aligned = lambda i, k: lambda _, w: (0, 6 * (2 * w[1] + i) + (3 * w[0]) // 2 + k)

            def fill(w, *refs):
                odd = jnp.full((wrows, HEAD), w[0] % 2) == 1
                low = lax.broadcasted_iota(jnp.int32, (wrows, HEAD), 1) < HEAD // 2
                cols = []
                for m in range(2):
                    full, rest = [], []
                    for i in range(2):
                        w0, w1 = (refs[4 * m + 2 * i + k][...].astype(F32) for k in range(2))
                        r0, r1 = half_roll(w0), half_roll(w1)
                        full.append(jnp.where(odd, jnp.where(low, r0, r1), w0))
                        rest.append(jnp.where(odd, r1, w1) if i == 0 else jnp.where(odd, w1, r1))
                    cols += [*full, jnp.where(low, *rest)]
                out, down = refs[-1], refs[-2]
                for j, a in enumerate(cols):
                    out[j // 2 * wrows : (j // 2 + 1) * wrows, j % 2 * HEAD : (j % 2 + 1) * HEAD] = a.astype(BF)
                for j in range(2):
                    out[cut_b + j * 192 : cut_b + (j + 1) * 192, :] = down[:, j * B : (j + 1) * B]

            return pl.pallas_call(
                fill,
                out_shape=sds((cut_b + 384, B), BF),
                grid_spec=pltpu.PrefetchScalarGridSpec(
                    num_scalar_prefetch=1,
                    grid=(1,),
                    in_specs=[pl.BlockSpec((wrows, HEAD), aligned(i, k)) for _ in range(2) for i in range(2) for k in range(2)]
                    + [pl.BlockSpec((192, width // 2), lambda _, w: (w[0], w[1]))],
                    out_specs=pl.BlockSpec((cut_b + 384, B), lambda _, w: (0, 0)),
                ),
                compiler_params=pltpu.CompilerParams(vmem_limit_bytes=VMEM_LIMIT),
            )(where, *[stay(w_gate)] * 4, *[stay(w_up)] * 4, stay(w_down))

        def both(a):
            return [a, swap(a, "c")] if halves else [a]

        def rows_to_chip(got, cut):
            blocks = plane.exchange(lambda i: lax.dynamic_slice_in_dim(got, i, 1, 0)[0, cut:])
            return arrange(plane, t, blocks, cb)

        got_a = lax.all_gather(pick([w_query, w_key, w_value], w_out), "shard", axis=0, tiled=False)

        seg_rows = jnp.pad(segment_ids.astype(BF), ((0, 15), (0, width - length)))
        tok = plane.gather(tokens[:half], jnp.concatenate([tokens[half:], seg_rows], 0))
        cot_own, w_gate, w_up, w_down, tok[1], tok[n - 2] = tie((cotangent, w_gate, w_up, w_down, tok[1], tok[n - 2]))
        cot = plane.gather(cot_own[:half], cot_own[half:])
        piece_b = pick_spread() if spread else pick([w_gate, w_up], w_down)
        prep, _ = over_blocks(
            functools.partial(prep_block, length), [gain_in, freq], tok,
            [[hbm((length, width), BF), hbm((length, HEAD), F32), hbm((length, HEAD), F32), hbm((length, length), F32)]] * n,
            0,
        )
        got_a, prep, piece_b, cot = tie((got_a, prep, piece_b, cot))
        nin, tables = [a[0] for a in prep], [a[1:] for a in prep]
        got_b = lax.all_gather(piece_b, "shard", axis=0, tiled=False)
        wo = rows_to_chip(got_a, cut_a)
        wa, wo = both(got_a), both(wo)

        def term_type(r):
            return sds((rows, width), F32 if r == 0 and plane.square else BF)

        def run(block, shared, ins, outs, flops, order, total=None):
            got, totals = {}, []
            for group in [g[i : i + 2] for g in order for i in range(0, len(g), 2)]:
                mine = [ins[r] for r in group]
                res, tot = over_blocks(block, shared, mine, [outs(r) for r in group], flops, total)
                got.update(zip(group, res))
                totals.append(tot)
            return [{r: got[r][i] for r in got} for i in range(len(outs(0)))], totals

        (lin, vals, mixed, partial), _ = run(
            functools.partial(attend_block, parts, wrows), [qg, kg, wa, wo],
            [[stay(a) for a in (nin[r], *tables[r])] for r in range(n)],
            lambda r: [hbm((length, parts * 3 * HEAD), F32), hbm((length, parts * HEAD), BF),
                       hbm((length, parts * GROUP * HEAD), BF), term_type(r)],
            2 * length * width * parts * 6 * HEAD, three,
        )
        lin, vals, mixed, partial = ([a[r] for r in range(n)] for a in (lin, vals, mixed, partial))
        terms = plane.scatter(partial)
        hidden, nm0, nm1 = kernel_call(
            mid_kernel,
            [hbm((rows, width), F32), sds((half, width), BF), sds((half, width), BF)],
            [tokens, gain_mid, *terms],
        )
        nm = plane.gather(nm0, nm1)
        got_b, nm[1][1], nm[n - 2][0] = tie((got_b, nm[1][1], nm[n - 2][0]))
        wgu, wd = both(got_b), [] if spread else both(rows_to_chip(got_b, cut_b))

        def mlp(order):
            return run(
                functools.partial(mlp_block, spread, parts, wrows, ff), [core, wgu, wd],
                {r: [*nm[r], *[stay(a) for a in cot[r]]] for g in order for r in g},
                lambda r: [sds((rows, parts * ff), BF), sds((rows, parts * 2 * ff), BF),
                           hbm((rows, width), term_type(r).dtype), term_type(r)],
                2 * length * width * parts * 7 * ff, order,
            )[0]

        blocks = mlp([[0], [n - 1], list(range(1, n - 1))])
        product, dgu, partial, d_mid = ([a[r] for r in range(n)] for a in blocks)
        terms_mid = plane.scatter(d_mid)

        def pair(make, between=lambda a: a):
            if halves:
                return make(0, swap(between(make(1, None)), "c"))
            return lax.psum(make(0, None), "c")

        def exchanged(low):
            return plane.exchange(lambda i: lax.dynamic_index_in_dim(low, i, 0, keepdims=False))

        def merged(lhs, rhs, width_, other, low, gains=()):
            if halves:
                return grad_columns(plane, t, lhs, rhs, 0, width_, size, swap(other, "c"), low, gains)
            a = grad_columns(plane, t, lhs, rhs, 0, width_, size, None)
            return jnp.concatenate([lax.psum(a, "c"), jnp.stack(low, 0)], 1)

        if spread:
            make_b = lambda other: grad_mlp(core, nm, dgu, product, cot, other, size, ff)
            product, terms_mid[-1] = tie((product, terms_mid[-1]))
            other_b = make_b(None)
            terms_mid, other_b = tie((terms_mid, other_b))
        d_hidden, dh0, dh1, mlp_grad = kernel_call(
            mid_back_kernel,
            [hbm((rows, width), F32), sds((half, width), BF), sds((half, width), BF), sds((1, width), F32)],
            [hidden, cotangent, gain_mid, *terms_mid],
        )
        dh = plane.gather_near(dh0, dh1)
        if spread:
            grads_b = make_b(swap(other_b, "c"))
        else:
            dgu = [[a] for a in dgu]
            gu_other = grad_columns(plane, t, nm, dgu, 1, 2 * ff, size, None) if halves else None
            grads_b = merged(nm, dgu, 2 * ff, gu_other, exchanged(pair(lambda h, o: grad_rows(product, cot, half, h, ff, n, o))))
        dh[1], dh[n - 2], grads_b, dh[0] = tie((dh[1], dh[n - 2], grads_b, dh[0]))
        grads_b = lax.psum_scatter(grads_b.reshape(-1, B), "shard", scatter_dimension=0, tiled=True)

        def back(order, dh):
            return run(
                functools.partial(attend_back_block, parts, wrows), [qg, kg, wa, [stay(a) for a in wo]],
                {r: [*[stay(a) for a in dh[r]], *[stay(a) for a in (*tok[r], lin[r], vals[r], *tables[r])]]
                 for g in order for r in g},
                lambda r: [hbm((rows, parts * 4 * HEAD), BF), hbm((rows, width), term_type(r).dtype)],
                2 * length * width * parts * 6 * HEAD, order, sds((1, width + 2 * HEAD), F32),
            )

        own_back, gains = back([[0]], dh)
        dh = plane.gather_far(dh)
        dh[n - 1], own_back, partial = tie((dh[n - 1], own_back, partial))
        near_out = plane.send_near(partial)
        if halves:
            out, other = grad_rows_twice(
                [stay(a) for a in mixed], [[stay(a) for a in b] for b in dh], half, GROUP * HEAD, n)
            out = (out.astype(F32) + swap(other, "c").astype(F32)).astype(BF)
        else:
            out = pair(lambda h, o: grad_rows(mixed, dh, half, h, GROUP * HEAD, n, o))
        dh[1:], partial, out = tie((dh[1:], partial, out))
        out = exchanged(out)
        far_out = plane.send_far(partial)
        near_back, more = back([list(range(1, n - 1))], dh)
        dh[n - 1], out, far_out, near_back, partial, near_out = tie(
            (dh[n - 1], out, far_out, near_back, partial, near_out))
        terms_out = [partial[0], *near_out, far_out] if plane.square else plane.scatter(partial)
        near_in = plane.send_near(near_back[1])
        separate = plane.square and halves and size == n
        if separate:
            dh[n - 1], out = tie((dh[n - 1], arrange_rows(plane, t, out)))
            out = lax.psum_scatter(out, "shard", scatter_dimension=0, tiled=True)
        far_back, last = back([[n - 1]], dh)
        gains = gains + more + last
        far_back, grads_b, terms_out, near_in = tie((far_back, grads_b, terms_out, near_in))
        grads_b = plane.near(grads_b)
        dqkv, d_in = ([{**a, **b, **c}[r] for r in range(n)] for a, b, c in zip(own_back, near_back, far_back))
        dqkv = [[stay(a)] for a in dqkv]
        lhs = [[stay(a)] for a in nin]
        qkv_other = grad_columns(plane, t, lhs, dqkv, 1, 4 * HEAD, size, None) if halves else None
        if halves:
            qkv_other, grads_b, out = tie((qkv_other, grads_b, out))
        if separate:
            grads_a = merged(lhs, dqkv, 4 * HEAD, qkv_other, None, [mlp_grad, *gains])
            grads_b, grads_a = tie((grads_b, grads_a))
            grads_b = plane.far_halves(grads_b)
            d_in[n - 1], grads_b = tie((d_in[n - 1], grads_b))
            terms_in = [d_in[0], *near_in, plane.send_far(d_in)]
        else:
            grads_a = merged(lhs, dqkv, 4 * HEAD, qkv_other, out)
            grads_b = plane.far_halves(grads_b)
            terms_in = plane.scatter(d_in)
        grads_a = lax.psum_scatter(grads_a.reshape(-1, B), "shard", scatter_dimension=0, tiled=True)
        if separate:
            grads_a = jnp.concatenate([grads_a, out], 0)
        activations = kernel_call(out_kernel, [sds((rows, width), BF)], [hidden, *terms_out])[0]

        def assemble(mine, outs, write):
            got = [(r, 0, a) for r, a in enumerate(mine)]
            if halves:
                got += [(r, 1, swap(a, "c")) for r, a in enumerate(mine)]

            def body(where, *refs):
                total = 0.0
                for (r, other, _), ref in zip(got, refs):
                    core = jnp.bitwise_xor(where[1], other) if halves else 0
                    lines = write(ref, plane.place(where[0], r), core, refs[len(got) :])
                    total = total + lines if separate and write is write_a else total
                if separate and write is write_a:
                    i = 0
                    for out in refs[len(got) + 4 :]:
                        for j in range(0, out.shape[1], B):
                            k = min(B, out.shape[1])
                            at = 0 if out.shape[1] > HEAD else HEAD * (i % 2)
                            line = i if out.shape[1] > HEAD else 2 * width // B
                            out[:, j : j + k] = total[line : line + 1, at : at + k]
                            i += 1

            if write is write_spread:
                body = lambda where, *refs: write(where, refs[: len(got)], refs[len(got) :])
            where = jnp.stack([t, c]).astype(jnp.int32)
            return kernel_call(body, outs, [where] + [a for _, _, a in got], scalars=1)

        def write_cols(ref, j, todo, src, core):
            a = ref[j * wrows : (j + 1) * wrows, :].astype(F32)
            for lo, hi, out, per, at in todo:
                start = pl.multiple_of((src * parts + core) * per + at, HEAD)
                out[:, pl.ds(start, hi - lo)] = a[:, lo:hi]

        def write_rows(ref, base, q, src, core, out):
            start = pl.multiple_of((core * n + src) * q, 16)
            for j in range(cb):
                a = ref[base + j * q : base + (j + 1) * q, :].astype(F32)
                out[pl.ds(start, q), j * B : (j + 1) * B] = a

        def write_b(ref, src, core, outs):
            gate, up, down = outs
            for j in range(2 * ff // B):
                todo = []
                for out, lo in ((gate, 0), (up, ff)):
                    a, b = max(j * B, lo), min((j + 1) * B, lo + ff)
                    if a < b:
                        todo.append((a - j * B, b - j * B, out, ff, a - lo))
                write_cols(ref, j, todo, src, core)
            write_rows(ref, cut_b, down_rows, src, core, down)

        def write_spread(where, refs, outs):
            gate, up, down = outs
            odd = jnp.full((wrows, HEAD), where[0] % 2) == 1
            low = lax.broadcasted_iota(jnp.int32, (wrows, HEAD), 1) < HEAD // 2
            for other in range(2):
                core = jnp.bitwise_xor(where[1], other)
                mine = refs[other * n : (other + 1) * n]
                for r, ref in enumerate(mine):
                    for j in range(2):
                        down[pl.ds(pl.multiple_of(plane.place(where[0], r) * 192, 64), 192),
                             pl.ds(pl.multiple_of((2 * core + j) * B, B), B)] = (
                            ref[cut_b + j * 192 : cut_b + (j + 1) * 192, :].astype(F32))
                for k in range(2):
                    one, two = mine[2 * k], mine[2 * k + 1]
                    pair_at = jnp.bitwise_xor(where[0] // 2, k)
                    for m, out in enumerate((gate, up)):
                        def block(ref, j):
                            j = 3 * m + j
                            return ref[j // 2 * wrows : (j // 2 + 1) * wrows, j % 2 * HEAD : (j % 2 + 1) * HEAD].astype(F32)

                        pairs = [(block(one, j), block(two, j)) for j in range(3)]
                        even = [jnp.where(odd, b, a) for a, b in pairs]
                        odds = [jnp.where(odd, a, b) for a, b in pairs]
                        for i in range(2):
                            at = pl.multiple_of(768 * (2 * core + i) + 384 * pair_at, HEAD)
                            rolled = half_roll(odds[i])
                            rest_even = even[2] if i == 0 else half_roll(even[2])
                            rest_odd = half_roll(odds[2]) if i == 0 else odds[2]
                            out[:, pl.ds(at, HEAD)] = even[i]
                            out[:, pl.ds(at + HEAD, HEAD)] = jnp.where(low, rest_even, rolled)
                            out[:, pl.ds(at + 2 * HEAD, HEAD)] = jnp.where(low, rolled, rest_odd)

        def write_a(ref, src, core, outs):
            q, k, v, out = outs[:4]
            write_cols(ref, 0, [(0, B, q, B, 0)], src, core)
            write_cols(ref, 1, [(0, HEAD, k, HEAD, 0), (HEAD, B, v, HEAD, 0)], src, core)
            write_rows(ref, cut_a + (16 if separate else 0), out_rows, src, core, out)
            return ref[cut_a : cut_a + 16, :].astype(F32)

        like = lambda w: sds(w.shape, F32)
        gate_g, up_g, down_g = assemble(grads_b, [like(w_gate), like(w_up), like(w_down)], write_spread if spread else write_b)
        grads_a, gate_g, up_g, down_g, activations, terms_in = tie(
            (grads_a, gate_g, up_g, down_g, activations, terms_in))
        input_grad = kernel_call(
            last_kernel, [sds((rows, width), BF)],
            [tokens, stay(d_hidden), gain_in, stay(terms_in[0]), *terms_in[1:]])[0]
        grads_a, input_grad = tie((plane.far_halves(plane.near(grads_a)), input_grad))
        outs_a = [like(w_query), like(w_key), like(w_value), like(w_out)]
        if separate:
            gain_outs = [sds((1, k), F32) for k in (width, width, HEAD, HEAD)]
            query_g, key_g, value_g, out_g, *gains = assemble(grads_a, outs_a + gain_outs, write_a)
            gains = [g[0] for g in gains]
        else:
            query_g, key_g, value_g, out_g = assemble(grads_a, outs_a, write_a)
            gains = functools.reduce(jnp.add, gains)
            gains = [gains[:, :width], mlp_grad, gains[:, width : width + HEAD], gains[:, width + HEAD :]]
            gains = [g[0] for g in lax.psum(gains, ("shard", "y", "x", "c"))]

        return (
            activations,
            input_grad,
            gains[0],
            query_g,
            key_g,
            value_g,
            gains[2],
            gains[3],
            out_g,
            gains[1],
            gate_g,
            up_g,
            down_g,
        )

    return body


def solution(mesh):
    size, replicas = mesh.shape["shard"], mesh.shape["replica"]
    ny, nx = replicas // 4, 2
    assert size == ny * nx
    plane = Plane(ny, nx)
    fine = Mesh(mesh.devices.reshape(size, ny, nx, 2), ("shard", "y", "x", "c"))
    halves = KV_HEADS % (2 * plane.n) == 0
    every = P(("shard", "y", "x", "c"), None)
    shard, copy = P("shard", None), P()
    return jax.shard_map(
        make_body(size, plane, halves),
        mesh=fine,
        in_specs=(every, every, copy, shard, shard, shard, copy, copy, shard, copy, shard, shard, shard, every),
        out_specs=(every, every, copy, shard, shard, shard, copy, copy, shard, copy, shard, shard, shard),
        check_vma=False,
    )
```
